32 devices in a mesh: expert: 8 (over z, core), replica: 4 (over y, x).
Axes of the slice: x: 2, y: 2, z: 4, core: 2. Of those that a mesh axis runs over, the one named last changes fastest.
Arguments:
- weights: bfloat16 [8, 3, 2048, 512], P('expert', None, 'replica'), may hold values from -0.125 to 0.125
- first_moment: float32 [8, 3, 2048, 512], P('expert', None, 'replica'), may hold values from -128 to 128
- second_moment: float32 [8, 3, 2048, 512], P('expert', None, 'replica'), may hold values from 100 to 100000
- out_grads: bfloat16 [4, 1024, 2048], P('replica', 'expert'), may hold values from -8 to 8
- routes: int32 [4, 1024, 1], P('replica', 'expert'), may hold values from 0 to 7; in each aligned block of 128 rows (0 to 127, 128 to 255, ..., all dimensions but the last counted through in order) at most 32 rows name the same one
- task_ids: int32 [4, 8], P('replica', 'expert'), may hold values from 0 to 7
- task_weights: float32 [8], replicated, may hold values from 0.25 to 4
- saved_inputs: bfloat16 [4, 8, 256, 2048], P('replica', 'expert'), may hold values from -8 to 8
Outputs:
- input_grads: bfloat16 [4, 1024, 2048], P('replica', 'expert')
- adam_step: float32 [8, 3, 2048, 512], P('expert', None, 'replica')
The draws below stay inside these ranges and needn't reach their ends.
Inputs may be any that keep to these rules, and one draw needn't show every extreme that they name: `routes`: at most 32 of the rows of one device go to one expert, and in every draw some device sends exactly 32 rows to some expert.
All inputs are finite; a program needn't handle non-finite values.
Results may differ from the reference program's by a relative error of at most 0.0057.
Values may be sent and summed in bfloat16 or wider, within the bound.
No kernel may reach another device: no remote copies, remote signals or barrier semaphores. Data moves between devices by JAX's collectives and lax.ppermute only.
A program may use at most 128 MiB of HBM per device.

```python
import math
import jax
import jax.numpy as jnp
import numpy as np
from jax import lax

D = 2048
F = 512
TOK_DEV = 128
BLOCK = 128
TASKS = 8
EXPERTS = 8
REPLICAS = 4
CAP = 32
SLOTS = 256
TOKENS = 1024
BLOCKS = 8


def segment_strength(key):
    levels = REPLICAS.bit_length() - 1
    flip_mask = jax.random.randint(jax.random.fold_in(key, 31), (), 0, REPLICAS, dtype=jnp.int32)
    labels = jnp.bitwise_xor(jnp.arange(REPLICAS, dtype=jnp.int32), flip_mask)
    seg_order = jnp.zeros((REPLICAS,), jnp.int32)
    for bit_pos in range(levels):
        seg_order = seg_order + (labels >> bit_pos & 1) * 2 ** (levels - 1 - bit_pos)
    fraction = seg_order.astype(jnp.float32) / float(max(REPLICAS - 1, 1))
    jitter = jax.random.uniform(jax.random.fold_in(key, 33), (REPLICAS,), jnp.float32, -0.3, 0.3)
    seg_level = jnp.exp(math.log(0.06) + fraction * math.log(2.0 / 0.06) + jitter)
    column_segment = jnp.arange(D, dtype=jnp.int32) // (D // REPLICAS)
    return seg_level[column_segment]


def common_part(key, length, salt):
    base_part = jax.random.normal(jax.random.fold_in(key, salt), (length,), jnp.float32)
    spread = jnp.exp(jax.random.uniform(jax.random.fold_in(key, salt + 1), (length,), jnp.float32, 0.0, math.log(2.5)))
    return base_part * spread * segment_strength(key)


def draw_out_grads(key, part):
    shared = common_part(key, D, 11)
    noise_part = jax.random.normal(jax.random.fold_in(key, 13), (REPLICAS, TOKENS, D), jnp.float32)
    return jnp.clip(noise_part + shared[None, None, :], -8.0, 8.0).astype(jnp.bfloat16)


def draw_saved_inputs(key, part):
    shared = common_part(key, D, 21)
    row_scale = jnp.exp(jax.random.uniform(jax.random.fold_in(key, 23), (REPLICAS, EXPERTS, SLOTS, 1), jnp.float32, 0.0, math.log(4.0)))
    noise_part = jax.random.normal(jax.random.fold_in(key, 25), (REPLICAS, EXPERTS, SLOTS, D), jnp.float32)
    return jnp.clip(noise_part * row_scale + shared[None, None, None, :], -8.0, 8.0).astype(jnp.bfloat16)


def with_ends(values, rng, low, high):
    place = [jax.random.randint(jax.random.fold_in(rng, axis), (), 0, length) for axis, length in enumerate(values.shape)]
    longest = values.shape.index(max(values.shape))
    next_to = place[:longest] + [(place[longest] + 1) % values.shape[longest]] + place[longest + 1:]
    return values.at[tuple(place)].set(low).at[tuple(next_to)].set(high)


def steps_of(stream_key, dims, cuts, smallest, largest):
    def one(position, parts):
        draws = jax.random.uniform(jax.random.fold_in(jax.random.fold_in(stream_key, 6), position), (parts,), jnp.float32, smallest / len(cuts), largest / len(cuts))
        return jnp.repeat(jnp.exp(draws), dims[position] // parts).reshape((-1,) + (1,) * (len(dims) - position - 1))

    gain = one(*cuts[0])
    for cut in cuts[1:]:
        gain = gain * one(*cut)
    return gain


def deal_out(stream_key, own, number, rows, amount, top, reach, lean):
    ranking = jax.random.permutation(stream_key, amount)
    packed, usual = load_shares(amount, rows * top, reach, lean, True), load_shares(amount, rows * top, reach, lean, False)
    places = jnp.arange(amount)

    def named(sizes, rotation):
        used = int((sizes > 0).sum())
        fixed = max(1, used // 4)
        shifted = fixed + (places - fixed + rotation * (used - fixed)) % max(1, amount - fixed)
        return jnp.zeros((amount,), jnp.int32).at[ranking[jnp.where(places < fixed, places, shifted)]].set(jnp.asarray(sizes, jnp.int32))

    sizes = jnp.where(number % 4 == 0, named(packed, number // 4), named(usual, number - number // 4 - 1))
    mixed = jax.random.permutation(jax.random.fold_in(own, 3), amount)
    source_of, sink = mixed[0:amount // 2 * 2:2], mixed[1:amount // 2 * 2:2]
    margin = jnp.minimum(sizes[source_of] - 1, reach - sizes[sink]) // 2
    margin = jnp.where((source_of == ranking[0]) | (sink == ranking[0]) | (sizes[sink] == 0), 0, jnp.maximum(margin, 0))
    shifted = jax.random.randint(jax.random.fold_in(own, 4), (amount // 2,), 0, 1 << 20) % (margin + 1)
    sizes = sizes.at[source_of].add(-shifted).at[sink].add(shifted)
    items = jnp.searchsorted(jnp.cumsum(sizes), jnp.arange(rows * top), side="right").astype(jnp.int32)
    table = items.reshape(top, rows).T
    table = table[jax.random.permutation(jax.random.fold_in(own, 1), rows)]
    rotation = jax.random.randint(jax.random.fold_in(own, 2), (rows, 1), 0, top)
    return jnp.take_along_axis(table, (jnp.arange(top)[None, :] + rotation) % top, axis=1)


def load_shares(count, total, bound, slope, full):
    portions = [(1 << 20) // math.isqrt(grade ** slope) + 1 for grade in range(1, count + 1)]
    largest = bound if full else min(bound, max(-(-total // count), total * portions[0] // sum(portions)))
    least = 1 if total - largest >= count - 1 else 0
    holding, surplus = [largest] + [least] * (count - 1), total - largest - least * (count - 1)
    while surplus > 0:
        movable = [i for i in range(1, count) if holding[i] < largest] or [i for i in range(1, count) if holding[i] < bound]
        whole, budget = sum([portions[i] for i in movable]), surplus
        for i in movable:
            extra = min(bound - holding[i], max(1, budget * portions[i] // whole), surplus)
            holding[i] = holding[i] + extra
            surplus = surplus - extra
    return np.array(holding)


def scatter_about(rng, extent, width, reach, pieces=(), held_as=jnp.bfloat16):
    drawn = width * jax.random.normal(rng, extent, jnp.float32)
    if pieces:
        drawn = drawn * steps_of(rng, extent, pieces, -0.22, 0.18)
    return jnp.clip(drawn, -reach, reach).astype(held_as)


def setup_inputs(seed: int = 0) -> dict:
    key_list = jax.random.split(jax.random.key(seed), 9)
    weights = scatter_about(key_list[0], (EXPERTS, 3, D, F), D ** -0.5, 0.125, ((0, 8), (2, 4)))
    first_moment = scatter_about(key_list[1], (EXPERTS, 3, D, F), 20.0, 128.0, ((0, 8), (2, 4)), jnp.float32)
    second_moment = jnp.clip(jnp.exp(math.log(100000.0) - 6.9077553 * jax.random.uniform(key_list[2], (EXPERTS, 3, D, F), jnp.float32) ** steps_of(key_list[2], (EXPERTS, 3, D, F), ((0, 8), (2, 4)), -0.2, 0.2)), 100.0, 100000.0)
    out_grads = draw_out_grads(jax.random.fold_in(key_list[8], 71), 0)
    routes_keys = jax.random.split(jax.random.fold_in(key_list[4], 1), REPLICAS * TOKENS // TOK_DEV)
    routes_turns = jax.random.permutation(jax.random.fold_in(key_list[4], 3), REPLICAS * TOKENS // TOK_DEV)
    routes = jax.vmap(lambda own, number: deal_out(jax.random.fold_in(key_list[4], 2), own, number, TOK_DEV, EXPERTS, 1, CAP, 2))(routes_keys, routes_turns).reshape((REPLICAS, TOKENS, 1))
    task_ids = with_ends(jax.random.randint(key_list[5], (REPLICAS, BLOCKS), 0, TASKS), jax.random.fold_in(key_list[5], 1), 0, TASKS - 1).astype(jnp.int32)
    task_weights = jnp.clip(jnp.exp(jax.random.uniform(key_list[6], (TASKS,), jnp.float32, math.log(0.25), math.log(4.0))), 0.25, 4.0)
    saved_inputs = draw_saved_inputs(jax.random.fold_in(key_list[8], 71), 0)
    return {"weights": weights, "first_moment": first_moment, "second_moment": second_moment, "out_grads": out_grads, "routes": routes, "task_ids": task_ids, "task_weights": task_weights, "saved_inputs": saved_inputs}


beta_first = 0.9
beta_second = 0.95
adam_eps = 1e-08
norm_eps = 1e-06
first_fix = 1.0 - (0.9 ** 50) ** 2
second_fix = 1.0 - (0.95 ** 50) ** 2

def round_half(values):
    narrow = values.astype(jnp.bfloat16)
    narrow = lax.optimization_barrier(narrow)
    return narrow.astype(jnp.float32)

def slot_layout(routes):
    expert_of = routes[:, :, 0].reshape(REPLICAS, EXPERTS, TOK_DEV).astype(jnp.int32)
    chosen = (expert_of[..., None] == jnp.arange(EXPERTS, dtype=jnp.int32)).astype(jnp.int32)
    before = (jnp.cumsum(chosen, axis=2) - chosen).astype(jnp.int32)
    slot_rank = lax.optimization_barrier(jnp.sum(before * chosen, axis=3)).astype(jnp.int32)
    source = jnp.arange(EXPERTS, dtype=jnp.int32)[None, :, None]
    slot_index = (source * CAP + slot_rank).astype(jnp.int32)
    return (expert_of.reshape(REPLICAS, TOKENS), slot_index.reshape(REPLICAS, TOKENS))

def adasum(grads):
    segment = jnp.arange(D, dtype=jnp.int32) // (D // REPLICAS)
    current = grads
    levels = REPLICAS.bit_length() - 1
    for level_now in range(levels):
        paired = current.reshape(current.shape[0] // 2, 2, 3, D, F)
        first_side = paired[:, 0]
        second_side = paired[:, 1]
        low_half = (segment >> level_now & 1 == 0)[None, None, :, None]
        side_first = jnp.where(low_half, first_side, round_half(first_side))
        side_second = jnp.where(low_half, round_half(second_side), second_side)
        cross_sum = lax.optimization_barrier(jnp.sum(side_first * side_second, axis=(1, 2, 3)))
        norm_first = lax.optimization_barrier(jnp.sum(side_first * side_first, axis=(1, 2, 3)))
        norm_second = lax.optimization_barrier(jnp.sum(side_second * side_second, axis=(1, 2, 3)))
        coef_first = 1.0 - cross_sum / (2.0 * (norm_first + norm_eps))
        coef_second = 1.0 - cross_sum / (2.0 * (norm_second + norm_eps))
        current = coef_first[:, None, None, None] * side_first + coef_second[:, None, None, None] * side_second
    return current[0]

def expert_step(operands):
    weight_e, inputs_e, incoming_e, moment_one, moment_two = operands
    weight_wide = weight_e.astype(jnp.float32)
    inputs_wide = inputs_e.astype(jnp.float32)
    incoming_wide = incoming_e.astype(jnp.float32)
    gate_pre = jnp.einsum('rsd,df->rsf', inputs_wide, weight_wide[0])
    up_pre = jnp.einsum('rsd,df->rsf', inputs_wide, weight_wide[1])
    gate_act = jax.nn.silu(gate_pre)
    hidden = (gate_act * up_pre).astype(jnp.bfloat16)
    hidden_grad = jnp.einsum('rsd,df->rsf', incoming_wide, weight_wide[2])
    sigmoid_gate = jax.nn.sigmoid(gate_pre)
    gate_grad = (hidden_grad * up_pre * sigmoid_gate * (1.0 + gate_pre * (1.0 - sigmoid_gate))).astype(jnp.bfloat16)
    up_grad = (hidden_grad * gate_act).astype(jnp.bfloat16)
    gate_wide = gate_grad.astype(jnp.float32)
    up_wide = up_grad.astype(jnp.float32)
    slot_grads = (jnp.einsum('rsf,df->rsd', gate_wide, weight_wide[0]) + jnp.einsum('rsf,df->rsd', up_wide, weight_wide[1])).astype(jnp.bfloat16)
    grads = jnp.stack([jnp.einsum('rsd,rsf->rdf', inputs_wide, gate_wide), jnp.einsum('rsd,rsf->rdf', inputs_wide, up_wide), jnp.einsum('rsd,rsf->rdf', incoming_wide, hidden.astype(jnp.float32))], axis=1)
    merged = adasum(grads)
    first_new = beta_first * moment_one + (1.0 - beta_first) * merged
    second_new = beta_second * moment_two + (1.0 - beta_second) * merged * merged
    adam_step = first_new / first_fix / (jnp.sqrt(second_new / second_fix) + adam_eps)
    return (slot_grads, adam_step)

def reference(weights, first_moment, second_moment, out_grads, routes, task_ids, task_weights, saved_inputs):
    expert_of, slot_index = slot_layout(routes)
    block_weight = task_weights[task_ids]
    scaled = (out_grads.astype(jnp.float32).reshape(REPLICAS, BLOCKS, BLOCK, D) * block_weight[:, :, None, None]).reshape(REPLICAS, TOKENS, D).astype(jnp.bfloat16)
    replica_of = jnp.broadcast_to(jnp.arange(REPLICAS, dtype=jnp.int32)[:, None], (REPLICAS, TOKENS))
    received = jnp.zeros((EXPERTS, REPLICAS, SLOTS, D), jnp.bfloat16).at[expert_of, replica_of, slot_index].set(scaled)
    inputs_by_expert = jnp.swapaxes(saved_inputs, 0, 1)
    slot_grads, adam_step = lax.map(expert_step, (weights, inputs_by_expert, received, first_moment, second_moment))
    input_grads = slot_grads[expert_of, replica_of, slot_index]
    return (input_grads, adam_step)
```

```python
import functools

import jax
import jax.numpy as jnp
from jax import lax
from jax.experimental import pallas as pl
from jax.experimental.pallas import tpu as pltpu
from jax.sharding import PartitionSpec as P

beta_first = 0.9
beta_second = 0.95
adam_eps = 1e-08
norm_eps = 1e-06
first_fix = 1.0 - (0.9**50) ** 2
second_fix = 1.0 - (0.95**50) ** 2
VMEM_BYTES = 56 * 1024 * 1024


def contract_first(left, right):
    return lax.dot_general(
        left, right, (((0,), (0,)), ((), ())), preferred_element_type=jnp.float32
    )


def contract_last(left, right):
    return lax.dot_general(
        left, right, (((1,), (1,)), ((), ())), preferred_element_type=jnp.float32
    )


def swap(blocks, axis):
    return lax.all_to_all(blocks, axis, split_axis=0, concat_axis=0, tiled=True)


def pair_list(count):
    return [(i, j) for i in range(count) for j in range(i, count)]


def gram_kernel(inputs_ref, incoming_ref, factors_ref, gram_ref, grads_ref):
    count = inputs_ref.shape[0]

    @pl.when(pl.program_id(0) == 0)
    def _():
        gram_ref[...] = jnp.zeros_like(gram_ref)

    for matrix in range(3):
        rows_ref = incoming_ref if matrix == 2 else inputs_ref
        for rep in range(count):
            grads_ref[rep] = contract_first(rows_ref[rep], factors_ref[rep, matrix])
        for place, (i, j) in enumerate(pair_list(count)):
            column_sum = jnp.sum(grads_ref[i] * grads_ref[j], axis=0, keepdims=True)
            gram_ref[pl.ds(place, 1), :] += column_sum


def merge_coefs(gram, count):
    vectors = [{rep: None} for rep in range(count)]

    def term(coef, value):
        return value if coef is None else coef * value

    def inner(left, right):
        total = None
        for i, left_coef in left.items():
            for j, right_coef in right.items():
                value = term(left_coef, term(right_coef, gram[min(i, j), max(i, j)]))
                total = value if total is None else total + value
        return total

    while len(vectors) > 1:
        merged = []
        for first, second in zip(vectors[0::2], vectors[1::2]):
            norm_first = jnp.maximum(inner(first, first), 0.0)
            norm_second = jnp.maximum(inner(second, second), 0.0)
            bound = jnp.sqrt(norm_first) * jnp.sqrt(norm_second)
            cross = jnp.minimum(jnp.maximum(inner(first, second), -bound), bound)
            coef_first = 1.0 - cross / (2.0 * (norm_first + norm_eps))
            coef_second = 1.0 - cross / (2.0 * (norm_second + norm_eps))
            joined = {rep: term(coef, coef_first) for rep, coef in first.items()}
            joined.update({rep: term(coef, coef_second) for rep, coef in second.items()})
            merged.append(joined)
        vectors = merged
    return [vectors[0][rep] for rep in range(count)]


def adam_kernel(
    gram_ref, inputs_ref, incoming_ref, factors_ref, first_ref, second_ref, step_ref, coef_ref
):
    count = inputs_ref.shape[0]

    @pl.when(pl.program_id(0) == 0)
    def _():
        sums = jnp.sum(jnp.sum(gram_ref[...], axis=0), axis=1, keepdims=True)
        gram = {pair: sums[place : place + 1] for place, pair in enumerate(pair_list(count))}
        for rep, coef in enumerate(merge_coefs(gram, count)):
            coef_ref[pl.ds(rep, 1), :] = jnp.broadcast_to(coef, (1, coef_ref.shape[1]))

    for matrix in range(3):
        rows_ref = incoming_ref if matrix == 2 else inputs_ref
        merged = None
        for rep in range(count):
            part = contract_first(rows_ref[rep], factors_ref[rep, matrix])
            part = part * coef_ref[pl.ds(rep, 1), :]
            merged = part if merged is None else merged + part
        first_new = beta_first * first_ref[0, matrix] + (1.0 - beta_first) * merged
        second_new = beta_second * second_ref[0, matrix] + (1.0 - beta_second) * merged * merged
        step_ref[0, matrix] = (first_new / first_fix) / (
            jnp.sqrt(second_new / second_fix) + adam_eps
        )


def adasum_adam(inputs, incoming, factors, first_moment, second_moment):
    count, slot_count, seg_rows = inputs.shape
    hidden_width = factors.shape[3]
    tile = min(seg_rows, 128)
    grid = (seg_rows // tile,)
    pairs = len(pair_list(count))
    rows_spec = pl.BlockSpec((count, slot_count, tile), lambda d: (0, 0, d))
    factors_spec = pl.BlockSpec(factors.shape, lambda d: (0, 0, 0, 0))
    moment_spec = pl.BlockSpec((1, 3, tile, hidden_width), lambda d: (0, 0, d, 0))
    params = pltpu.CompilerParams(
        dimension_semantics=("arbitrary",), vmem_limit_bytes=VMEM_BYTES
    )
    flops = 6 * count * slot_count * seg_rows * hidden_width
    row_bytes = 2 * (inputs.size + incoming.size + factors.size)
    partial = pl.pallas_call(
        gram_kernel,
        grid=grid,
        in_specs=[rows_spec, rows_spec, factors_spec],
        out_specs=pl.BlockSpec((pairs, hidden_width), lambda d: (0, 0)),
        out_shape=jax.ShapeDtypeStruct((pairs, hidden_width), jnp.float32),
        scratch_shapes=[pltpu.VMEM((count, tile, hidden_width), jnp.float32)],
        compiler_params=params,
        cost_estimate=pl.CostEstimate(
            flops=flops, bytes_accessed=row_bytes, transcendentals=0
        ),
        name="gram",
    )(inputs, incoming, factors)
    shared = jnp.sum(partial.reshape(pairs, hidden_width // 128, 128), axis=1)
    gathered = swap(jnp.broadcast_to(shared[None], (count, pairs, 128)), "replica")
    return pl.pallas_call(
        adam_kernel,
        grid=grid,
        in_specs=[
            pl.BlockSpec(gathered.shape, lambda d: (0, 0, 0)),
            rows_spec,
            rows_spec,
            factors_spec,
            moment_spec,
            moment_spec,
        ],
        out_specs=moment_spec,
        out_shape=jax.ShapeDtypeStruct(first_moment.shape, jnp.float32),
        scratch_shapes=[pltpu.VMEM((count, hidden_width), jnp.float32)],
        compiler_params=params,
        cost_estimate=pl.CostEstimate(
            flops=flops,
            bytes_accessed=row_bytes + 12 * first_moment.size,
            transcendentals=first_moment.size,
        ),
        name="adam",
    )(gathered, inputs, incoming, factors, first_moment, second_moment)


def shards(
    weights, first_moment, second_moment, out_grads, routes, task_ids, task_weights, saved_inputs
):
    expert_count = lax.axis_size("expert")
    rep_count = lax.axis_size("replica")
    row_count = out_grads.shape[1]
    model_width = out_grads.shape[2]
    hidden_width = weights.shape[3]
    slot_count = saved_inputs.shape[2]
    capacity = slot_count // expert_count
    block_count = task_ids.shape[1]
    block_rows = row_count // block_count
    task_count = task_weights.shape[0]
    seg_rows = model_width // rep_count

    def by_segment(matrix):
        return matrix.reshape(matrix.shape[0], rep_count, seg_rows).swapaxes(0, 1)

    chosen_task = (task_ids[0][:, None] == jnp.arange(task_count, dtype=jnp.int32)[None, :]).astype(
        jnp.float32
    )
    block_weight = jnp.sum(chosen_task * task_weights[None, :], axis=1)
    scaled = (
        (out_grads[0].reshape(block_count, block_rows, model_width) * block_weight[:, None, None])
        .reshape(row_count, model_width)
        .astype(jnp.bfloat16)
    )
    expert_of = routes[0, :, 0]
    chosen = (expert_of[:, None] == jnp.arange(expert_count, dtype=jnp.int32)[None, :]).astype(
        jnp.int32
    )
    slot_rank = jnp.sum((jnp.cumsum(chosen, axis=0) - chosen) * chosen, axis=1)
    label_rows = -(-row_count // seg_rows)

    def as_rows(labels):
        padded = jnp.pad(labels, (0, label_rows * seg_rows - row_count))
        return padded.reshape(label_rows, seg_rows).astype(jnp.bfloat16)

    labels = jnp.concatenate([as_rows(expert_of), as_rows(slot_rank)], axis=0)
    labels = jnp.pad(labels, ((0, -labels.shape[0] % 16), (0, 0)))
    labels = jnp.broadcast_to(labels[None], (rep_count,) + labels.shape)
    routed = swap(jnp.concatenate([by_segment(scaled), labels], axis=1), "replica")
    inputs = swap(by_segment(saved_inputs[0, 0]), "replica")

    def read_labels(first_row):
        rows = routed[:, row_count + first_row : row_count + first_row + label_rows]
        return rows.reshape(rep_count, label_rows * seg_rows)[:, :row_count].astype(jnp.int32)

    slot_index = read_labels(0) * capacity + read_labels(label_rows)
    placing = (
        slot_index[:, None, :] == jnp.arange(slot_count, dtype=jnp.int32)[None, :, None]
    ).astype(jnp.bfloat16)
    outgoing = jnp.einsum(
        "rqt,rtd->rqd", placing, routed[:, :row_count], preferred_element_type=jnp.float32
    ).astype(jnp.bfloat16)
    outgoing = outgoing.reshape(rep_count, expert_count, capacity, seg_rows).swapaxes(0, 1)
    incoming = swap(outgoing, "expert").swapaxes(0, 1).reshape(rep_count, slot_count, seg_rows)

    def product(rows, matrix):
        flat = rows.reshape(rep_count * slot_count, seg_rows)
        total = jnp.dot(flat, matrix, preferred_element_type=jnp.float32)
        return total.astype(jnp.bfloat16).reshape(rep_count, 1, slot_count, hidden_width)

    own_weights = weights[0]
    forward = jnp.concatenate(
        [product(inputs, own_weights[0]), product(inputs, own_weights[1])], axis=1
    )
    forward = jnp.sum(swap(forward, "replica").astype(jnp.float32), axis=0)
    backward = product(incoming, own_weights[2])
    hidden_grad = jnp.sum(swap(backward, "replica").astype(jnp.float32), axis=0)[0]
    gate_pre, up_pre = forward[0], forward[1]
    gate_act = jax.nn.silu(gate_pre)
    hidden = (gate_act * up_pre).astype(jnp.bfloat16)
    sigmoid_gate = jax.nn.sigmoid(gate_pre)
    gate_grad = (
        hidden_grad * up_pre * sigmoid_gate * (1.0 + gate_pre * (1.0 - sigmoid_gate))
    ).astype(jnp.bfloat16)
    up_grad = (hidden_grad * gate_act).astype(jnp.bfloat16)
    factors = jnp.stack([gate_grad, up_grad, hidden])
    factors = swap(jnp.broadcast_to(factors[None], (rep_count,) + factors.shape), "replica")

    slot_grads = (
        contract_last(factors[:, 0].reshape(-1, hidden_width), own_weights[0])
        + contract_last(factors[:, 1].reshape(-1, hidden_width), own_weights[1])
    ).astype(jnp.bfloat16)
    slot_grads = slot_grads.reshape(rep_count, expert_count, capacity, seg_rows).swapaxes(0, 1)
    returned = swap(slot_grads, "expert").swapaxes(0, 1).reshape(rep_count, slot_count, seg_rows)
    row_grads = jnp.einsum(
        "rqt,rqd->rtd", placing, returned, preferred_element_type=jnp.float32
    ).astype(jnp.bfloat16)
    input_grads = swap(row_grads, "replica").swapaxes(0, 1).reshape(1, row_count, model_width)

    adam_step = adasum_adam(inputs, incoming, factors, first_moment, second_moment)
    return (input_grads, adam_step)


def solution(mesh):
    return jax.shard_map(
        shards,
        mesh=mesh,
        in_specs=(
            P("expert", None, "replica", None),
            P("expert", None, "replica", None),
            P("expert", None, "replica", None),
            P("replica", "expert", None),
            P("replica", "expert", None),
            P("replica", "expert"),
            P(),
            P("replica", "expert", None, None),
        ),
        out_specs=(P("replica", "expert", None), P("expert", None, "replica", None)),
        check_vma=False,
    )
```

```python
import functools

import jax
import jax.numpy as jnp
from jax import lax
from jax.experimental import pallas as pl
from jax.experimental.pallas import tpu as pltpu
from jax.sharding import PartitionSpec as P

beta_first = 0.9
beta_second = 0.95
adam_eps = 1e-08
norm_eps = 1e-06
first_fix = 1.0 - (0.9**50) ** 2
second_fix = 1.0 - (0.95**50) ** 2
VMEM_BYTES = 56 * 1024 * 1024
LABEL_ROWS = 16


def contract_first(left, right):
    return lax.dot_general(
        left, right, (((0,), (0,)), ((), ())), preferred_element_type=jnp.float32
    )


def contract_last(left, right):
    return lax.dot_general(
        left, right, (((1,), (1,)), ((), ())), preferred_element_type=jnp.float32
    )


def multiply(left, right):
    return jnp.dot(left, right, preferred_element_type=jnp.float32)


def from_peer(array, offset):
    count = lax.axis_size("replica")
    return lax.ppermute(array, "replica", [(i, i ^ offset) for i in range(count)])


def exchange(parts):
    return [parts[0]] + [from_peer(part, k) for k, part in enumerate(parts) if k]


def gather_pair(first, second):
    count = lax.axis_size("replica")
    if count != 4:
        return list(zip(exchange([first] * count), exchange([second] * count)))
    first_two = from_peer(first, 2)
    second_one = from_peer(second, 1)
    first_one = from_peer(first, 1)
    second_two = from_peer(second, 2)
    first_three = from_peer(first_two, 1)
    second_three = from_peer(second_one, 2)
    return [
        (first, second),
        (first_one, second_one),
        (first_two, second_two),
        (first_three, second_three),
    ]


def pair_list(count):
    return [(i, j) for i in range(count) for j in range(i, count)]


def whole(array):
    return pl.BlockSpec(array.shape, lambda *_: (0,) * array.ndim)


SMEM = pl.BlockSpec(memory_space=pltpu.SMEM)


def call(kernel, name, operands, specs, outs, out_specs=None, grid=(1,), scratch=(), flops=0):
    size = sum(x.size * x.dtype.itemsize for x in list(operands) + list(outs))
    return pl.pallas_call(
        kernel,
        grid=grid,
        in_specs=specs,
        out_specs=out_specs if out_specs is not None else [whole(out) for out in outs],
        out_shape=outs,
        scratch_shapes=list(scratch),
        compiler_params=pltpu.CompilerParams(
            dimension_semantics=("arbitrary",) * len(grid), vmem_limit_bytes=VMEM_BYTES
        ),
        cost_estimate=pl.CostEstimate(flops=flops, bytes_accessed=size, transcendentals=0),
        name=name,
    )(*operands)


def segment(rep_ref, offset, width):
    return pl.ds(pl.multiple_of((rep_ref[0] ^ offset) * width, width), width)


def rows_kernel(rep_ref, ids_ref, task_ref, column_ref, row_ref, grads_ref, *out_refs):
    row_count = grads_ref.shape[0]
    seg_rows = out_refs[0].shape[1]
    block_count = ids_ref.shape[1]
    block_rows = row_count // block_count
    square = (row_count, row_count)
    earlier = lax.broadcasted_iota(jnp.int32, square, 0) < lax.broadcasted_iota(
        jnp.int32, square, 1
    )
    counted = jnp.where(column_ref[...] == row_ref[...], 1.0, 0.0)
    rank = jnp.sum(jnp.where(earlier, counted, 0.0), axis=0, keepdims=True)
    line = lax.broadcasted_iota(jnp.int32, (LABEL_ROWS, row_count), 0)
    labels = jnp.where(line == 0, row_ref[...].astype(jnp.float32), 0.0)
    labels = jnp.where(line == 1, rank, labels).astype(jnp.bfloat16)
    for offset, out_ref in enumerate(out_refs):
        columns = segment(rep_ref, offset, seg_rows)
        for block in range(block_count):
            rows = pl.ds(block * block_rows, block_rows)
            weight = task_ref[ids_ref[0, block]]
            out_ref[rows, :] = (grads_ref[rows, columns].astype(jnp.float32) * weight).astype(
                jnp.bfloat16
            )
        if row_count < seg_rows:
            out_ref[pl.ds(row_count, LABEL_ROWS), :] = jnp.zeros(
                (LABEL_ROWS, seg_rows), jnp.bfloat16
            )
        out_ref[pl.ds(row_count, LABEL_ROWS), pl.ds(0, row_count)] = labels


def split_kernel(rep_ref, matrix_ref, *out_refs):
    for offset, out_ref in enumerate(out_refs):
        out_ref[...] = matrix_ref[:, segment(rep_ref, offset, out_ref.shape[1])]


def one_hot(block_ref, row_count, slot_count, capacity):
    labels = block_ref[pl.ds(row_count, LABEL_ROWS), pl.ds(0, row_count)].astype(jnp.float32)
    slot = (labels[0:1] * capacity + labels[1:2]).astype(jnp.int32)
    places = lax.broadcasted_iota(jnp.int32, (slot_count, row_count), 0)
    return jnp.where(places == slot, 1.0, 0.0).astype(jnp.bfloat16)


def place_kernel(row_count, *refs):
    block_refs, out_ref = refs[:-1], refs[-1]
    expert_count, _, capacity, seg_rows = out_ref.shape
    slot_count = expert_count * capacity
    for offset, block_ref in enumerate(block_refs):
        placing = one_hot(block_ref, row_count, slot_count, capacity)
        placed = multiply(placing, block_ref[pl.ds(0, row_count), :])
        placed = placed.reshape(expert_count, capacity, seg_rows)
        out_ref[:, offset] = placed.astype(jnp.bfloat16)


def unplace_kernel(block_ref, returned_ref, out_ref):
    expert_count, capacity, model_width = returned_ref.shape
    slot_count = expert_count * capacity
    row_count = out_ref.shape[1]
    placing = one_hot(block_ref, row_count, slot_count, capacity)
    returned = flat_rows(returned_ref[...])
    out_ref[0] = contract_first(placing, returned).astype(jnp.bfloat16)


def flat_rows(blocks):
    rows = blocks.shape[0] * blocks.shape[1]
    if blocks.shape[1] % 16:
        wide = blocks.astype(jnp.float32).reshape(rows, blocks.shape[2])
        return wide.astype(jnp.bfloat16)
    return blocks.reshape(rows, blocks.shape[2])


def back_kernel(incoming_ref, weight_ref, *out_refs):
    for offset, out_ref in enumerate(out_refs):
        rows = flat_rows(incoming_ref[:, offset])
        out_ref[...] = multiply(rows, weight_ref[0, 0]).astype(out_ref.dtype)


def forward_kernel(offsets, has_start, rep_ref, inputs_ref, *refs):
    out_ref = refs[-1]
    weight_refs = refs[:-1]
    gate = up = None
    if has_start:
        gate, up = weight_refs[0][0], weight_refs[0][1]
        weight_refs = weight_refs[1:]
    for place, offset in enumerate(offsets):
        gate_ref, up_ref = weight_refs[2 * place : 2 * place + 2]
        rows = inputs_ref[:, segment(rep_ref, offset, gate_ref.shape[0])]
        gate_part, up_part = multiply(rows, gate_ref[...]), multiply(rows, up_ref[...])
        gate = gate_part if gate is None else gate + gate_part
        up = up_part if up is None else up + up_part
    out_ref[0] = gate
    out_ref[1] = up


def factor_kernel(forward_ref, *refs):
    back_refs, (first_ref, second_ref) = refs[:-2], refs[-2:]
    slot_count = forward_ref.shape[1]
    half = slot_count // 2
    hidden_grad = back_refs[0][...]
    for back_ref in back_refs[1:]:
        hidden_grad = hidden_grad + back_ref[...].astype(jnp.float32)
    gate_pre, up_pre = forward_ref[0], forward_ref[1]
    sigmoid_gate = jax.nn.sigmoid(gate_pre)
    gate_act = gate_pre * sigmoid_gate
    hidden = (gate_act * up_pre).astype(jnp.bfloat16)
    first_ref[pl.ds(0, slot_count), :] = (
        hidden_grad * up_pre * sigmoid_gate * (1.0 + gate_pre * (1.0 - sigmoid_gate))
    ).astype(jnp.bfloat16)
    second_ref[pl.ds(0, slot_count), :] = (hidden_grad * gate_act).astype(jnp.bfloat16)
    first_ref[pl.ds(slot_count, half), :] = hidden[:half]
    second_ref[pl.ds(slot_count, half), :] = hidden[half:]


def slot_kernel(rep_ref, first_ref, second_ref, *refs):
    weight_refs, out_ref = refs[:-1], refs[-1]
    expert_count, capacity, _ = out_ref.shape
    slot_count = expert_count * capacity
    gate_grad = first_ref[pl.ds(0, slot_count), :]
    up_grad = second_ref[pl.ds(0, slot_count), :]
    for offset in range(len(weight_refs) // 2):
        gate_ref, up_ref = weight_refs[2 * offset : 2 * offset + 2]
        total = contract_last(gate_grad, gate_ref[...]) + contract_last(up_grad, up_ref[...])
        total = total.reshape(expert_count, capacity, total.shape[1]).astype(jnp.bfloat16)
        out_ref[:, :, segment(rep_ref, offset, total.shape[2])] = total


def weight_grad(matrix, offset, inputs_refs, incoming_ref, factor_refs):
    first_ref, second_ref = factor_refs[2 * offset : 2 * offset + 2]
    slot_count = inputs_refs[offset].shape[0]
    if matrix < 2:
        factor_ref = second_ref if matrix else first_ref
        return contract_first(inputs_refs[offset][...], factor_ref[pl.ds(0, slot_count), :])
    half = slot_count // 2
    middle = incoming_ref.shape[0] // 2
    return contract_first(
        flat_rows(incoming_ref[:middle, offset]), first_ref[pl.ds(slot_count, half), :]
    ) + contract_first(
        flat_rows(incoming_ref[middle:, offset]), second_ref[pl.ds(slot_count, half), :]
    )


def gram_kernel(count, rep_ref, *refs):
    inputs_refs, incoming_ref = refs[:count], refs[count]
    factor_refs = refs[count + 1 : 3 * count + 1]
    gram_ref, grads_ref, sums_ref = refs[3 * count + 1 :]

    @pl.when(pl.program_id(0) == 0)
    def _():
        sums_ref[...] = jnp.zeros_like(sums_ref)

    for matrix in range(3):
        for offset in range(count):
            grads_ref[rep_ref[0] ^ offset] = weight_grad(
                matrix, offset, inputs_refs, incoming_ref, factor_refs
            )
        for place, (i, j) in enumerate(pair_list(count)):
            sums_ref[pl.ds(place, 1), :] += jnp.sum(
                grads_ref[i] * grads_ref[j], axis=0, keepdims=True
            )

    @pl.when(pl.program_id(0) == pl.num_programs(0) - 1)
    def _():
        total = sums_ref[:, pl.ds(0, 128)]
        for lane in range(128, sums_ref.shape[1], 128):
            total = total + sums_ref[:, pl.ds(lane, 128)]
        gram_ref[...] = total


def merge_coefs(gram, count):
    vectors = [{rep: None} for rep in range(count)]

    def term(coef, value):
        return value if coef is None else coef * value

    def inner(left, right):
        total = None
        for i, left_coef in left.items():
            for j, right_coef in right.items():
                value = term(left_coef, term(right_coef, gram[min(i, j), max(i, j)]))
                total = value if total is None else total + value
        return total

    while len(vectors) > 1:
        merged = []
        for first, second in zip(vectors[0::2], vectors[1::2]):
            norm_first = jnp.maximum(inner(first, first), 0.0)
            norm_second = jnp.maximum(inner(second, second), 0.0)
            bound = jnp.sqrt(norm_first) * jnp.sqrt(norm_second)
            cross = jnp.minimum(jnp.maximum(inner(first, second), -bound), bound)
            coef_first = 1.0 - cross / (2.0 * (norm_first + norm_eps))
            coef_second = 1.0 - cross / (2.0 * (norm_second + norm_eps))
            joined = {rep: term(coef, coef_first) for rep, coef in first.items()}
            joined.update({rep: term(coef, coef_second) for rep, coef in second.items()})
            merged.append(joined)
        vectors = merged
    return [vectors[0][rep] for rep in range(count)]


def adam_kernel(count, rep_ref, *refs):
    gram_refs, refs = refs[:count], refs[count:]
    inputs_refs, incoming_ref = refs[:count], refs[count]
    factor_refs = refs[count + 1 : 3 * count + 1]
    first_ref, second_ref, step_ref, coef_ref = refs[3 * count + 1 :]

    @pl.when(pl.program_id(0) == 0)
    def _():
        sums = gram_refs[0][...]
        for gram_ref in gram_refs[1:]:
            sums = sums + gram_ref[...]
        sums = jnp.sum(sums, axis=1, keepdims=True)
        gram = {pair: sums[place : place + 1] for place, pair in enumerate(pair_list(count))}
        for rep, coef in enumerate(merge_coefs(gram, count)):
            coef_ref[rep] = jnp.broadcast_to(coef, coef_ref.shape[1:])

    for matrix in range(3):
        merged = None
        for offset in range(count):
            part = weight_grad(matrix, offset, inputs_refs, incoming_ref, factor_refs)
            part = part * coef_ref[rep_ref[0] ^ offset]
            merged = part if merged is None else merged + part
        first_new = beta_first * first_ref[0, matrix] + (1.0 - beta_first) * merged
        second_new = beta_second * second_ref[0, matrix] + (1.0 - beta_second) * merged * merged
        step_ref[0, matrix] = (first_new / first_fix) / (
            jnp.sqrt(second_new / second_fix) + adam_eps
        )


def adasum_adam_many(rep, inputs, incoming, factors, first_moment, second_moment):
    count = len(inputs)
    half = inputs[0].shape[0] // 2
    grads = []
    for offset, (first, second) in enumerate(factors):
        received = incoming[:, offset].reshape(2 * half, incoming.shape[3])
        hidden = jnp.concatenate([first[2 * half :], second[2 * half :]])
        grads.append(
            jnp.stack(
                [
                    contract_first(inputs[offset], first[: 2 * half]),
                    contract_first(inputs[offset], second[: 2 * half]),
                    contract_first(received, hidden),
                ]
            )
        )
    grads = jnp.stack(grads)[rep[0] ^ jnp.arange(count)]
    flat = grads.reshape(count, -1)
    gram = lax.psum(jnp.matmul(flat, flat.T, precision=lax.Precision.HIGHEST), "replica")
    coefs = jnp.eye(count, dtype=jnp.float32)
    while coefs.shape[0] > 1:
        inner = jnp.matmul(
            jnp.matmul(coefs, gram, precision=lax.Precision.HIGHEST),
            coefs.T,
            precision=lax.Precision.HIGHEST,
        )
        norms = jnp.maximum(jnp.diagonal(inner), 0.0)
        norm_first, norm_second = norms[0::2], norms[1::2]
        bound = jnp.sqrt(norm_first) * jnp.sqrt(norm_second)
        cross = jnp.clip(jnp.diagonal(inner, offset=1)[0::2], -bound, bound)
        coef_first = 1.0 - cross / (2.0 * (norm_first + norm_eps))
        coef_second = 1.0 - cross / (2.0 * (norm_second + norm_eps))
        coefs = coef_first[:, None] * coefs[0::2] + coef_second[:, None] * coefs[1::2]
    merged = jnp.sum(coefs[0][:, None, None, None] * grads, axis=0)
    first_new = beta_first * first_moment[0] + (1.0 - beta_first) * merged
    second_new = beta_second * second_moment[0] + (1.0 - beta_second) * merged * merged
    return ((first_new / first_fix) / (jnp.sqrt(second_new / second_fix) + adam_eps))[None]


def adasum_adam(rep, inputs, incoming, factors, first_moment, second_moment):
    count = len(inputs)
    if count > 4:
        return adasum_adam_many(rep, inputs, incoming, factors, first_moment, second_moment)
    slot_count, seg_rows = inputs[0].shape
    hidden_width = first_moment.shape[3]
    expert_count, _, capacity, _ = incoming.shape
    tile = min(seg_rows, 128)
    grid = (seg_rows // tile,)
    pairs = -(-len(pair_list(count)) // 8) * 8
    flat = [array for pair in factors for array in pair]
    operands = [*inputs, incoming, *flat]
    specs = [
        *[pl.BlockSpec((slot_count, tile), lambda d: (0, d)) for _ in inputs],
        pl.BlockSpec((expert_count, count, capacity, tile), lambda d: (0, 0, 0, d)),
        *[whole(array) for array in flat],
    ]
    flops = 6 * count * slot_count * seg_rows * hidden_width
    (partial,) = call(
        functools.partial(gram_kernel, count),
        "gram",
        [rep, *operands],
        [SMEM, *specs],
        [jax.ShapeDtypeStruct((pairs, 128), jnp.float32)],
        grid=grid,
        scratch=[
            pltpu.VMEM((count, tile, hidden_width), jnp.float32),
            pltpu.VMEM((pairs, hidden_width), jnp.float32),
        ],
        flops=flops,
    )
    grams = exchange([partial] * count)
    moment_spec = pl.BlockSpec((1, 3, tile, hidden_width), lambda d: (0, 0, d, 0))
    (adam_step,) = call(
        functools.partial(adam_kernel, count),
        "adam",
        [rep, *grams, *operands, first_moment, second_moment],
        [SMEM, *[whole(gram) for gram in grams], *specs, moment_spec, moment_spec],
        [jax.ShapeDtypeStruct(first_moment.shape, jnp.float32)],
        out_specs=[moment_spec],
        grid=grid,
        scratch=[pltpu.VMEM((count, 1, hidden_width), jnp.float32)],
        flops=flops,
    )
    return adam_step


def shards(
    weights, first_moment, second_moment, out_grads, routes, task_ids, task_weights, saved_inputs
):
    expert_count = lax.axis_size("expert")
    rep_count = lax.axis_size("replica")
    row_count = out_grads.shape[1]
    model_width = out_grads.shape[2]
    hidden_width = weights.shape[3]
    slot_count = saved_inputs.shape[2]
    capacity = slot_count // expert_count
    seg_rows = model_width // rep_count
    half = slot_count // 2
    offsets = range(rep_count)
    rep = lax.axis_index("replica").astype(jnp.int32).reshape(1)
    shape = jax.ShapeDtypeStruct

    block = shape((row_count + LABEL_ROWS, seg_rows), jnp.bfloat16)
    row_blocks = call(
        rows_kernel,
        "rows",
        [
            rep,
            task_ids,
            task_weights,
            routes[0],
            routes[0].reshape(1, row_count),
            out_grads[0],
        ],
        [SMEM, SMEM, SMEM]
        + [whole(x) for x in (routes[0], routes[0].reshape(1, row_count), out_grads[0])],
        [block for _ in offsets],
    )
    routed = exchange(row_blocks)

    own_weights = [weights[0, 0], weights[0, 1]]
    projections = gather_pair(*own_weights)

    inputs_home = saved_inputs[0, 0]
    inputs = exchange(
        call(
            split_kernel,
            "split",
            [rep, inputs_home],
            [SMEM, whole(inputs_home)],
            [shape((slot_count, seg_rows), jnp.bfloat16) for _ in offsets],
        )
    )

    (outgoing,) = call(
        functools.partial(place_kernel, row_count),
        "place",
        routed,
        [whole(x) for x in routed],
        [shape((expert_count, rep_count, capacity, seg_rows), jnp.bfloat16)],
        flops=2 * rep_count * slot_count * row_count * seg_rows,
    )
    incoming = lax.all_to_all(outgoing, "expert", split_axis=0, concat_axis=0, tiled=True)

    forward = None
    late = [3] if rep_count == 4 else []
    for name, group in (("forward", [k for k in offsets if k not in late]), ("rest", late)):
        if not group:
            continue
        operands = [rep, inputs_home] + ([] if forward is None else [forward])
        operands += [array for k in group for array in projections[k]]
        (forward,) = call(
            functools.partial(forward_kernel, group, forward is not None),
            name,
            operands,
            [SMEM] + [whole(x) for x in operands[1:]],
            [shape((2, slot_count, hidden_width), jnp.float32)],
            flops=4 * len(group) * slot_count * seg_rows * hidden_width,
        )

    back_shape = (slot_count, hidden_width)
    back = exchange(
        call(
            back_kernel,
            "back",
            [incoming, weights],
            [
                whole(incoming),
                pl.BlockSpec((1, 1, seg_rows, hidden_width), lambda i: (0, 2, 0, 0)),
            ],
            [shape(back_shape, jnp.bfloat16 if k else jnp.float32) for k in offsets],
            flops=2 * rep_count * slot_count * seg_rows * hidden_width,
        )
    )
    first, second = call(
        factor_kernel,
        "factors",
        [forward, *back],
        [whole(x) for x in (forward, *back)],
        [shape((slot_count + half, hidden_width), jnp.bfloat16)] * 2,
    )
    factors = gather_pair(first, second)

    operands = [rep, first, second] + [array for pair in projections for array in pair]
    (slot_grads,) = call(
        slot_kernel,
        "slots",
        operands,
        [SMEM] + [whole(x) for x in operands[1:]],
        [shape((expert_count, capacity, model_width), jnp.bfloat16)],
        flops=4 * slot_count * model_width * hidden_width,
    )
    returned = lax.all_to_all(slot_grads, "expert", split_axis=0, concat_axis=0, tiled=True)
    (input_grads,) = call(
        unplace_kernel,
        "unplace",
        [routed[0], returned],
        [whole(routed[0]), whole(returned)],
        [shape((1, row_count, model_width), jnp.bfloat16)],
        flops=2 * slot_count * row_count * model_width,
    )

    adam_step = adasum_adam(rep, inputs, incoming, factors, first_moment, second_moment)
    return (input_grads, adam_step)


def solution(mesh):
    return jax.shard_map(
        shards,
        mesh=mesh,
        in_specs=(
            P("expert", None, "replica", None),
            P("expert", None, "replica", None),
            P("expert", None, "replica", None),
            P("replica", "expert", None),
            P("replica", "expert", None),
            P("replica", "expert"),
            P(),
            P("replica", "expert", None, None),
        ),
        out_specs=(P("replica", "expert", None), P("expert", None, "replica", None)),
        check_vma=False,
    )
```

```python
import functools

import jax
import jax.numpy as jnp
from jax import lax
from jax.experimental import pallas as pl
from jax.experimental.pallas import tpu as pltpu
from jax.sharding import PartitionSpec as P

beta_first = 0.9
beta_second = 0.95
adam_eps = 1e-08
norm_eps = 1e-06
first_fix = 1.0 - (0.9**50) ** 2
second_fix = 1.0 - (0.95**50) ** 2
MIB = 1024 * 1024
LABEL_ROWS = 16


def contract_first(left, right):
    return lax.dot_general(
        left, right, (((0,), (0,)), ((), ())), preferred_element_type=jnp.float32
    )


def contract_last(left, right):
    return lax.dot_general(
        left, right, (((1,), (1,)), ((), ())), preferred_element_type=jnp.float32
    )


def multiply(left, right):
    return jnp.dot(left, right, preferred_element_type=jnp.float32)


def from_peer(array, offset):
    count = lax.axis_size("replica")
    return lax.ppermute(array, "replica", [(i, i ^ offset) for i in range(count)])


def exchange(parts):
    return [parts[0]] + [from_peer(part, k) for k, part in enumerate(parts) if k]


def gather_pair(first, second):
    count = lax.axis_size("replica")
    if count != 4:
        return list(zip(exchange([first] * count), exchange([second] * count)))
    first_two = from_peer(first, 2)
    second_one = from_peer(second, 1)
    first_one = from_peer(first, 1)
    second_two = from_peer(second, 2)
    first_three = from_peer(first_two, 1)
    second_three = from_peer(second_one, 2)
    return [
        (first, second),
        (first_one, second_one),
        (first_two, second_two),
        (first_three, second_three),
    ]


def pair_list(count):
    return [(i, j) for i in range(count) for j in range(i, count)]


SMEM = pl.BlockSpec(memory_space=pltpu.SMEM)
VMEM = pl.BlockSpec(memory_space=pltpu.VMEM)


def call(kernel, name, operands, specs, outs, out_specs=None, grid=(), scratch=(), extra=8):
    size = sum(x.size * x.dtype.itemsize for x in list(operands) + list(outs))
    return pl.pallas_call(
        kernel,
        grid=grid,
        in_specs=specs,
        out_specs=out_specs if out_specs is not None else [VMEM for _ in outs],
        out_shape=outs,
        scratch_shapes=list(scratch),
        compiler_params=pltpu.CompilerParams(
            dimension_semantics=("arbitrary",) * len(grid),
            vmem_limit_bytes=min(56 * MIB, size + extra * MIB),
        ),
        cost_estimate=pl.CostEstimate(flops=0, bytes_accessed=0, transcendentals=0),
        name=name,
    )(*operands)


def segment(rep_ref, offset, width):
    return pl.ds(pl.multiple_of((rep_ref[0] ^ offset) * width, width), width)


def rows_kernel(expert_count, rep_ref, ids_ref, task_ref, row_ref, grads_ref, *out_refs):
    row_count = grads_ref.shape[0]
    seg_rows = out_refs[0].shape[1]
    block_count = ids_ref.shape[1]
    block_rows = row_count // block_count
    square = (row_count, row_count)
    earlier = lax.broadcasted_iota(jnp.int32, square, 0) < lax.broadcasted_iota(
        jnp.int32, square, 1
    )
    experts = lax.broadcasted_iota(jnp.int32, (expert_count, row_count), 0)
    chosen = jnp.where(experts == row_ref[...], 1.0, 0.0)
    before = multiply(
        chosen.astype(jnp.bfloat16), jnp.where(earlier, 1.0, 0.0).astype(jnp.bfloat16)
    )
    rank = jnp.sum(chosen * before, axis=0, keepdims=True)
    line = lax.broadcasted_iota(jnp.int32, (LABEL_ROWS, row_count), 0)
    labels = jnp.where(line == 0, row_ref[...].astype(jnp.float32), 0.0)
    labels = jnp.where(line == 1, rank, labels).astype(jnp.bfloat16)
    for offset, out_ref in enumerate(out_refs):
        columns = segment(rep_ref, offset, seg_rows)
        for block in range(block_count):
            rows = pl.ds(block * block_rows, block_rows)
            weight = task_ref[ids_ref[0, block]]
            out_ref[rows, :] = (grads_ref[rows, columns].astype(jnp.float32) * weight).astype(
                jnp.bfloat16
            )
        if row_count < seg_rows:
            out_ref[pl.ds(row_count, LABEL_ROWS), :] = jnp.zeros(
                (LABEL_ROWS, seg_rows), jnp.bfloat16
            )
        out_ref[pl.ds(row_count, LABEL_ROWS), pl.ds(0, row_count)] = labels


def split_kernel(rep_ref, matrix_ref, *out_refs):
    for offset, out_ref in enumerate(out_refs):
        out_ref[...] = matrix_ref[:, segment(rep_ref, offset, out_ref.shape[1])]


def one_hot(block_ref, row_count, slot_count, capacity):
    labels = block_ref[pl.ds(row_count, LABEL_ROWS), pl.ds(0, row_count)].astype(jnp.float32)
    slot = (labels[0:1] * capacity + labels[1:2]).astype(jnp.int32)
    places = lax.broadcasted_iota(jnp.int32, (slot_count, row_count), 0)
    return jnp.where(places == slot, 1.0, 0.0).astype(jnp.bfloat16)


def place_kernel(row_count, *refs):
    block_refs, out_ref = refs[:-1], refs[-1]
    expert_count, _, capacity, seg_rows = out_ref.shape
    slot_count = expert_count * capacity
    for offset, block_ref in enumerate(block_refs):
        placing = one_hot(block_ref, row_count, slot_count, capacity)
        placed = multiply(placing, block_ref[pl.ds(0, row_count), :])
        placed = placed.reshape(expert_count, capacity, seg_rows)
        out_ref[:, offset] = placed.astype(jnp.bfloat16)


def unplace_kernel(block_ref, returned_ref, out_ref):
    expert_count, capacity, model_width = returned_ref.shape
    slot_count = expert_count * capacity
    row_count = out_ref.shape[1]
    placing = one_hot(block_ref, row_count, slot_count, capacity)
    returned = flat_rows(returned_ref[...])
    out_ref[0] = contract_first(placing, returned).astype(jnp.bfloat16)


def flat_rows(blocks):
    rows = blocks.shape[0] * blocks.shape[1]
    if blocks.shape[1] % 16:
        wide = blocks.astype(jnp.float32).reshape(rows, blocks.shape[2])
        return wide.astype(jnp.bfloat16)
    return blocks.reshape(rows, blocks.shape[2])


def back_kernel(incoming_ref, weight_ref, *out_refs):
    for offset, out_ref in enumerate(out_refs):
        rows = flat_rows(incoming_ref[:, offset])
        out_ref[...] = multiply(rows, weight_ref[...]).astype(out_ref.dtype)


def forward_kernel(offsets, has_start, rep_ref, inputs_ref, *refs):
    out_ref = refs[-1]
    weight_refs = refs[:-1]
    gate = up = None
    if has_start:
        gate, up = weight_refs[0][0], weight_refs[0][1]
        weight_refs = weight_refs[1:]
    for place, offset in enumerate(offsets):
        gate_ref, up_ref = weight_refs[2 * place : 2 * place + 2]
        rows = inputs_ref[:, segment(rep_ref, offset, gate_ref.shape[0])]
        gate_part, up_part = multiply(rows, gate_ref[...]), multiply(rows, up_ref[...])
        gate = gate_part if gate is None else gate + gate_part
        up = up_part if up is None else up + up_part
    out_ref[0] = gate
    out_ref[1] = up


def hidden_kernel(forward_ref, first_ref, second_ref):
    half = forward_ref.shape[1] // 2
    for part, out_ref in enumerate((first_ref, second_ref)):
        rows = pl.ds(part * half, half)
        gate_pre = forward_ref[0, rows]
        gate_act = gate_pre * jax.nn.sigmoid(gate_pre)
        out_ref[...] = (gate_act * forward_ref[1, rows]).astype(jnp.bfloat16)


def factor_kernel(forward_ref, *refs):
    back_refs, (gate_ref, up_ref) = refs[:-2], refs[-2:]
    hidden_grad = back_refs[0][...]
    for back_ref in back_refs[1:]:
        hidden_grad = hidden_grad + back_ref[...].astype(jnp.float32)
    gate_pre, up_pre = forward_ref[0], forward_ref[1]
    sigmoid_gate = jax.nn.sigmoid(gate_pre)
    gate_act = gate_pre * sigmoid_gate
    gate_ref[...] = (
        hidden_grad * up_pre * sigmoid_gate * (1.0 + gate_pre * (1.0 - sigmoid_gate))
    ).astype(jnp.bfloat16)
    up_ref[...] = (hidden_grad * gate_act).astype(jnp.bfloat16)


def slot_kernel(rep_ref, first_ref, second_ref, *refs):
    weight_refs, out_ref = refs[:-1], refs[-1]
    expert_count, capacity, _ = out_ref.shape
    gate_grad, up_grad = first_ref[...], second_ref[...]
    for offset in range(len(weight_refs) // 2):
        gate_ref, up_ref = weight_refs[2 * offset : 2 * offset + 2]
        total = contract_last(gate_grad, gate_ref[...]) + contract_last(up_grad, up_ref[...])
        total = total.reshape(expert_count, capacity, total.shape[1]).astype(jnp.bfloat16)
        out_ref[:, :, segment(rep_ref, offset, total.shape[2])] = total


def gram_kernel(count, offsets, place, rep_ref, *refs):
    if place:
        before_ref, earlier_ref, refs = refs[0], refs[1], refs[2:]
    incoming_ref, operand_refs, grads_ref, gram_ref = refs[0], refs[1:-2], refs[-2], refs[-1]
    middle = incoming_ref.shape[0] // 2
    seg_rows, hidden_width = grads_ref.shape[2:]
    for at, offset in enumerate(offsets):
        inputs_ref, gate_ref, up_ref, first_ref, second_ref = operand_refs[5 * at : 5 * at + 5]
        grads_ref[at, 0] = contract_first(inputs_ref[...], gate_ref[...])
        grads_ref[at, 1] = contract_first(inputs_ref[...], up_ref[...])
        grads_ref[at, 2] = contract_first(
            flat_rows(incoming_ref[:middle, offset]), first_ref[...]
        ) + contract_first(flat_rows(incoming_ref[middle:, offset]), second_ref[...])
    gram_ref[...] = before_ref[...] if place else jnp.zeros_like(gram_ref)
    known = list(range(place)) + list(offsets)
    pairs = [(i, j) for i, j in pair_list(len(known)) if j >= place]
    lines = 8

    def add(step, sums):
        rows = pl.ds(pl.multiple_of(lax.rem(step, seg_rows // lines) * lines, lines), lines)
        matrix = lax.div(step, seg_rows // lines)
        blocks = [earlier_ref[at, matrix, rows] for at in range(place)]
        blocks += [grads_ref[at, matrix, rows] for at in range(len(offsets))]
        return tuple(total + blocks[i] * blocks[j] for total, (i, j) in zip(sums, pairs))

    zero = jnp.zeros((lines, hidden_width), jnp.float32)
    sums = lax.fori_loop(0, 3 * (seg_rows // lines), add, tuple(zero for _ in pairs))
    for total, (i, j) in zip(sums, pairs):
        total = jnp.sum(total, axis=0, keepdims=True)
        part = total[:, :128]
        for lane in range(128, hidden_width, 128):
            part = part + total[:, lane : lane + 128]
        first, second = rep_ref[0] ^ known[i], rep_ref[0] ^ known[j]
        row = jnp.minimum(first, second) * count + jnp.maximum(first, second)
        gram_ref[pl.ds(row, 1), :] = part


def merge_coefs(gram, count):
    vectors = [{rep: None} for rep in range(count)]

    def term(coef, value):
        return value if coef is None else coef * value

    def inner(left, right):
        total = None
        for i, left_coef in left.items():
            for j, right_coef in right.items():
                value = term(left_coef, term(right_coef, gram[min(i, j), max(i, j)]))
                total = value if total is None else total + value
        return total

    while len(vectors) > 1:
        merged = []
        for first, second in zip(vectors[0::2], vectors[1::2]):
            norm_first = jnp.maximum(inner(first, first), 0.0)
            norm_second = jnp.maximum(inner(second, second), 0.0)
            bound = jnp.sqrt(norm_first) * jnp.sqrt(norm_second)
            cross = jnp.minimum(jnp.maximum(inner(first, second), -bound), bound)
            coef_first = 1.0 - cross / (2.0 * (norm_first + norm_eps))
            coef_second = 1.0 - cross / (2.0 * (norm_second + norm_eps))
            joined = {rep: term(coef, coef_first) for rep, coef in first.items()}
            joined.update({rep: term(coef, coef_second) for rep, coef in second.items()})
            merged.append(joined)
        vectors = merged
    return [vectors[0][rep] for rep in range(count)]


def adam_kernel(count, places, rep_ref, *refs):
    gram_refs, grads_refs = refs[:count], refs[count : count + len(places)]
    first_ref, second_ref, step_ref, coef_ref = refs[count + len(places) :]
    hidden_width = step_ref.shape[3]

    @pl.when(pl.program_id(0) == 0)
    def _():
        sums = gram_refs[0][...]
        for gram_ref in gram_refs[1:]:
            sums = sums + gram_ref[...]
        sums = jnp.sum(sums, axis=1, keepdims=True)
        gram = {(i, j): sums[i * count + j : i * count + j + 1] for i, j in pair_list(count)}
        for rep, coef in enumerate(merge_coefs(gram, count)):
            coef_ref[rep] = jnp.broadcast_to(coef, coef_ref.shape[1:])

    matrix = pl.program_id(0)
    lines = 16

    def step(index, _):
        rows = pl.ds(pl.multiple_of(index * lines, lines), lines)
        merged = None
        for grads_ref, offsets in zip(grads_refs, places):
            for at, offset in enumerate(offsets):
                part = grads_ref[at, matrix, rows] * coef_ref[rep_ref[0] ^ offset]
                merged = part if merged is None else merged + part
        first_new = (beta_first / first_fix) * first_ref[0, 0, rows] + (
            (1.0 - beta_first) / first_fix
        ) * merged
        second_new = (beta_second / second_fix) * second_ref[0, 0, rows] + (
            (1.0 - beta_second) / second_fix
        ) * (merged * merged)
        step_ref[0, 0, rows] = first_new / (jnp.sqrt(second_new) + adam_eps)
        return 0

    lax.fori_loop(0, step_ref.shape[2] // lines, step, 0)


def adasum_adam_many(rep, inputs, incoming, factors, first_moment, second_moment):
    count = len(inputs)
    half = inputs[0].shape[0] // 2
    grads = []
    for offset, (gate_grad, up_grad, *halves) in enumerate(factors):
        received = incoming[:, offset].reshape(2 * half, incoming.shape[3])
        hidden = jnp.concatenate(halves)
        grads.append(
            jnp.stack(
                [
                    contract_first(inputs[offset], gate_grad),
                    contract_first(inputs[offset], up_grad),
                    contract_first(received, hidden),
                ]
            )
        )
    grads = jnp.stack(grads)[rep[0] ^ jnp.arange(count)]
    flat = grads.reshape(count, -1)
    gram = lax.psum(jnp.matmul(flat, flat.T, precision=lax.Precision.HIGHEST), "replica")
    coefs = jnp.eye(count, dtype=jnp.float32)
    while coefs.shape[0] > 1:
        inner = jnp.matmul(
            jnp.matmul(coefs, gram, precision=lax.Precision.HIGHEST),
            coefs.T,
            precision=lax.Precision.HIGHEST,
        )
        norms = jnp.maximum(jnp.diagonal(inner), 0.0)
        norm_first, norm_second = norms[0::2], norms[1::2]
        bound = jnp.sqrt(norm_first) * jnp.sqrt(norm_second)
        cross = jnp.clip(jnp.diagonal(inner, offset=1)[0::2], -bound, bound)
        coef_first = 1.0 - cross / (2.0 * (norm_first + norm_eps))
        coef_second = 1.0 - cross / (2.0 * (norm_second + norm_eps))
        coefs = coef_first[:, None] * coefs[0::2] + coef_second[:, None] * coefs[1::2]
    merged = jnp.sum(coefs[0][:, None, None, None] * grads, axis=0)
    first_new = beta_first * first_moment[0] + (1.0 - beta_first) * merged
    second_new = beta_second * second_moment[0] + (1.0 - beta_second) * merged * merged
    return ((first_new / first_fix) / (jnp.sqrt(second_new / second_fix) + adam_eps))[None]


def adasum_adam(rep, inputs, incoming, factors, first_moment, second_moment):
    count = len(inputs)
    if count > 4:
        return adasum_adam_many(rep, inputs, incoming, factors, first_moment, second_moment)
    seg_rows, hidden_width = first_moment.shape[2:]
    shape = jax.ShapeDtypeStruct
    groups = [[k for k in range(count) if k < 3], [k for k in range(count) if k == 3]]
    groups = [group for group in groups if group]
    grads, gram, place = [], None, 0
    for group in groups:
        operands = [rep] if gram is None else [rep, gram, grads[0]]
        operands += [incoming] + [x for k in group for x in (inputs[k], *factors[k])]
        more, gram = call(
            functools.partial(gram_kernel, count, group, place),
            "gram_late" if place else "gram",
            operands,
            [SMEM] + [VMEM] * (len(operands) - 1),
            [
                shape((len(group), 3, seg_rows, hidden_width), jnp.float32),
                shape((max(8, count * count), 128), jnp.float32),
            ],
        )
        grads.append(more)
        place += len(group)
    grams = exchange([gram] * count)
    moment_spec = pl.BlockSpec((1, 1, seg_rows, hidden_width), lambda m: (0, m, 0, 0))
    (adam_step,) = call(
        functools.partial(adam_kernel, count, groups),
        "adam",
        [rep, *grams, *grads, first_moment, second_moment],
        [SMEM] + [VMEM] * (len(grams) + len(grads)) + [moment_spec, moment_spec],
        [shape(first_moment.shape, jnp.float32)],
        out_specs=[moment_spec],
        grid=(3,),
        scratch=[pltpu.VMEM((count, 1, hidden_width), jnp.float32)],
    )
    return adam_step


def shards(
    weights, first_moment, second_moment, out_grads, routes, task_ids, task_weights, saved_inputs
):
    expert_count = lax.axis_size("expert")
    rep_count = lax.axis_size("replica")
    row_count = out_grads.shape[1]
    model_width = out_grads.shape[2]
    hidden_width = weights.shape[3]
    slot_count = saved_inputs.shape[2]
    capacity = slot_count // expert_count
    seg_rows = model_width // rep_count
    half = slot_count // 2
    offsets = range(rep_count)
    rep = lax.axis_index("replica").astype(jnp.int32).reshape(1)
    shape = jax.ShapeDtypeStruct

    block = shape((row_count + LABEL_ROWS, seg_rows), jnp.bfloat16)
    row_blocks = call(
        functools.partial(rows_kernel, expert_count),
        "rows",
        [rep, task_ids, task_weights, routes[0].reshape(1, row_count), out_grads[0]],
        [SMEM, SMEM, SMEM, VMEM, VMEM],
        [block for _ in offsets],
    )
    routed = exchange(row_blocks)

    own_weights = [weights[0, 0], weights[0, 1]]
    projections = gather_pair(*own_weights)

    inputs_home = saved_inputs[0, 0]
    inputs = exchange(
        call(
            split_kernel,
            "split",
            [rep, inputs_home],
            [SMEM, VMEM],
            [shape((slot_count, seg_rows), jnp.bfloat16) for _ in offsets],
        )
    )

    (outgoing,) = call(
        functools.partial(place_kernel, row_count),
        "place",
        routed,
        [VMEM] * len(routed),
        [shape((expert_count, rep_count, capacity, seg_rows), jnp.bfloat16)],
    )
    incoming = lax.all_to_all(outgoing, "expert", split_axis=0, concat_axis=0, tiled=True)

    forward = None
    late = [3] if rep_count == 4 else []
    for name, group in (("forward", [k for k in offsets if k not in late]), ("rest", late)):
        if not group:
            continue
        operands = [rep, inputs_home] + ([] if forward is None else [forward])
        operands += [array for k in group for array in projections[k]]
        (forward,) = call(
            functools.partial(forward_kernel, group, forward is not None),
            name,
            operands,
            [SMEM] + [VMEM] * (len(operands) - 1),
            [shape((2, slot_count, hidden_width), jnp.float32)],
        )

    back_shape = (slot_count, hidden_width)
    back = exchange(
        call(
            back_kernel,
            "back",
            [incoming, weights[0, 2]],
            [VMEM, VMEM],
            [shape(back_shape, jnp.bfloat16 if k else jnp.float32) for k in offsets],
        )
    )
    half_shape = shape((half, hidden_width), jnp.bfloat16)
    hidden = gather_pair(
        *call(hidden_kernel, "hidden", [forward], [VMEM], [half_shape, half_shape])
    )
    forward, inputs = lax.optimization_barrier((forward, inputs))
    full_shape = shape((slot_count, hidden_width), jnp.bfloat16)
    gate_grad, up_grad = call(
        factor_kernel,
        "factors",
        [forward, *back],
        [VMEM] * (1 + len(back)),
        [full_shape, full_shape],
    )
    factors = [a + b for a, b in zip(gather_pair(gate_grad, up_grad), hidden)]

    operands = [rep, gate_grad, up_grad] + [array for pair in projections for array in pair]
    (slot_grads,) = call(
        slot_kernel,
        "slots",
        operands,
        [SMEM] + [VMEM] * (len(operands) - 1),
        [shape((expert_count, capacity, model_width), jnp.bfloat16)],
    )
    returned = lax.all_to_all(slot_grads, "expert", split_axis=0, concat_axis=0, tiled=True)
    (input_grads,) = call(
        unplace_kernel,
        "unplace",
        [routed[0], returned],
        [VMEM, VMEM],
        [shape((1, row_count, model_width), jnp.bfloat16)],
    )

    adam_step = adasum_adam(rep, inputs, incoming, factors, first_moment, second_moment)
    return (input_grads, adam_step)


def solution(mesh):
    return jax.shard_map(
        shards,
        mesh=mesh,
        in_specs=(
            P("expert", None, "replica", None),
            P("expert", None, "replica", None),
            P("expert", None, "replica", None),
            P("replica", "expert", None),
            P("replica", "expert", None),
            P("replica", "expert"),
            P(),
            P("replica", "expert", None, None),
        ),
        out_specs=(P("replica", "expert", None), P("expert", None, "replica", None)),
        check_vma=False,
    )
```

```python
import functools

import jax
import jax.numpy as jnp
from jax import lax
from jax.experimental import pallas as pl
from jax.experimental.pallas import tpu as pltpu
from jax.sharding import PartitionSpec as P

beta_first = 0.9
beta_second = 0.95
adam_eps = 1e-08
norm_eps = 1e-06
first_fix = 1.0 - (0.9**50) ** 2
second_fix = 1.0 - (0.95**50) ** 2
MIB = 1024 * 1024
LABEL_ROWS = 16


def contract_first(left, right):
    return lax.dot_general(
        left, right, (((0,), (0,)), ((), ())), preferred_element_type=jnp.float32
    )


def contract_last(left, right):
    return lax.dot_general(
        left, right, (((1,), (1,)), ((), ())), preferred_element_type=jnp.float32
    )


def multiply(left, right):
    return jnp.dot(left, right, preferred_element_type=jnp.float32)


def from_peer(array, offset):
    count = lax.axis_size("replica")
    return lax.ppermute(array, "replica", [(i, i ^ offset) for i in range(count)])


def across_chips(parts):
    count = lax.axis_size("expert")
    return [parts[0]] + [
        lax.ppermute(part, "expert", [(i, i ^ 2 * k) for i in range(count)])
        for k, part in enumerate(parts)
        if k
    ]


def pick_kernel(chips, *refs):
    block_refs = [ref.at[k] for ref in refs[chips:] for k in range(ref.shape[0])]
    for part_ref, block_ref in zip(refs[:chips], block_refs):
        block_ref[...] = part_ref[1]


def finish_spread(came, after=(), pieces=1):
    count = lax.axis_size("expert")
    chips = len(came)
    block = jax.ShapeDtypeStruct((chips // pieces,) + came[0].shape[1:], came[0].dtype)
    others = call(
        functools.partial(pick_kernel, chips),
        "pick",
        came,
        [VMEM] * chips,
        [block] * pieces,
        after=after,
    )
    swapped = [lax.ppermute(x, "expert", [(i, i ^ 1) for i in range(count)]) for x in others]
    return [*came, *swapped]


def spread_block(chips, refs, offset):
    if offset % 2 == 0:
        return refs[offset // 2].at[0]
    blocks = [ref.at[k] for ref in refs[chips:] for k in range(ref.shape[0])]
    return blocks[offset // 2]


def exchange(parts):
    return [parts[0]] + [from_peer(part, k) for k, part in enumerate(parts) if k]


def cut_kernel(from_two_ref, from_one_ref, first_ref, second_ref):
    first_ref[...] = from_two_ref[0]
    second_ref[...] = from_one_ref[1]


def gather_near(payload):
    count = lax.axis_size("replica")
    if count != 4:
        return exchange([payload] * count)
    from_two = from_peer(payload, 2)
    return [payload, from_peer(payload, 1), from_two]


def gather_rest(near, after):
    whole = [(part,) for part in near]
    if lax.axis_size("replica") != 4:
        return whole
    half = jax.ShapeDtypeStruct(near[0].shape[1:], near[0].dtype)
    first, second = call(
        cut_kernel, "cut", [near[2], near[1]], [VMEM, VMEM], [half, half], after=after
    )
    return whole + [(from_peer(first, 1), from_peer(second, 2))]


def halves(refs):
    return refs if len(refs) == 2 else (refs[0].at[0], refs[0].at[1])


def regroup(refs, lengths):
    groups, at = [], 0
    for length in lengths:
        groups.append(refs[at : at + length])
        at += length
    return groups


def flatten(groups):
    return [array for group in groups for array in group]


def pair_list(count):
    return [(i, j) for i in range(count) for j in range(i, count)]


SMEM = pl.BlockSpec(memory_space=pltpu.SMEM)
VMEM = pl.BlockSpec(memory_space=pltpu.VMEM)


def call(
    kernel, name, operands, specs, outs, out_specs=None, grid=(), scratch=(), after=(), cost=0
):
    size = sum(x.size * x.dtype.itemsize for x in list(operands) + list(outs))
    taken = len(operands)

    def body(*refs):
        kernel(*refs[:taken], *refs[taken + len(after) :])

    return pl.pallas_call(
        body,
        grid=grid,
        in_specs=list(specs) + [pl.BlockSpec(memory_space=pl.ANY)] * len(after),
        out_specs=out_specs if out_specs is not None else [VMEM for _ in outs],
        out_shape=outs,
        scratch_shapes=list(scratch),
        compiler_params=pltpu.CompilerParams(
            dimension_semantics=("arbitrary",) * len(grid),
            vmem_limit_bytes=min(56 * MIB, size + 8 * MIB),
        ),
        cost_estimate=pl.CostEstimate(flops=0, bytes_accessed=cost, transcendentals=0),
        name=name,
    )(*operands, *after)


def segment(pos_ref, offset, width):
    return pl.ds(pl.multiple_of((pos_ref[0] ^ offset) * width, width), width)


def rows_kernel(expert_count, pos_ref, ids_ref, task_ref, row_ref, grads_ref, *out_refs):
    row_count = grads_ref.shape[0]
    seg_rows = out_refs[0].shape[1]
    block_count = ids_ref.shape[1]
    block_rows = row_count // block_count
    square = (row_count, row_count)
    earlier = lax.broadcasted_iota(jnp.int32, square, 0) < lax.broadcasted_iota(
        jnp.int32, square, 1
    )
    experts = lax.broadcasted_iota(jnp.int32, (expert_count, row_count), 0)
    chosen = jnp.where(experts == row_ref[...], 1.0, 0.0)
    before = multiply(
        chosen.astype(jnp.bfloat16), jnp.where(earlier, 1.0, 0.0).astype(jnp.bfloat16)
    )
    rank = jnp.sum(chosen * before, axis=0, keepdims=True)
    line = lax.broadcasted_iota(jnp.int32, (LABEL_ROWS, row_count), 0)
    labels = jnp.where(line == 0, row_ref[...].astype(jnp.float32), 0.0)
    labels = jnp.where(line == 1, rank, labels).astype(jnp.bfloat16)
    for offset, out_ref in enumerate(out_refs):
        columns = segment(pos_ref, offset, seg_rows)
        for block in range(block_count):
            rows = pl.ds(block * block_rows, block_rows)
            weight = task_ref[ids_ref[0, block]]
            out_ref[rows, :] = (grads_ref[rows, columns].astype(jnp.float32) * weight).astype(
                jnp.bfloat16
            )
        if row_count < seg_rows:
            out_ref[pl.ds(row_count, LABEL_ROWS), :] = jnp.zeros(
                (LABEL_ROWS, seg_rows), jnp.bfloat16
            )
        out_ref[pl.ds(row_count, LABEL_ROWS), pl.ds(0, row_count)] = labels


def split_kernel(pos_ref, matrix_ref, *out_refs):
    for offset, out_ref in enumerate(out_refs):
        out_ref[...] = matrix_ref[:, segment(pos_ref, offset, out_ref.shape[1])]


def one_hot(block_ref, row_count, slot_count, capacity):
    labels = block_ref[pl.ds(row_count, LABEL_ROWS), pl.ds(0, row_count)].astype(jnp.float32)
    slot = (labels[0:1] * capacity + labels[1:2]).astype(jnp.int32)
    places = lax.broadcasted_iota(jnp.int32, (slot_count, row_count), 0)
    return jnp.where(places == slot, 1.0, 0.0).astype(jnp.bfloat16)


def place_kernel(count, pos_ref, *refs):
    block_refs, out_refs, placed_ref = refs[:count], refs[count:-1], refs[-1]
    _, expert_count, capacity, seg_rows = placed_ref.shape
    slot_count = expert_count * capacity
    row_count = block_refs[0].shape[0] - LABEL_ROWS
    for offset, block_ref in enumerate(block_refs):
        placing = one_hot(block_ref, row_count, slot_count, capacity)
        placed = multiply(placing, block_ref[pl.ds(0, row_count), :])
        placed = placed.reshape(expert_count, capacity, seg_rows)
        placed_ref[offset] = placed.astype(jnp.bfloat16)
        for expert in range(expert_count):
            out_refs[expert // 2][expert % 2, offset] = placed_ref[offset, pos_ref[1] ^ expert]


def unplace_kernel(pos_ref, block_ref, *refs):
    returned_refs, out_ref, slots_ref = refs[:-2], refs[-2], refs[-1]
    expert_count, capacity, _ = slots_ref.shape
    slot_count = expert_count * capacity
    row_count = out_ref.shape[1]
    placing = one_hot(block_ref, row_count, slot_count, capacity)
    for expert in range(expert_count):
        block_ref = spread_block(expert_count // 2, returned_refs, expert)
        slots_ref[pos_ref[1] ^ expert] = block_ref[...]
    out_ref[0] = contract_first(placing, flat_rows(slots_ref[...])).astype(jnp.bfloat16)


def flat_rows(blocks):
    rows = blocks.shape[0] * blocks.shape[1]
    if blocks.shape[1] % 16:
        wide = blocks.astype(jnp.float32).reshape(rows, blocks.shape[2])
        return wide.astype(jnp.bfloat16)
    return blocks.reshape(rows, blocks.shape[2])


def back_kernel(chips, arrays, pos_ref, weight_ref, *refs):
    came_refs, incoming_ref, out_refs = refs[:arrays], refs[arrays], refs[arrays + 1 :]
    for offset, out_ref in enumerate(out_refs):
        for expert in range(2 * chips):
            block_ref = spread_block(chips, came_refs, expert)
            incoming_ref[offset, pos_ref[1] ^ expert] = block_ref[offset]
        rows = flat_rows(incoming_ref[offset])
        out_ref[...] = multiply(rows, weight_ref[...]).astype(out_ref.dtype)


def forward_kernel(offsets, lengths, has_start, pos_ref, inputs_ref, *refs):
    out_ref = refs[-1]
    weight_refs = refs[:-1]
    gate = up = None
    if has_start:
        gate, up = weight_refs[0][0], weight_refs[0][1]
        weight_refs = weight_refs[1:]
    for offset, group in zip(offsets, regroup(weight_refs, lengths)):
        gate_ref, up_ref = halves(group)
        rows = inputs_ref[:, segment(pos_ref, offset, gate_ref.shape[0])]
        gate_part, up_part = multiply(rows, gate_ref[...]), multiply(rows, up_ref[...])
        gate = gate_part if gate is None else gate + gate_part
        up = up_part if up is None else up + up_part
    out_ref[0] = gate
    out_ref[1] = up


def factor_kernel(forward_ref, *refs):
    back_refs, out_ref = refs[:-1], refs[-1]
    slot_count = forward_ref.shape[1]
    half = slot_count // 2
    hidden_grad = back_refs[0][...]
    for back_ref in back_refs[1:]:
        hidden_grad = hidden_grad + back_ref[...].astype(jnp.float32)
    gate_pre, up_pre = forward_ref[0], forward_ref[1]
    sigmoid_gate = jax.nn.sigmoid(gate_pre)
    gate_act = gate_pre * sigmoid_gate
    hidden = (gate_act * up_pre).astype(jnp.bfloat16)
    gate_grad = hidden_grad * up_pre * sigmoid_gate * (1.0 + gate_pre * (1.0 - sigmoid_gate))
    out_ref[0, pl.ds(0, slot_count)] = gate_grad.astype(jnp.bfloat16)
    out_ref[1, pl.ds(0, slot_count)] = (hidden_grad * gate_act).astype(jnp.bfloat16)
    for part in range(2):
        out_ref[part, pl.ds(slot_count, half)] = hidden[part * half : (part + 1) * half]


def slot_kernel(lengths, pos_ref, factor_ref, *refs):
    chips = refs[-1].shape[1] // 2
    weight_refs, out_refs, slots_ref = refs[: -chips - 1], refs[-chips - 1 : -1], refs[-1]
    _, expert_count, capacity, seg_rows = slots_ref.shape
    rows = pl.ds(0, expert_count * capacity)
    gate_grad, up_grad = factor_ref[0, rows], factor_ref[1, rows]
    for offset, group in enumerate(regroup(weight_refs, lengths)):
        gate_ref, up_ref = halves(group)
        total = contract_last(gate_grad, gate_ref[...]) + contract_last(up_grad, up_ref[...])
        total = total.reshape(expert_count, capacity, seg_rows)
        slots_ref[offset] = total.astype(jnp.bfloat16)
        columns = segment(pos_ref, offset, seg_rows)
        for expert in range(expert_count):
            out_ref = out_refs[expert // 2]
            out_ref[expert % 2, :, columns] = slots_ref[offset, pos_ref[1] ^ expert]


def gram_kernel(count, offsets, lengths, place, pos_ref, *refs):
    if place:
        before_ref, earlier_ref, refs = refs[0], refs[1], refs[2:]
    incoming_ref, operand_refs, grads_ref, gram_ref = refs[0], refs[1:-2], refs[-2], refs[-1]
    middle = incoming_ref.shape[1] // 2
    seg_rows, hidden_width = grads_ref.shape[2:]
    groups = regroup(operand_refs, lengths)
    for at, offset in enumerate(offsets):
        (inputs_ref,), factor_refs = groups[2 * at : 2 * at + 2]
        slot_count = inputs_ref.shape[0]
        rest = pl.ds(slot_count, slot_count // 2)
        gate_ref, up_ref = (ref.at[pl.ds(0, slot_count)] for ref in halves(factor_refs))
        first_ref, second_ref = (ref.at[rest] for ref in halves(factor_refs))
        grads_ref[at, 0] = contract_first(inputs_ref[...], gate_ref[...])
        grads_ref[at, 1] = contract_first(inputs_ref[...], up_ref[...])
        grads_ref[at, 2] = contract_first(
            flat_rows(incoming_ref[offset, :middle]), first_ref[...]
        ) + contract_first(flat_rows(incoming_ref[offset, middle:]), second_ref[...])
    gram_ref[...] = before_ref[...] if place else jnp.zeros_like(gram_ref)
    known = list(range(place)) + list(offsets)
    pairs = [(i, j) for i, j in pair_list(len(known)) if j >= place]
    lines = 8

    def add(step, sums):
        rows = pl.ds(pl.multiple_of(lax.rem(step, seg_rows // lines) * lines, lines), lines)
        matrix = lax.div(step, seg_rows // lines)
        blocks = [earlier_ref[at, matrix, rows] for at in range(place)]
        blocks += [grads_ref[at, matrix, rows] for at in range(len(offsets))]
        return tuple(total + blocks[i] * blocks[j] for total, (i, j) in zip(sums, pairs))

    zero = jnp.zeros((lines, hidden_width), jnp.float32)
    sums = lax.fori_loop(0, 3 * (seg_rows // lines), add, tuple(zero for _ in pairs), unroll=4)
    for total, (i, j) in zip(sums, pairs):
        total = jnp.sum(total, axis=0, keepdims=True)
        part = total[:, :128]
        for lane in range(128, hidden_width, 128):
            part = part + total[:, lane : lane + 128]
        first, second = pos_ref[0] ^ known[i], pos_ref[0] ^ known[j]
        row = jnp.minimum(first, second) * count + jnp.maximum(first, second)
        gram_ref[pl.ds(row, 1), :] = part


def merge_coefs(gram, count):
    vectors = [{rep: None} for rep in range(count)]

    def term(coef, value):
        return value if coef is None else coef * value

    def inner(left, right):
        total = None
        for i, left_coef in left.items():
            for j, right_coef in right.items():
                value = term(left_coef, term(right_coef, gram[min(i, j), max(i, j)]))
                total = value if total is None else total + value
        return total

    while len(vectors) > 1:
        merged = []
        for first, second in zip(vectors[0::2], vectors[1::2]):
            norm_first = jnp.maximum(inner(first, first), 0.0)
            norm_second = jnp.maximum(inner(second, second), 0.0)
            bound = jnp.sqrt(norm_first) * jnp.sqrt(norm_second)
            cross = jnp.minimum(jnp.maximum(inner(first, second), -bound), bound)
            coef_first = 1.0 - cross / (2.0 * (norm_first + norm_eps))
            coef_second = 1.0 - cross / (2.0 * (norm_second + norm_eps))
            joined = {rep: term(coef, coef_first) for rep, coef in first.items()}
            joined.update({rep: term(coef, coef_second) for rep, coef in second.items()})
            merged.append(joined)
        vectors = merged
    return [vectors[0][rep] for rep in range(count)]


def adam_kernel(count, places, pos_ref, *refs):
    gram_refs, grads_refs = refs[:count], refs[count : count + len(places)]
    first_ref, second_ref, step_ref, coef_ref = refs[count + len(places) :]
    hidden_width = step_ref.shape[3]

    @pl.when(pl.program_id(0) == 0)
    def _():
        sums = gram_refs[0][...]
        for gram_ref in gram_refs[1:]:
            sums = sums + gram_ref[...]
        sums = jnp.sum(sums, axis=1, keepdims=True)
        gram = {(i, j): sums[i * count + j : i * count + j + 1] for i, j in pair_list(count)}
        for rep, coef in enumerate(merge_coefs(gram, count)):
            coef_ref[rep] = jnp.broadcast_to(coef, coef_ref.shape[1:])

    matrix = pl.program_id(0)
    lines = 16

    def step(index, _):
        rows = pl.ds(pl.multiple_of(index * lines, lines), lines)
        merged = None
        for grads_ref, offsets in zip(grads_refs, places):
            for at, offset in enumerate(offsets):
                part = grads_ref[at, matrix, rows] * coef_ref[pos_ref[0] ^ offset]
                merged = part if merged is None else merged + part
        first_new = (beta_first / first_fix) * first_ref[0, 0, rows] + (
            (1.0 - beta_first) / first_fix
        ) * merged
        second_new = (beta_second / second_fix) * second_ref[0, 0, rows] + (
            (1.0 - beta_second) / second_fix
        ) * (merged * merged)
        step_ref[0, 0, rows] = first_new / (jnp.sqrt(second_new) + adam_eps)
        return 0

    lax.fori_loop(0, step_ref.shape[2] // lines, step, 0, unroll=4)


def adasum_adam_many(rep, inputs, incoming, factors, first_moment, second_moment):
    count = len(inputs)
    half = inputs[0].shape[0] // 2
    grads = []
    for offset in range(count):
        (payload,) = factors[offset]
        gate_grad, up_grad = payload[:, : 2 * half]
        hidden = payload[:, 2 * half :].reshape(2 * half, -1)
        received = incoming[offset].reshape(2 * half, incoming.shape[3])
        grads.append(
            jnp.stack(
                [
                    contract_first(inputs[offset], gate_grad),
                    contract_first(inputs[offset], up_grad),
                    contract_first(received, hidden),
                ]
            )
        )
    grads = jnp.stack(grads)[rep[0] ^ jnp.arange(count)]
    flat = grads.reshape(count, -1)
    gram = lax.psum(jnp.matmul(flat, flat.T, precision=lax.Precision.HIGHEST), "replica")
    coefs = jnp.eye(count, dtype=jnp.float32)
    while coefs.shape[0] > 1:
        inner = jnp.matmul(
            jnp.matmul(coefs, gram, precision=lax.Precision.HIGHEST),
            coefs.T,
            precision=lax.Precision.HIGHEST,
        )
        norms = jnp.maximum(jnp.diagonal(inner), 0.0)
        norm_first, norm_second = norms[0::2], norms[1::2]
        bound = jnp.sqrt(norm_first) * jnp.sqrt(norm_second)
        cross = jnp.clip(jnp.diagonal(inner, offset=1)[0::2], -bound, bound)
        coef_first = 1.0 - cross / (2.0 * (norm_first + norm_eps))
        coef_second = 1.0 - cross / (2.0 * (norm_second + norm_eps))
        coefs = coef_first[:, None] * coefs[0::2] + coef_second[:, None] * coefs[1::2]
    merged = jnp.sum(coefs[0][:, None, None, None] * grads, axis=0)
    first_new = beta_first * first_moment[0] + (1.0 - beta_first) * merged
    second_new = beta_second * second_moment[0] + (1.0 - beta_second) * merged * merged
    return ((first_new / first_fix) / (jnp.sqrt(second_new / second_fix) + adam_eps))[None]


def adasum(rep, inputs, incoming, factors):
    count = len(inputs)
    seg_rows, hidden_width = inputs[0].shape[1], factors[0][0].shape[2]
    shape = jax.ShapeDtypeStruct
    groups = [[k for k in range(count) if k < 3], [k for k in range(count) if k == 3]]
    groups = [group for group in groups if group]
    grads, gram, first_gram, place = [], None, None, 0
    for group in groups:
        operands = [rep] if gram is None else [rep, gram, grads[0]]
        parts = [x for k in group for x in ((inputs[k],), factors[k])]
        operands += [incoming] + flatten(parts)
        more, gram = call(
            functools.partial(gram_kernel, count, group, [len(x) for x in parts], place),
            "gram_late" if place else "gram",
            operands,
            [SMEM] + [VMEM] * (len(operands) - 1),
            [
                shape((len(group), 3, seg_rows, hidden_width), jnp.float32),
                shape((max(8, count * count), 128), jnp.float32),
            ],
            cost=0 if place else 0,
        )
        first_gram = gram if first_gram is None else first_gram
        grads.append(more)
        place += len(group)
    return groups, grads, gram, first_gram


def adam(rep, groups, grads, gram, first_moment, second_moment, after):
    count = sum(len(group) for group in groups)
    seg_rows, hidden_width = first_moment.shape[2:]
    grams = exchange([gram] * count)
    moment_spec = pl.BlockSpec((1, 1, seg_rows, hidden_width), lambda m: (0, m, 0, 0))
    (adam_step,) = call(
        functools.partial(adam_kernel, count, groups),
        "adam",
        [rep, *grams, *grads, first_moment, second_moment],
        [SMEM] + [VMEM] * (len(grams) + len(grads)) + [moment_spec, moment_spec],
        [jax.ShapeDtypeStruct(first_moment.shape, jnp.float32)],
        out_specs=[moment_spec],
        grid=(3,),
        scratch=[pltpu.VMEM((count, 1, hidden_width), jnp.float32)],
        after=after,
    )
    return adam_step


def shards(
    weights, first_moment, second_moment, out_grads, routes, task_ids, task_weights, saved_inputs
):
    expert_count = lax.axis_size("expert")
    rep_count = lax.axis_size("replica")
    row_count = out_grads.shape[1]
    model_width = out_grads.shape[2]
    hidden_width = weights.shape[3]
    slot_count = saved_inputs.shape[2]
    capacity = slot_count // expert_count
    seg_rows = model_width // rep_count
    half = slot_count // 2
    offsets = range(rep_count)
    chips = expert_count // 2
    rep = jnp.stack([lax.axis_index("replica"), lax.axis_index("expert")]).astype(jnp.int32)
    shape = jax.ShapeDtypeStruct

    block = shape((row_count + LABEL_ROWS, seg_rows), jnp.bfloat16)
    row_blocks = call(
        functools.partial(rows_kernel, expert_count),
        "rows",
        [rep, task_ids, task_weights, routes[0].reshape(1, row_count), out_grads[0]],
        [SMEM, SMEM, SMEM, VMEM, VMEM],
        [block for _ in offsets],
    )
    routed = exchange(row_blocks)

    near_projections = gather_near(weights[0, :2])

    inputs_home = saved_inputs[0, 0]
    inputs = exchange(
        call(
            split_kernel,
            "split",
            [rep, inputs_home],
            [SMEM, VMEM],
            [shape((slot_count, seg_rows), jnp.bfloat16) for _ in offsets],
        )
    )

    part = shape((2, rep_count, capacity, seg_rows), jnp.bfloat16)
    placed = (
        call(
            functools.partial(place_kernel, rep_count),
            "place",
            [rep, *routed],
            [SMEM] + [VMEM] * len(routed),
            [part] * chips,
            scratch=[
                pltpu.VMEM((rep_count, expert_count, capacity, seg_rows), jnp.bfloat16)
            ],
        )
    )

    came = across_chips(placed)
    projections = gather_rest(near_projections, after=placed[:1])

    forward = None
    late = [3] if rep_count == 4 else []
    for name, group in (("forward", [k for k in offsets if k not in late]), ("rest", late)):
        if not group:
            continue
        operands = [rep, inputs_home] + ([] if forward is None else [forward])
        operands += flatten(projections[k] for k in group)
        lengths = [len(projections[k]) for k in group]
        (forward,) = call(
            functools.partial(forward_kernel, group, lengths, forward is not None),
            name,
            operands,
            [SMEM] + [VMEM] * (len(operands) - 1),
            [shape((2, slot_count, hidden_width), jnp.float32)],
            cost=0 if name == "rest" else 0,
        )

    came = finish_spread(came)

    back_shape = (slot_count, hidden_width)
    incoming, *back = call(
        functools.partial(back_kernel, chips, len(came)),
        "back",
        [rep, weights[0, 2], *came],
        [SMEM] + [VMEM] * (1 + len(came)),
        [shape((rep_count, expert_count, capacity, seg_rows), jnp.bfloat16)]
        + [shape(back_shape, jnp.bfloat16 if k else jnp.float32) for k in offsets],
        after=[forward],
    )
    back = exchange(back)
    (own_factors,) = call(
        factor_kernel,
        "factors",
        [forward, *back],
        [VMEM] * (1 + len(back)),
        [shape((2, slot_count + half, hidden_width), jnp.bfloat16)],
        after=inputs[1:],
    )
    near_factors = gather_near(own_factors)

    operands = [rep, own_factors] + flatten(projections)
    returning = across_chips(
        call(
            functools.partial(slot_kernel, [len(group) for group in projections]),
            "slots",
            operands,
            [SMEM] + [VMEM] * (len(operands) - 1),
            [shape((2, capacity, model_width), jnp.bfloat16)] * chips,
            scratch=[
                pltpu.VMEM((rep_count, expert_count, capacity, seg_rows), jnp.bfloat16)
            ],
        )
    )
    factors = gather_rest(near_factors, after=returning[:1])
    if rep_count <= 4:
        *merging, first_gram = adasum(rep, inputs, incoming, factors)
        returned = finish_spread(returning, [first_gram], pieces=2)
        unplace_after = merging[2:]
    else:
        returned, unplace_after = finish_spread(returning), ()
    (input_grads,) = call(
        unplace_kernel,
        "unplace",
        [rep, routed[0], *returned],
        [SMEM] + [VMEM] * (1 + len(returned)),
        [shape((1, row_count, model_width), jnp.bfloat16)],
        scratch=[pltpu.VMEM((expert_count, capacity, model_width), jnp.bfloat16)],
        after=unplace_after,
    )
    if rep_count <= 4:
        adam_step = adam(rep, *merging, first_moment, second_moment, [input_grads])
    else:
        adam_step = adasum_adam_many(
            rep, inputs, incoming, factors, first_moment, second_moment
        )
    return (input_grads, adam_step)


def solution(mesh):
    return jax.shard_map(
        shards,
        mesh=mesh,
        in_specs=(
            P("expert", None, "replica", None),
            P("expert", None, "replica", None),
            P("expert", None, "replica", None),
            P("replica", "expert", None),
            P("replica", "expert", None),
            P("replica", "expert"),
            P(),
            P("replica", "expert", None, None),
        ),
        out_specs=(P("replica", "expert", None), P("expert", None, "replica", None)),
        check_vma=False,
    )
```

```python
import functools

import jax
import jax.numpy as jnp
from jax import lax
from jax.experimental import pallas as pl
from jax.experimental.pallas import tpu as pltpu
from jax.sharding import PartitionSpec as P

beta_first = 0.9
beta_second = 0.95
adam_eps = 1e-08
norm_eps = 1e-06
first_fix = 1.0 - (0.9**50) ** 2
second_fix = 1.0 - (0.95**50) ** 2
MIB = 1024 * 1024
LABEL_ROWS = 16


def contract_first(left, right):
    return lax.dot_general(
        left, right, (((0,), (0,)), ((), ())), preferred_element_type=jnp.float32
    )


def contract_last(left, right):
    return lax.dot_general(
        left, right, (((1,), (1,)), ((), ())), preferred_element_type=jnp.float32
    )


def multiply(left, right):
    return jnp.dot(left, right, preferred_element_type=jnp.float32)


def from_peer(array, offset):
    count = lax.axis_size("replica")
    return lax.ppermute(array, "replica", [(i, i ^ offset) for i in range(count)])


def across_chips(parts):
    count = lax.axis_size("expert")
    return [parts[0]] + [
        lax.ppermute(part, "expert", [(i, i ^ 2 * k) for i in range(count)])
        for k, part in enumerate(parts)
        if k
    ]


def pick_kernel(chips, *refs):
    block_refs = [ref.at[k] for ref in refs[chips:] for k in range(ref.shape[0])]
    for part_ref, block_ref in zip(refs[:chips], block_refs):
        block_ref[...] = part_ref[1]


def finish_spread(came, after=(), pieces=1):
    count = lax.axis_size("expert")
    chips = len(came)
    block = jax.ShapeDtypeStruct((chips // pieces,) + came[0].shape[1:], came[0].dtype)
    others = call(
        functools.partial(pick_kernel, chips),
        "pick",
        came,
        [VMEM] * chips,
        [block] * pieces,
        after=after,
    )
    swapped = [lax.ppermute(x, "expert", [(i, i ^ 1) for i in range(count)]) for x in others]
    return [*came, *swapped]


def spread_block(chips, refs, offset):
    if offset % 2 == 0:
        return refs[offset // 2].at[0]
    blocks = [ref.at[k] for ref in refs[chips:] for k in range(ref.shape[0])]
    return blocks[offset // 2]


def exchange(parts):
    return [parts[0]] + [from_peer(part, k) for k, part in enumerate(parts) if k]


def copy_kernel(weights_ref, out_ref):
    out_ref[...] = weights_ref[0, pl.ds(0, out_ref.shape[0])]


def cut_kernel(from_two_ref, from_one_ref, first_ref, second_ref):
    first_ref[...] = from_two_ref[0]
    second_ref[...] = from_one_ref[1]


def gather_near(payload):
    count = lax.axis_size("replica")
    if count != 4:
        return exchange([payload] * count)
    from_two = from_peer(payload, 2)
    return [payload, from_peer(payload, 1), from_two]


def gather_rest(near, after):
    whole = [(part,) for part in near]
    if lax.axis_size("replica") != 4:
        return whole
    half = jax.ShapeDtypeStruct(near[0].shape[1:], near[0].dtype)
    first, second = call(
        cut_kernel, "cut", [near[2], near[1]], [VMEM, VMEM], [half, half], after=after
    )
    return whole + [(from_peer(first, 1), from_peer(second, 2))]


def halves(refs):
    return refs if len(refs) == 2 else (refs[0].at[0], refs[0].at[1])


def regroup(refs, lengths):
    groups, at = [], 0
    for length in lengths:
        groups.append(refs[at : at + length])
        at += length
    return groups


def flatten(groups):
    return [array for group in groups for array in group]


def pair_list(count):
    return [(i, j) for i in range(count) for j in range(i, count)]


SMEM = pl.BlockSpec(memory_space=pltpu.SMEM)
VMEM = pl.BlockSpec(memory_space=pltpu.VMEM)


def call(
    kernel, name, operands, specs, outs, out_specs=None, grid=(), scratch=(), after=(), cost=0, room=0
):
    size = sum(x.size * x.dtype.itemsize for x in list(operands) + list(outs))
    taken = len(operands)

    def body(*refs):
        kernel(*refs[:taken], *refs[taken + len(after) :])

    return pl.pallas_call(
        body,
        grid=grid,
        in_specs=list(specs) + [VMEM] * len(after),
        out_specs=out_specs if out_specs is not None else [VMEM for _ in outs],
        out_shape=outs,
        scratch_shapes=list(scratch),
        compiler_params=pltpu.CompilerParams(
            dimension_semantics=("arbitrary",) * len(grid),
            vmem_limit_bytes=max(room, min(56 * MIB, size + 8 * MIB)),
        ),
        cost_estimate=pl.CostEstimate(flops=0, bytes_accessed=cost, transcendentals=0),
        name=name,
    )(*operands, *after)


def segment(pos_ref, offset, width):
    return pl.ds(pl.multiple_of((pos_ref[0] ^ offset) * width, width), width)


def rows_kernel(expert_count, pos_ref, ids_ref, task_ref, row_ref, grads_ref, inputs_ref, *out_refs):
    row_count = grads_ref.shape[0]
    seg_rows = out_refs[0].shape[1]
    block_count = ids_ref.shape[1]
    block_rows = row_count // block_count
    square = (row_count, row_count)
    earlier = lax.broadcasted_iota(jnp.int32, square, 0) < lax.broadcasted_iota(
        jnp.int32, square, 1
    )
    experts = lax.broadcasted_iota(jnp.int32, (expert_count, row_count), 0)
    chosen = jnp.where(experts == row_ref[...], 1.0, 0.0)
    before = multiply(
        chosen.astype(jnp.bfloat16), jnp.where(earlier, 1.0, 0.0).astype(jnp.bfloat16)
    )
    rank = jnp.sum(chosen * before, axis=0, keepdims=True)
    line = lax.broadcasted_iota(jnp.int32, (LABEL_ROWS, row_count), 0)
    labels = jnp.where(line == 0, row_ref[...].astype(jnp.float32), 0.0)
    labels = jnp.where(line == 1, rank, labels).astype(jnp.bfloat16)
    for offset, out_ref in enumerate(out_refs):
        columns = segment(pos_ref, offset, seg_rows)
        for block in range(block_count):
            rows = pl.ds(block * block_rows, block_rows)
            weight = task_ref[ids_ref[0, block]]
            out_ref[rows, :] = (grads_ref[rows, columns].astype(jnp.float32) * weight).astype(
                jnp.bfloat16
            )
        if row_count < seg_rows:
            out_ref[pl.ds(row_count, LABEL_ROWS), :] = jnp.zeros(
                (LABEL_ROWS, seg_rows), jnp.bfloat16
            )
        out_ref[pl.ds(row_count, LABEL_ROWS), pl.ds(0, row_count)] = labels
        head = row_count + LABEL_ROWS
        out_ref[pl.ds(head, inputs_ref.shape[0]), :] = inputs_ref[:, columns]


def one_hot(block_ref, row_count, slot_count, capacity):
    labels = block_ref[pl.ds(row_count, LABEL_ROWS), pl.ds(0, row_count)].astype(jnp.float32)
    slot = (labels[0:1] * capacity + labels[1:2]).astype(jnp.int32)
    places = lax.broadcasted_iota(jnp.int32, (slot_count, row_count), 0)
    return jnp.where(places == slot, 1.0, 0.0).astype(jnp.bfloat16)


def place_kernel(count, row_count, pos_ref, *refs):
    block_refs, out_refs, placed_ref = refs[:count], refs[count:-1], refs[-1]
    _, expert_count, capacity, seg_rows = placed_ref.shape
    slot_count = expert_count * capacity
    for offset, block_ref in enumerate(block_refs):
        placing = one_hot(block_ref, row_count, slot_count, capacity)
        placed = multiply(placing, block_ref[pl.ds(0, row_count), :])
        placed = placed.reshape(expert_count, capacity, seg_rows)
        placed_ref[offset] = placed.astype(jnp.bfloat16)
        for expert in range(expert_count):
            out_refs[expert // 2][expert % 2, offset] = placed_ref[offset, pos_ref[1] ^ expert]


def unplace_kernel(pos_ref, block_ref, *refs):
    returned_refs, out_ref, slots_ref = refs[:-2], refs[-2], refs[-1]
    expert_count, capacity, _ = slots_ref.shape
    slot_count = expert_count * capacity
    row_count = out_ref.shape[1]
    placing = one_hot(block_ref, row_count, slot_count, capacity)
    for expert in range(expert_count):
        block_ref = spread_block(expert_count // 2, returned_refs, expert)
        slots_ref[pos_ref[1] ^ expert] = block_ref[...]
    out_ref[0] = contract_first(placing, flat_rows(slots_ref[...])).astype(jnp.bfloat16)


def flat_rows(blocks):
    rows = blocks.shape[0] * blocks.shape[1]
    if blocks.shape[1] % 16:
        wide = blocks.astype(jnp.float32).reshape(rows, blocks.shape[2])
        return wide.astype(jnp.bfloat16)
    return blocks.reshape(rows, blocks.shape[2])


def back_kernel(chips, arrays, pos_ref, weight_ref, *refs):
    came_refs, incoming_ref, out_refs = refs[:arrays], refs[arrays], refs[arrays + 1 :]
    for offset, out_ref in enumerate(out_refs):
        for expert in range(2 * chips):
            block_ref = spread_block(chips, came_refs, expert)
            incoming_ref[offset, pos_ref[1] ^ expert] = block_ref[offset]
        rows = flat_rows(incoming_ref[offset])
        out_ref[...] = multiply(rows, weight_ref[...]).astype(out_ref.dtype)


def forward_kernel(offsets, lengths, has_start, pos_ref, inputs_ref, *refs):
    out_ref = refs[-1]
    weight_refs = refs[:-1]
    gate = up = None
    if has_start:
        gate, up = weight_refs[0][0], weight_refs[0][1]
        weight_refs = weight_refs[1:]
    for offset, group in zip(offsets, regroup(weight_refs, lengths)):
        gate_ref, up_ref = halves(group)
        rows = inputs_ref[:, segment(pos_ref, offset, gate_ref.shape[0])]
        gate_part, up_part = multiply(rows, gate_ref[...]), multiply(rows, up_ref[...])
        gate = gate_part if gate is None else gate + gate_part
        up = up_part if up is None else up + up_part
    out_ref[0] = gate
    out_ref[1] = up


def factor_kernel(forward_ref, *refs):
    back_refs, out_ref = refs[:-1], refs[-1]
    slot_count = forward_ref.shape[1]
    half = slot_count // 2
    hidden_grad = back_refs[0][...]
    for back_ref in back_refs[1:]:
        hidden_grad = hidden_grad + back_ref[...].astype(jnp.float32)
    gate_pre, up_pre = forward_ref[0], forward_ref[1]
    sigmoid_gate = jax.nn.sigmoid(gate_pre)
    gate_act = gate_pre * sigmoid_gate
    hidden = (gate_act * up_pre).astype(jnp.bfloat16)
    gate_grad = hidden_grad * up_pre * sigmoid_gate * (1.0 + gate_pre * (1.0 - sigmoid_gate))
    out_ref[0, pl.ds(0, slot_count)] = gate_grad.astype(jnp.bfloat16)
    out_ref[1, pl.ds(0, slot_count)] = (hidden_grad * gate_act).astype(jnp.bfloat16)
    for part in range(2):
        out_ref[part, pl.ds(slot_count, half)] = hidden[part * half : (part + 1) * half]


def slot_kernel(lengths, pos_ref, factor_ref, *refs):
    chips = refs[-1].shape[1] // 2
    weight_refs, out_refs, slots_ref = refs[: -chips - 1], refs[-chips - 1 : -1], refs[-1]
    _, expert_count, capacity, seg_rows = slots_ref.shape
    rows = pl.ds(0, expert_count * capacity)
    gate_grad, up_grad = factor_ref[0, rows], factor_ref[1, rows]
    for offset, group in enumerate(regroup(weight_refs, lengths)):
        gate_ref, up_ref = halves(group)
        total = contract_last(gate_grad, gate_ref[...]) + contract_last(up_grad, up_ref[...])
        total = total.reshape(expert_count, capacity, seg_rows)
        slots_ref[offset] = total.astype(jnp.bfloat16)
        columns = segment(pos_ref, offset, seg_rows)
        for expert in range(expert_count):
            out_ref = out_refs[expert // 2]
            out_ref[expert % 2, :, columns] = slots_ref[offset, pos_ref[1] ^ expert]


def gram_kernel(count, offsets, lengths, place, pos_ref, *refs):
    if place:
        before_ref, earlier_ref, refs = refs[0], refs[1], refs[2:]
    incoming_ref, operand_refs, grads_ref, gram_ref = refs[0], refs[1:-2], refs[-2], refs[-1]
    middle = incoming_ref.shape[1] // 2
    seg_rows, hidden_width = grads_ref.shape[2:]
    slot_count = incoming_ref.shape[1] * incoming_ref.shape[2]
    groups = regroup(operand_refs, lengths)
    for at, offset in enumerate(offsets):
        (inputs_ref,), factor_refs = groups[2 * at : 2 * at + 2]
        rest = pl.ds(slot_count, slot_count // 2)
        columns = inputs_ref[pl.ds(inputs_ref.shape[0] - slot_count, slot_count), :]
        gate_ref, up_ref = (ref.at[pl.ds(0, slot_count)] for ref in halves(factor_refs))
        first_ref, second_ref = (ref.at[rest] for ref in halves(factor_refs))
        grads_ref[at, 0] = contract_first(columns, gate_ref[...])
        grads_ref[at, 1] = contract_first(columns, up_ref[...])
        grads_ref[at, 2] = contract_first(
            flat_rows(incoming_ref[offset, :middle]), first_ref[...]
        ) + contract_first(flat_rows(incoming_ref[offset, middle:]), second_ref[...])
    gram_ref[...] = before_ref[...] if place else jnp.zeros_like(gram_ref)
    known = list(range(place)) + list(offsets)
    pairs = [(i, j) for i, j in pair_list(len(known)) if j >= place]
    lines = 8

    def add(step, sums):
        rows = pl.ds(pl.multiple_of(lax.rem(step, seg_rows // lines) * lines, lines), lines)
        matrix = lax.div(step, seg_rows // lines)
        blocks = [earlier_ref[at, matrix, rows] for at in range(place)]
        blocks += [grads_ref[at, matrix, rows] for at in range(len(offsets))]
        return tuple(total + blocks[i] * blocks[j] for total, (i, j) in zip(sums, pairs))

    zero = jnp.zeros((lines, hidden_width), jnp.float32)
    sums = lax.fori_loop(0, 3 * (seg_rows // lines), add, tuple(zero for _ in pairs), unroll=4)
    for total, (i, j) in zip(sums, pairs):
        total = jnp.sum(total, axis=0, keepdims=True)
        part = total[:, :128]
        for lane in range(128, hidden_width, 128):
            part = part + total[:, lane : lane + 128]
        first, second = pos_ref[0] ^ known[i], pos_ref[0] ^ known[j]
        row = jnp.minimum(first, second) * count + jnp.maximum(first, second)
        gram_ref[pl.ds(row, 1), :] = part


def merge_coefs(gram, count):
    vectors = [{rep: None} for rep in range(count)]

    def term(coef, value):
        return value if coef is None else coef * value

    def inner(left, right):
        total = None
        for i, left_coef in left.items():
            for j, right_coef in right.items():
                value = term(left_coef, term(right_coef, gram[min(i, j), max(i, j)]))
                total = value if total is None else total + value
        return total

    while len(vectors) > 1:
        merged = []
        for first, second in zip(vectors[0::2], vectors[1::2]):
            norm_first = jnp.maximum(inner(first, first), 0.0)
            norm_second = jnp.maximum(inner(second, second), 0.0)
            bound = jnp.sqrt(norm_first) * jnp.sqrt(norm_second)
            cross = jnp.minimum(jnp.maximum(inner(first, second), -bound), bound)
            coef_first = 1.0 - cross / (2.0 * (norm_first + norm_eps))
            coef_second = 1.0 - cross / (2.0 * (norm_second + norm_eps))
            joined = {rep: term(coef, coef_first) for rep, coef in first.items()}
            joined.update({rep: term(coef, coef_second) for rep, coef in second.items()})
            merged.append(joined)
        vectors = merged
    return [vectors[0][rep] for rep in range(count)]


def adam_kernel(count, places, pos_ref, *refs):
    gram_refs, grads_refs = refs[:count], refs[count : count + len(places)]
    first_ref, second_ref, step_ref, coef_ref = refs[count + len(places) :]
    hidden_width = step_ref.shape[3]

    @pl.when((pl.program_id(0) == 0) & (pl.program_id(1) == 0))
    def _():
        sums = gram_refs[0][...]
        for gram_ref in gram_refs[1:]:
            sums = sums + gram_ref[...]
        sums = jnp.sum(sums, axis=1, keepdims=True)
        gram = {(i, j): sums[i * count + j : i * count + j + 1] for i, j in pair_list(count)}
        for rep, coef in enumerate(merge_coefs(gram, count)):
            coef_ref[rep] = jnp.broadcast_to(coef, coef_ref.shape[1:])

    matrix = pl.program_id(0)
    lines = 16

    def step(index, _):
        rows = pl.ds(pl.multiple_of(index * lines, lines), lines)
        start = pl.program_id(1) * step_ref.shape[2] + index * lines
        grad_rows = pl.ds(pl.multiple_of(start, lines), lines)
        merged = None
        for grads_ref, offsets in zip(grads_refs, places):
            for at, offset in enumerate(offsets):
                part = grads_ref[at, matrix, grad_rows] * coef_ref[pos_ref[0] ^ offset]
                merged = part if merged is None else merged + part
        first_new = (beta_first / first_fix) * first_ref[0, 0, rows] + (
            (1.0 - beta_first) / first_fix
        ) * merged
        second_new = (beta_second / second_fix) * second_ref[0, 0, rows] + (
            (1.0 - beta_second) / second_fix
        ) * (merged * merged)
        step_ref[0, 0, rows] = first_new / (jnp.sqrt(second_new) + adam_eps)
        return 0

    lax.fori_loop(0, step_ref.shape[2] // lines, step, 0, unroll=4)


def adasum_adam_many(rep, inputs, incoming, factors, first_moment, second_moment):
    count = len(inputs)
    half = inputs[0].shape[0] // 2
    grads = []
    for offset in range(count):
        (payload,) = factors[offset]
        gate_grad, up_grad = payload[:, : 2 * half]
        hidden = payload[:, 2 * half :].reshape(2 * half, -1)
        received = incoming[offset].reshape(2 * half, incoming.shape[3])
        grads.append(
            jnp.stack(
                [
                    contract_first(inputs[offset], gate_grad),
                    contract_first(inputs[offset], up_grad),
                    contract_first(received, hidden),
                ]
            )
        )
    grads = jnp.stack(grads)[rep[0] ^ jnp.arange(count)]
    flat = grads.reshape(count, -1)
    gram = lax.psum(jnp.matmul(flat, flat.T, precision=lax.Precision.HIGHEST), "replica")
    coefs = jnp.eye(count, dtype=jnp.float32)
    while coefs.shape[0] > 1:
        inner = jnp.matmul(
            jnp.matmul(coefs, gram, precision=lax.Precision.HIGHEST),
            coefs.T,
            precision=lax.Precision.HIGHEST,
        )
        norms = jnp.maximum(jnp.diagonal(inner), 0.0)
        norm_first, norm_second = norms[0::2], norms[1::2]
        bound = jnp.sqrt(norm_first) * jnp.sqrt(norm_second)
        cross = jnp.clip(jnp.diagonal(inner, offset=1)[0::2], -bound, bound)
        coef_first = 1.0 - cross / (2.0 * (norm_first + norm_eps))
        coef_second = 1.0 - cross / (2.0 * (norm_second + norm_eps))
        coefs = coef_first[:, None] * coefs[0::2] + coef_second[:, None] * coefs[1::2]
    merged = jnp.sum(coefs[0][:, None, None, None] * grads, axis=0)
    first_new = beta_first * first_moment[0] + (1.0 - beta_first) * merged
    second_new = beta_second * second_moment[0] + (1.0 - beta_second) * merged * merged
    return ((first_new / first_fix) / (jnp.sqrt(second_new / second_fix) + adam_eps))[None]


def adasum(rep, inputs, incoming, factors):
    count = len(inputs)
    seg_rows, hidden_width = inputs[0].shape[1], factors[0][0].shape[2]
    shape = jax.ShapeDtypeStruct
    groups = [[k for k in range(count) if k < 3], [k for k in range(count) if k == 3]]
    groups = [group for group in groups if group]
    grads, gram, first_gram, place = [], None, None, 0
    for group in groups:
        operands = [rep] if gram is None else [rep, gram, grads[0]]
        parts = [x for k in group for x in ((inputs[k],), factors[k])]
        operands += [incoming] + flatten(parts)
        more, gram = call(
            functools.partial(gram_kernel, count, group, [len(x) for x in parts], place),
            "gram_late" if place else "gram",
            operands,
            [SMEM] + [VMEM] * (len(operands) - 1),
            [
                shape((len(group), 3, seg_rows, hidden_width), jnp.float32),
                shape((max(8, count * count), 128), jnp.float32),
            ],
            cost=0 if place else 0,
        )
        first_gram = gram if first_gram is None else first_gram
        grads.append(more)
        place += len(group)
    return groups, grads, gram, first_gram


def adam(rep, groups, grads, gram, first_moment, second_moment, after):
    count = sum(len(group) for group in groups)
    seg_rows, hidden_width = first_moment.shape[2:]
    grams = exchange([gram] * count)
    tile = min(seg_rows, 256)
    moment_spec = pl.BlockSpec((1, 1, tile, hidden_width), lambda m, d: (0, m, d, 0))
    (adam_step,) = call(
        functools.partial(adam_kernel, count, groups),
        "adam",
        [rep, *grams, *grads, first_moment, second_moment],
        [SMEM] + [VMEM] * (len(grams) + len(grads)) + [moment_spec, moment_spec],
        [jax.ShapeDtypeStruct(first_moment.shape, jnp.float32)],
        out_specs=[moment_spec],
        grid=(3, seg_rows // tile),
        scratch=[pltpu.VMEM((count, 1, hidden_width), jnp.float32)],
        after=after,
    )
    return adam_step


def shards(
    weights, first_moment, second_moment, out_grads, routes, task_ids, task_weights, saved_inputs
):
    expert_count = lax.axis_size("expert")
    rep_count = lax.axis_size("replica")
    row_count = out_grads.shape[1]
    model_width = out_grads.shape[2]
    hidden_width = weights.shape[3]
    slot_count = saved_inputs.shape[2]
    capacity = slot_count // expert_count
    seg_rows = model_width // rep_count
    half = slot_count // 2
    offsets = range(rep_count)
    chips = expert_count // 2
    rep = jnp.stack([lax.axis_index("replica"), lax.axis_index("expert")]).astype(jnp.int32)
    shape = jax.ShapeDtypeStruct

    inputs_home = saved_inputs[0, 0]
    head = row_count + LABEL_ROWS
    block = shape((head + slot_count, seg_rows), jnp.bfloat16)
    small = [routes[0].reshape(1, row_count), out_grads[0], inputs_home]
    row_blocks = call(
        functools.partial(rows_kernel, expert_count),
        "rows",
        [rep, task_ids, task_weights, *small],
        [SMEM] * 3 + [pl.BlockSpec(x.shape, lambda i: (0, 0)) for x in small],
        [block for _ in offsets],
        grid=(1,),
        room=56 * MIB,
    )
    routed = exchange(row_blocks)

    pair = (2, seg_rows, hidden_width)
    (own_projections,) = call(
        copy_kernel,
        "projections",
        [weights],
        [VMEM],
        [shape(pair, jnp.bfloat16)],
        after=routed[1:],
    )
    near_projections = gather_near(own_projections)

    part = shape((2, rep_count, capacity, seg_rows), jnp.bfloat16)
    placed = (
        call(
            functools.partial(place_kernel, rep_count, row_count),
            "place",
            [rep, *routed],
            [SMEM] + [VMEM] * len(routed),
            [part] * chips,
            scratch=[
                pltpu.VMEM((rep_count, expert_count, capacity, seg_rows), jnp.bfloat16)
            ],
        )
    )

    came = across_chips(placed)
    projections = gather_rest(near_projections, after=placed[:1])

    forward = None
    late = [3] if rep_count == 4 else []
    for name, group in (("forward", [k for k in offsets if k not in late]), ("rest", late)):
        if not group:
            continue
        operands = [rep, inputs_home] + ([] if forward is None else [forward])
        operands += flatten(projections[k] for k in group)
        lengths = [len(projections[k]) for k in group]
        (forward,) = call(
            functools.partial(forward_kernel, group, lengths, forward is not None),
            name,
            operands,
            [SMEM] + [VMEM] * (len(operands) - 1),
            [shape((2, slot_count, hidden_width), jnp.float32)],
            cost=0 if name == "rest" else 0,
        )

    came = finish_spread(came)

    back_shape = (slot_count, hidden_width)
    incoming, *back = call(
        functools.partial(back_kernel, chips, len(came)),
        "back",
        [rep, weights[0, 2], *came],
        [SMEM] + [VMEM] * (1 + len(came)),
        [shape((rep_count, expert_count, capacity, seg_rows), jnp.bfloat16)]
        + [shape(back_shape, jnp.bfloat16 if k else jnp.float32) for k in offsets],
    )
    back = exchange(back)
    (own_factors,) = call(
        factor_kernel,
        "factors",
        [forward, *back],
        [VMEM] * (1 + len(back)),
        [shape((2, slot_count + half, hidden_width), jnp.bfloat16)],
    )
    near_factors = gather_near(own_factors)

    operands = [rep, own_factors] + flatten(projections)
    returning = across_chips(
        call(
            functools.partial(slot_kernel, [len(group) for group in projections]),
            "slots",
            operands,
            [SMEM] + [VMEM] * (len(operands) - 1),
            [shape((2, capacity, model_width), jnp.bfloat16)] * chips,
            scratch=[
                pltpu.VMEM((rep_count, expert_count, capacity, seg_rows), jnp.bfloat16)
            ],
        )
    )
    factors = gather_rest(near_factors, after=returning[:1])
    if rep_count <= 4:
        *merging, first_gram = adasum(rep, routed, incoming, factors)
        returned = finish_spread(returning, [first_gram], pieces=2)
        unplace_after = merging[2:]
    else:
        returned, unplace_after = finish_spread(returning), ()
    (input_grads,) = call(
        unplace_kernel,
        "unplace",
        [rep, routed[0], *returned],
        [SMEM] + [VMEM] * (1 + len(returned)),
        [shape((1, row_count, model_width), jnp.bfloat16)],
        scratch=[pltpu.VMEM((expert_count, capacity, model_width), jnp.bfloat16)],
        after=unplace_after,
    )
    if rep_count <= 4:
        adam_step = adam(rep, *merging, first_moment, second_moment, ())
    else:
        adam_step = adasum_adam_many(
            rep, [x[head:] for x in routed], incoming, factors, first_moment, second_moment
        )
    return (input_grads, adam_step)


def solution(mesh):
    return jax.shard_map(
        shards,
        mesh=mesh,
        in_specs=(
            P("expert", None, "replica", None),
            P("expert", None, "replica", None),
            P("expert", None, "replica", None),
            P("replica", "expert", None),
            P("replica", "expert", None),
            P("replica", "expert"),
            P(),
            P("replica", "expert", None, None),
        ),
        out_specs=(P("replica", "expert", None), P("expert", None, "replica", None)),
        check_vma=False,
    )
```

```python
import functools

import jax
import jax.numpy as jnp
from jax import lax
from jax.experimental import pallas as pl
from jax.experimental.pallas import tpu as pltpu
from jax.sharding import PartitionSpec as P

beta_first = 0.9
beta_second = 0.95
adam_eps = 1e-08
norm_eps = 1e-06
first_fix = 1.0 - (0.9**50) ** 2
second_fix = 1.0 - (0.95**50) ** 2
MIB = 1024 * 1024
LABEL_ROWS = 16


def contract_first(left, right):
    return lax.dot_general(
        left, right, (((0,), (0,)), ((), ())), preferred_element_type=jnp.float32
    )


def contract_last(left, right):
    return lax.dot_general(
        left, right, (((1,), (1,)), ((), ())), preferred_element_type=jnp.float32
    )


def multiply(left, right):
    return jnp.dot(left, right, preferred_element_type=jnp.float32)


def from_peer(array, offset):
    count = lax.axis_size("replica")
    return lax.ppermute(array, "replica", [(i, i ^ offset) for i in range(count)])


def across_chips(parts):
    count = lax.axis_size("expert")
    return [parts[0]] + [
        lax.ppermute(part, "expert", [(i, i ^ 2 * k) for i in range(count)])
        for k, part in enumerate(parts)
        if k
    ]


def pick_kernel(chips, *refs):
    block_refs = [ref.at[k] for ref in refs[chips:] for k in range(ref.shape[0])]
    for part_ref, block_ref in zip(refs[:chips], block_refs):
        block_ref[...] = part_ref[1]


def finish_spread(came, after=(), pieces=1):
    count = lax.axis_size("expert")
    chips = len(came)
    block = jax.ShapeDtypeStruct((chips // pieces,) + came[0].shape[1:], came[0].dtype)
    others = call(
        functools.partial(pick_kernel, chips),
        "pick",
        came,
        [VMEM] * chips,
        [block] * pieces,
        after=after,
    )
    swapped = [lax.ppermute(x, "expert", [(i, i ^ 1) for i in range(count)]) for x in others]
    return [*came, *swapped]


def spread_block(chips, refs, offset):
    if offset % 2 == 0:
        return refs[offset // 2].at[0]
    blocks = [ref.at[k] for ref in refs[chips:] for k in range(ref.shape[0])]
    return blocks[offset // 2]


def exchange(parts):
    return [parts[0]] + [from_peer(part, k) for k, part in enumerate(parts) if k]


def split_kernel(rep_ref, matrix_ref, *out_refs):
    for offset, out_ref in enumerate(out_refs):
        out_ref[...] = matrix_ref[:, segment(rep_ref, offset, out_ref.shape[1])]


def payload_kernel(rep_ref, pair_ref, inputs_ref, *out_refs):
    seg_rows = pair_ref.shape[1]
    slot_count = inputs_ref.shape[0]
    half = slot_count // 2
    for part, out_ref in enumerate(out_refs):
        out_ref[pl.ds(0, seg_rows), :] = pair_ref[0]
        out_ref[pl.ds(seg_rows, seg_rows), :] = pair_ref[1]
        columns = segment(rep_ref, part + 1, seg_rows)
        out_ref[pl.ds(2 * seg_rows, slot_count), :] = inputs_ref[:, columns]
        columns = segment(rep_ref, 3, seg_rows)
        out_ref[pl.ds(2 * seg_rows + slot_count, half), :] = inputs_ref[
            pl.ds(part * half, half), columns
        ]


def pass_kernel(from_two_ref, from_one_ref, *out_refs):
    for part, (near_ref, out_ref) in enumerate(zip((from_two_ref, from_one_ref), out_refs)):
        seg_rows = near_ref.shape[1]
        half = out_ref.shape[0] - seg_rows
        out_ref[pl.ds(0, seg_rows), :] = near_ref[pl.ds(part * seg_rows, seg_rows), :]
        out_ref[pl.ds(seg_rows, half), :] = near_ref[pl.ds(near_ref.shape[0] - half, half), :]


def projection_rows(refs):
    if len(refs) == 1 and len(refs[0].shape) == 3:
        return refs[0].at[0], refs[0].at[1]
    seg_rows = refs[0].shape[1]
    start = 0 if len(refs) == 2 else seg_rows
    return refs[0].at[pl.ds(0, seg_rows)], refs[-1].at[pl.ds(start, seg_rows)]


def input_rows(rep_ref, refs, slot_count, seg_rows):
    if len(refs) == 2:
        rows = pl.ds(seg_rows, slot_count // 2)
        return jnp.concatenate([refs[1][rows], refs[0][rows]], axis=0)
    (ref,) = refs
    if ref.shape[0] > slot_count:
        return ref[pl.ds(2 * seg_rows, slot_count), :]
    return ref[...] if ref.shape[1] == seg_rows else ref[:, segment(rep_ref, 0, seg_rows)]


def cut_kernel(from_two_ref, from_one_ref, first_ref, second_ref):
    first_ref[...] = from_two_ref[0]
    second_ref[...] = from_one_ref[1]


def gather_near(payload):
    count = lax.axis_size("replica")
    if count != 4:
        return exchange([payload] * count)
    from_two = from_peer(payload, 2)
    return [payload, from_peer(payload, 1), from_two]


def gather_rest(near, after):
    whole = [(part,) for part in near]
    if lax.axis_size("replica") != 4:
        return whole
    half = jax.ShapeDtypeStruct(near[0].shape[1:], near[0].dtype)
    first, second = call(
        cut_kernel, "cut", [near[2], near[1]], [VMEM, VMEM], [half, half], after=after
    )
    return whole + [(from_peer(first, 1), from_peer(second, 2))]


def halves(refs):
    return refs if len(refs) == 2 else (refs[0].at[0], refs[0].at[1])


def regroup(refs, lengths):
    groups, at = [], 0
    for length in lengths:
        groups.append(refs[at : at + length])
        at += length
    return groups


def flatten(groups):
    return [array for group in groups for array in group]


def pair_list(count):
    return [(i, j) for i in range(count) for j in range(i, count)]


SMEM = pl.BlockSpec(memory_space=pltpu.SMEM)
VMEM = pl.BlockSpec(memory_space=pltpu.VMEM)


def call(
    kernel, name, operands, specs, outs, out_specs=None, grid=(), scratch=(), after=(), cost=0, room=0
):
    size = sum(x.size * x.dtype.itemsize for x in list(operands) + list(outs))
    taken = len(operands)

    def body(*refs):
        kernel(*refs[:taken], *refs[taken + len(after) :])

    return pl.pallas_call(
        body,
        grid=grid,
        in_specs=list(specs) + [VMEM] * len(after),
        out_specs=out_specs if out_specs is not None else [VMEM for _ in outs],
        out_shape=outs,
        scratch_shapes=list(scratch),
        compiler_params=pltpu.CompilerParams(
            dimension_semantics=("arbitrary",) * len(grid),
            vmem_limit_bytes=max(room, min(56 * MIB, size + 8 * MIB)),
        ),
        cost_estimate=pl.CostEstimate(flops=0, bytes_accessed=cost, transcendentals=0),
        name=name,
    )(*operands, *after)


def segment(pos_ref, offset, width):
    return pl.ds(pl.multiple_of((pos_ref[0] ^ offset) * width, width), width)


def rows_kernel(expert_count, pos_ref, ids_ref, task_ref, row_ref, grads_ref, *out_refs):
    row_count = grads_ref.shape[0]
    seg_rows = out_refs[0].shape[1]
    block_count = ids_ref.shape[1]
    block_rows = row_count // block_count
    square = (row_count, row_count)
    earlier = lax.broadcasted_iota(jnp.int32, square, 0) < lax.broadcasted_iota(
        jnp.int32, square, 1
    )
    experts = lax.broadcasted_iota(jnp.int32, (expert_count, row_count), 0)
    chosen = jnp.where(experts == row_ref[...], 1.0, 0.0)
    before = multiply(
        chosen.astype(jnp.bfloat16), jnp.where(earlier, 1.0, 0.0).astype(jnp.bfloat16)
    )
    rank = jnp.sum(chosen * before, axis=0, keepdims=True)
    line = lax.broadcasted_iota(jnp.int32, (LABEL_ROWS, row_count), 0)
    labels = jnp.where(line == 0, row_ref[...].astype(jnp.float32), 0.0)
    labels = jnp.where(line == 1, rank, labels).astype(jnp.bfloat16)
    for offset, out_ref in enumerate(out_refs):
        columns = segment(pos_ref, offset, seg_rows)
        for block in range(block_count):
            rows = pl.ds(block * block_rows, block_rows)
            weight = task_ref[ids_ref[0, block]]
            out_ref[rows, :] = (grads_ref[rows, columns].astype(jnp.float32) * weight).astype(
                jnp.bfloat16
            )
        if row_count < seg_rows:
            out_ref[pl.ds(row_count, LABEL_ROWS), :] = jnp.zeros(
                (LABEL_ROWS, seg_rows), jnp.bfloat16
            )
        out_ref[pl.ds(row_count, LABEL_ROWS), pl.ds(0, row_count)] = labels


def one_hot(block_ref, row_count, slot_count, capacity):
    labels = block_ref[pl.ds(row_count, LABEL_ROWS), pl.ds(0, row_count)].astype(jnp.float32)
    slot = (labels[0:1] * capacity + labels[1:2]).astype(jnp.int32)
    places = lax.broadcasted_iota(jnp.int32, (slot_count, row_count), 0)
    return jnp.where(places == slot, 1.0, 0.0).astype(jnp.bfloat16)


def place_kernel(count, row_count, pos_ref, *refs):
    block_refs, out_refs, placed_ref = refs[:count], refs[count:-1], refs[-1]
    _, expert_count, capacity, seg_rows = placed_ref.shape
    slot_count = expert_count * capacity
    for offset, block_ref in enumerate(block_refs):
        placing = one_hot(block_ref, row_count, slot_count, capacity)
        placed = multiply(placing, block_ref[pl.ds(0, row_count), :])
        placed = placed.reshape(expert_count, capacity, seg_rows)
        placed_ref[offset] = placed.astype(jnp.bfloat16)
        for expert in range(expert_count):
            out_refs[expert // 2][expert % 2, offset] = placed_ref[offset, pos_ref[1] ^ expert]


def unplace_kernel(pos_ref, block_ref, *refs):
    returned_refs, out_ref, slots_ref = refs[:-2], refs[-2], refs[-1]
    expert_count, capacity, _ = slots_ref.shape
    slot_count = expert_count * capacity
    row_count = out_ref.shape[1]
    placing = one_hot(block_ref, row_count, slot_count, capacity)
    for expert in range(expert_count):
        block_ref = spread_block(expert_count // 2, returned_refs, expert)
        slots_ref[pos_ref[1] ^ expert] = block_ref[...]
    out_ref[0] = contract_first(placing, flat_rows(slots_ref[...])).astype(jnp.bfloat16)


def flat_rows(blocks):
    rows = blocks.shape[0] * blocks.shape[1]
    if blocks.shape[1] % 16:
        wide = blocks.astype(jnp.float32).reshape(rows, blocks.shape[2])
        return wide.astype(jnp.bfloat16)
    return blocks.reshape(rows, blocks.shape[2])


def back_kernel(chips, arrays, pos_ref, weight_ref, *refs):
    came_refs, incoming_ref, out_refs = refs[:arrays], refs[arrays], refs[arrays + 1 :]
    for offset, out_ref in enumerate(out_refs):
        for expert in range(2 * chips):
            block_ref = spread_block(chips, came_refs, expert)
            incoming_ref[offset, pos_ref[1] ^ expert] = block_ref[offset]
        rows = flat_rows(incoming_ref[offset])
        out_ref[...] = multiply(rows, weight_ref[...]).astype(out_ref.dtype)


def forward_kernel(offsets, lengths, has_start, pos_ref, inputs_ref, *refs):
    out_ref = refs[-1]
    weight_refs = refs[:-1]
    gate = up = None
    if has_start:
        gate, up = weight_refs[0][0], weight_refs[0][1]
        weight_refs = weight_refs[1:]
    for offset, group in zip(offsets, regroup(weight_refs, lengths)):
        gate_ref, up_ref = projection_rows(group)
        rows = inputs_ref[:, segment(pos_ref, offset, gate_ref.shape[0])]
        gate_part, up_part = multiply(rows, gate_ref[...]), multiply(rows, up_ref[...])
        gate = gate_part if gate is None else gate + gate_part
        up = up_part if up is None else up + up_part
    out_ref[0] = gate
    out_ref[1] = up


def factor_kernel(forward_ref, *refs):
    back_refs, out_ref = refs[:-1], refs[-1]
    slot_count = forward_ref.shape[1]
    half = slot_count // 2
    hidden_grad = back_refs[0][...]
    for back_ref in back_refs[1:]:
        hidden_grad = hidden_grad + back_ref[...].astype(jnp.float32)
    gate_pre, up_pre = forward_ref[0], forward_ref[1]
    sigmoid_gate = jax.nn.sigmoid(gate_pre)
    gate_act = gate_pre * sigmoid_gate
    hidden = (gate_act * up_pre).astype(jnp.bfloat16)
    gate_grad = hidden_grad * up_pre * sigmoid_gate * (1.0 + gate_pre * (1.0 - sigmoid_gate))
    out_ref[0, pl.ds(0, slot_count)] = gate_grad.astype(jnp.bfloat16)
    out_ref[1, pl.ds(0, slot_count)] = (hidden_grad * gate_act).astype(jnp.bfloat16)
    for part in range(2):
        out_ref[part, pl.ds(slot_count, half)] = hidden[part * half : (part + 1) * half]


def slot_kernel(lengths, pos_ref, factor_ref, *refs):
    chips = refs[-1].shape[1] // 2
    weight_refs, out_refs, slots_ref = refs[: -chips - 1], refs[-chips - 1 : -1], refs[-1]
    _, expert_count, capacity, seg_rows = slots_ref.shape
    rows = pl.ds(0, expert_count * capacity)
    gate_grad, up_grad = factor_ref[0, rows], factor_ref[1, rows]
    for offset, group in enumerate(regroup(weight_refs, lengths)):
        gate_ref, up_ref = projection_rows(group)
        total = contract_last(gate_grad, gate_ref[...]) + contract_last(up_grad, up_ref[...])
        total = total.reshape(expert_count, capacity, seg_rows)
        slots_ref[offset] = total.astype(jnp.bfloat16)
        columns = segment(pos_ref, offset, seg_rows)
        for expert in range(expert_count):
            out_ref = out_refs[expert // 2]
            out_ref[expert % 2, :, columns] = slots_ref[offset, pos_ref[1] ^ expert]


def gram_kernel(count, offsets, lengths, place, pos_ref, *refs):
    if place:
        before_ref, earlier_ref, refs = refs[0], refs[1], refs[2:]
    incoming_ref, operand_refs, grads_ref, gram_ref = refs[0], refs[1:-2], refs[-2], refs[-1]
    middle = incoming_ref.shape[1] // 2
    seg_rows, hidden_width = grads_ref.shape[2:]
    slot_count = incoming_ref.shape[1] * incoming_ref.shape[2]
    groups = regroup(operand_refs, lengths)
    for at, offset in enumerate(offsets):
        input_refs, factor_refs = groups[2 * at : 2 * at + 2]
        rest = pl.ds(slot_count, slot_count // 2)
        columns = input_rows(pos_ref, input_refs, slot_count, seg_rows)
        gate_ref, up_ref = (ref.at[pl.ds(0, slot_count)] for ref in halves(factor_refs))
        first_ref, second_ref = (ref.at[rest] for ref in halves(factor_refs))
        grads_ref[at, 0] = contract_first(columns, gate_ref[...])
        grads_ref[at, 1] = contract_first(columns, up_ref[...])
        grads_ref[at, 2] = contract_first(
            flat_rows(incoming_ref[offset, :middle]), first_ref[...]
        ) + contract_first(flat_rows(incoming_ref[offset, middle:]), second_ref[...])
    gram_ref[...] = before_ref[...] if place else jnp.zeros_like(gram_ref)
    known = list(range(place)) + list(offsets)
    pairs = [(i, j) for i, j in pair_list(len(known)) if j >= place]
    lines = 8

    def add(step, sums):
        rows = pl.ds(pl.multiple_of(lax.rem(step, seg_rows // lines) * lines, lines), lines)
        matrix = lax.div(step, seg_rows // lines)
        blocks = [earlier_ref[at, matrix, rows] for at in range(place)]
        blocks += [grads_ref[at, matrix, rows] for at in range(len(offsets))]
        return tuple(total + blocks[i] * blocks[j] for total, (i, j) in zip(sums, pairs))

    zero = jnp.zeros((lines, hidden_width), jnp.float32)
    sums = lax.fori_loop(0, 3 * (seg_rows // lines), add, tuple(zero for _ in pairs), unroll=4)
    for total, (i, j) in zip(sums, pairs):
        total = jnp.sum(total, axis=0, keepdims=True)
        part = total[:, :128]
        for lane in range(128, hidden_width, 128):
            part = part + total[:, lane : lane + 128]
        first, second = pos_ref[0] ^ known[i], pos_ref[0] ^ known[j]
        row = jnp.minimum(first, second) * count + jnp.maximum(first, second)
        gram_ref[pl.ds(row, 1), :] = part


def merge_coefs(gram, count):
    vectors = [{rep: None} for rep in range(count)]

    def term(coef, value):
        return value if coef is None else coef * value

    def inner(left, right):
        total = None
        for i, left_coef in left.items():
            for j, right_coef in right.items():
                value = term(left_coef, term(right_coef, gram[min(i, j), max(i, j)]))
                total = value if total is None else total + value
        return total

    while len(vectors) > 1:
        merged = []
        for first, second in zip(vectors[0::2], vectors[1::2]):
            norm_first = jnp.maximum(inner(first, first), 0.0)
            norm_second = jnp.maximum(inner(second, second), 0.0)
            bound = jnp.sqrt(norm_first) * jnp.sqrt(norm_second)
            cross = jnp.minimum(jnp.maximum(inner(first, second), -bound), bound)
            coef_first = 1.0 - cross / (2.0 * (norm_first + norm_eps))
            coef_second = 1.0 - cross / (2.0 * (norm_second + norm_eps))
            joined = {rep: term(coef, coef_first) for rep, coef in first.items()}
            joined.update({rep: term(coef, coef_second) for rep, coef in second.items()})
            merged.append(joined)
        vectors = merged
    return [vectors[0][rep] for rep in range(count)]


def adam_kernel(count, places, pos_ref, *refs):
    gram_refs, grads_refs = refs[:count], refs[count : count + len(places)]
    first_ref, second_ref, step_ref, coef_ref = refs[count + len(places) :]
    hidden_width = step_ref.shape[3]

    @pl.when((pl.program_id(0) == 0) & (pl.program_id(1) == 0))
    def _():
        sums = gram_refs[0][...]
        for gram_ref in gram_refs[1:]:
            sums = sums + gram_ref[...]
        sums = jnp.sum(sums, axis=1, keepdims=True)
        gram = {(i, j): sums[i * count + j : i * count + j + 1] for i, j in pair_list(count)}
        for rep, coef in enumerate(merge_coefs(gram, count)):
            coef_ref[rep] = jnp.broadcast_to(coef, coef_ref.shape[1:])

    matrix = pl.program_id(0)
    lines = 16

    def step(index, _):
        rows = pl.ds(pl.multiple_of(index * lines, lines), lines)
        start = pl.program_id(1) * step_ref.shape[2] + index * lines
        grad_rows = pl.ds(pl.multiple_of(start, lines), lines)
        merged = None
        for grads_ref, offsets in zip(grads_refs, places):
            for at, offset in enumerate(offsets):
                part = grads_ref[at, matrix, grad_rows] * coef_ref[pos_ref[0] ^ offset]
                merged = part if merged is None else merged + part
        first_new = (beta_first / first_fix) * first_ref[0, 0, rows] + (
            (1.0 - beta_first) / first_fix
        ) * merged
        second_new = (beta_second / second_fix) * second_ref[0, 0, rows] + (
            (1.0 - beta_second) / second_fix
        ) * (merged * merged)
        root = second_new * lax.rsqrt(second_new)
        step_ref[0, 0, rows] = first_new / (root + adam_eps)
        return 0

    lax.fori_loop(0, step_ref.shape[2] // lines, step, 0, unroll=4)


def adasum_adam_many(rep, inputs, incoming, factors, first_moment, second_moment):
    count = len(inputs)
    half = inputs[0].shape[0] // 2
    grads = []
    for offset in range(count):
        (payload,) = factors[offset]
        gate_grad, up_grad = payload[:, : 2 * half]
        hidden = payload[:, 2 * half :].reshape(2 * half, -1)
        received = incoming[offset].reshape(2 * half, incoming.shape[3])
        grads.append(
            jnp.stack(
                [
                    contract_first(inputs[offset], gate_grad),
                    contract_first(inputs[offset], up_grad),
                    contract_first(received, hidden),
                ]
            )
        )
    grads = jnp.stack(grads)[rep[0] ^ jnp.arange(count)]
    flat = grads.reshape(count, -1)
    gram = lax.psum(jnp.matmul(flat, flat.T, precision=lax.Precision.HIGHEST), "replica")
    coefs = jnp.eye(count, dtype=jnp.float32)
    while coefs.shape[0] > 1:
        inner = jnp.matmul(
            jnp.matmul(coefs, gram, precision=lax.Precision.HIGHEST),
            coefs.T,
            precision=lax.Precision.HIGHEST,
        )
        norms = jnp.maximum(jnp.diagonal(inner), 0.0)
        norm_first, norm_second = norms[0::2], norms[1::2]
        bound = jnp.sqrt(norm_first) * jnp.sqrt(norm_second)
        cross = jnp.clip(jnp.diagonal(inner, offset=1)[0::2], -bound, bound)
        coef_first = 1.0 - cross / (2.0 * (norm_first + norm_eps))
        coef_second = 1.0 - cross / (2.0 * (norm_second + norm_eps))
        coefs = coef_first[:, None] * coefs[0::2] + coef_second[:, None] * coefs[1::2]
    merged = jnp.sum(coefs[0][:, None, None, None] * grads, axis=0)
    first_new = beta_first * first_moment[0] + (1.0 - beta_first) * merged
    second_new = beta_second * second_moment[0] + (1.0 - beta_second) * merged * merged
    return ((first_new / first_fix) / (jnp.sqrt(second_new / second_fix) + adam_eps))[None]


def adasum(rep, inputs, incoming, factors):
    count = len(inputs)
    seg_rows, hidden_width = incoming.shape[3], factors[0][0].shape[2]
    shape = jax.ShapeDtypeStruct
    groups = [[k for k in range(count) if k < 3], [k for k in range(count) if k == 3]]
    groups = [group for group in groups if group]
    grads, gram, first_gram, place = [], None, None, 0
    for group in groups:
        operands = [rep] if gram is None else [rep, gram, grads[0]]
        parts = [x for k in group for x in (inputs[k], factors[k])]
        operands += [incoming] + flatten(parts)
        more, gram = call(
            functools.partial(gram_kernel, count, group, [len(x) for x in parts], place),
            "gram_late" if place else "gram",
            operands,
            [SMEM] + [VMEM] * (len(operands) - 1),
            [
                shape((len(group), 3, seg_rows, hidden_width), jnp.float32),
                shape((max(8, count * count), 128), jnp.float32),
            ],
            cost=0 if place else 0,
        )
        first_gram = gram if first_gram is None else first_gram
        grads.append(more)
        place += len(group)
    return groups, grads, gram, first_gram


def adam(rep, groups, grads, gram, first_moment, second_moment, after):
    count = sum(len(group) for group in groups)
    seg_rows, hidden_width = first_moment.shape[2:]
    grams = exchange([gram] * count)
    tile = min(seg_rows, 256)
    moment_spec = pl.BlockSpec((1, 1, tile, hidden_width), lambda m, d: (0, m, d, 0))
    (adam_step,) = call(
        functools.partial(adam_kernel, count, groups),
        "adam",
        [rep, *grams, *grads, first_moment, second_moment],
        [SMEM] + [VMEM] * (len(grams) + len(grads)) + [moment_spec, moment_spec],
        [jax.ShapeDtypeStruct(first_moment.shape, jnp.float32)],
        out_specs=[moment_spec],
        grid=(3, seg_rows // tile),
        scratch=[pltpu.VMEM((count, 1, hidden_width), jnp.float32)],
        after=after,
    )
    return adam_step


def shards(
    weights, first_moment, second_moment, out_grads, routes, task_ids, task_weights, saved_inputs
):
    expert_count = lax.axis_size("expert")
    rep_count = lax.axis_size("replica")
    row_count = out_grads.shape[1]
    model_width = out_grads.shape[2]
    hidden_width = weights.shape[3]
    slot_count = saved_inputs.shape[2]
    capacity = slot_count // expert_count
    seg_rows = model_width // rep_count
    half = slot_count // 2
    offsets = range(rep_count)
    chips = expert_count // 2
    rep = jnp.stack([lax.axis_index("replica"), lax.axis_index("expert")]).astype(jnp.int32)
    shape = jax.ShapeDtypeStruct

    block = shape((row_count + LABEL_ROWS, seg_rows), jnp.bfloat16)
    small = [routes[0].reshape(1, row_count), out_grads[0]]
    row_blocks = call(
        functools.partial(rows_kernel, expert_count),
        "rows",
        [rep, task_ids, task_weights, *small],
        [SMEM] * 3 + [pl.BlockSpec(x.shape, lambda i: (0, 0)) for x in small],
        [block for _ in offsets],
        grid=(1,),
        room=56 * MIB,
    )
    routed = exchange(row_blocks)

    inputs_home = saved_inputs[0, 0]
    pair = weights[0, :2]
    packed = rep_count == 4 and seg_rows == hidden_width
    if packed:
        payload = shape((2 * seg_rows + slot_count + half, seg_rows), jnp.bfloat16)
        to_one, to_two = call(
            payload_kernel,
            "payload",
            [rep, pair, inputs_home],
            [SMEM, VMEM, VMEM],
            [payload, payload],
            after=routed[1:],
        )
        from_two, from_one = from_peer(to_two, 2), from_peer(to_one, 1)
        projections = [(pair,), (from_one,), (from_two,)]
        inputs = [(inputs_home,), (from_one,), (from_two,)]
    else:
        projections = [(x,) for x in exchange([pair] * rep_count)]
        pieces = [shape((slot_count, seg_rows), jnp.bfloat16) for _ in offsets]
        pieces = call(split_kernel, "split", [rep, inputs_home], [SMEM, VMEM], pieces)
        inputs = [(x,) for x in exchange(pieces)]

    part = shape((2, rep_count, capacity, seg_rows), jnp.bfloat16)
    placed = (
        call(
            functools.partial(place_kernel, rep_count, row_count),
            "place",
            [rep, *routed],
            [SMEM] + [VMEM] * len(routed),
            [part] * chips,
            scratch=[
                pltpu.VMEM((rep_count, expert_count, capacity, seg_rows), jnp.bfloat16)
            ],
        )
    )

    came = across_chips(placed)

    came = finish_spread(came)

    back_shape = (slot_count, hidden_width)
    incoming, *back = call(
        functools.partial(back_kernel, chips, len(came)),
        "back",
        [rep, weights[0, 2], *came],
        [SMEM] + [VMEM] * (1 + len(came)),
        [shape((rep_count, expert_count, capacity, seg_rows), jnp.bfloat16)]
        + [shape(back_shape, jnp.bfloat16 if k else jnp.float32) for k in offsets],
    )
    own_back = back[:1]
    back = exchange(back)
    if packed:
        passed = shape((seg_rows + half, seg_rows), jnp.bfloat16)
        first, second = call(
            pass_kernel,
            "pass",
            [from_two, from_one],
            [VMEM, VMEM],
            [passed, passed],
            after=own_back,
        )
        last = (from_peer(first, 1), from_peer(second, 2))
        projections.append(last)
        inputs.append(last)

    forward = None
    late = [3] if packed else []
    for name, group in (("forward", [k for k in offsets if k not in late]), ("rest", late)):
        if not group:
            continue
        operands = [rep, inputs_home] + ([] if forward is None else [forward])
        operands += flatten(projections[k] for k in group)
        lengths = [len(projections[k]) for k in group]
        (forward,) = call(
            functools.partial(forward_kernel, group, lengths, forward is not None),
            name,
            operands,
            [SMEM] + [VMEM] * (len(operands) - 1),
            [shape((2, slot_count, hidden_width), jnp.float32)],
            cost=0 if name == "rest" else 0,
        )

    (own_factors,) = call(
        factor_kernel,
        "factors",
        [forward, *back],
        [VMEM] * (1 + len(back)),
        [shape((2, slot_count + half, hidden_width), jnp.bfloat16)],
    )
    near_factors = gather_near(own_factors)

    operands = [rep, own_factors] + flatten(projections)
    returning = across_chips(
        call(
            functools.partial(slot_kernel, [len(group) for group in projections]),
            "slots",
            operands,
            [SMEM] + [VMEM] * (len(operands) - 1),
            [shape((2, capacity, model_width), jnp.bfloat16)] * chips,
            scratch=[
                pltpu.VMEM((rep_count, expert_count, capacity, seg_rows), jnp.bfloat16)
            ],
        )
    )
    factors = gather_rest(near_factors, after=returning[:1])
    if rep_count <= 4:
        *merging, first_gram = adasum(rep, inputs, incoming, factors)
        returned = finish_spread(returning, [first_gram], pieces=2)
        unplace_after = merging[2:]
    else:
        returned, unplace_after = finish_spread(returning), ()
    (input_grads,) = call(
        unplace_kernel,
        "unplace",
        [rep, routed[0], *returned],
        [SMEM] + [VMEM] * (1 + len(returned)),
        [shape((1, row_count, model_width), jnp.bfloat16)],
        scratch=[pltpu.VMEM((expert_count, capacity, model_width), jnp.bfloat16)],
        after=unplace_after,
    )
    if rep_count <= 4:
        adam_step = adam(rep, *merging, first_moment, second_moment, ())
    else:
        adam_step = adasum_adam_many(
            rep, [x for (x,) in inputs], incoming, factors, first_moment, second_moment
        )
    return (input_grads, adam_step)


def solution(mesh):
    return jax.shard_map(
        shards,
        mesh=mesh,
        in_specs=(
            P("expert", None, "replica", None),
            P("expert", None, "replica", None),
            P("expert", None, "replica", None),
            P("replica", "expert", None),
            P("replica", "expert", None),
            P("replica", "expert"),
            P(),
            P("replica", "expert", None, None),
        ),
        out_specs=(P("replica", "expert", None), P("expert", None, "replica", None)),
        check_vma=False,
    )
```

```python
import functools

import jax
import jax.numpy as jnp
from jax import lax
from jax.experimental import pallas as pl
from jax.experimental.pallas import tpu as pltpu
from jax.sharding import PartitionSpec as P

beta_first = 0.9
beta_second = 0.95
adam_eps = 1e-08
norm_eps = 1e-06
first_fix = 1.0 - (0.9**50) ** 2
second_fix = 1.0 - (0.95**50) ** 2
MIB = 1024 * 1024
LABEL_ROWS = 16


def contract_first(left, right):
    return lax.dot_general(
        left, right, (((0,), (0,)), ((), ())), preferred_element_type=jnp.float32
    )


def contract_last(left, right):
    return lax.dot_general(
        left, right, (((1,), (1,)), ((), ())), preferred_element_type=jnp.float32
    )


def multiply(left, right):
    return jnp.dot(left, right, preferred_element_type=jnp.float32)


def from_peer(array, offset):
    count = lax.axis_size("replica")
    return lax.ppermute(array, "replica", [(i, i ^ offset) for i in range(count)])


def across_chips(parts):
    count = lax.axis_size("expert")
    return [parts[0]] + [
        lax.ppermute(part, "expert", [(i, i ^ 2 * k) for i in range(count)])
        for k, part in enumerate(parts)
        if k
    ]


def pick_kernel(chips, *refs):
    block_refs = [ref.at[k] for ref in refs[chips:] for k in range(ref.shape[0])]
    for part_ref, block_ref in zip(refs[:chips], block_refs):
        block_ref[...] = part_ref[1]


def finish_spread(came, after=(), pieces=1):
    count = lax.axis_size("expert")
    chips = len(came)
    block = jax.ShapeDtypeStruct((chips // pieces,) + came[0].shape[1:], came[0].dtype)
    others = call(
        functools.partial(pick_kernel, chips),
        "pick",
        came,
        [VMEM] * chips,
        [block] * pieces,
        after=after,
    )
    swapped = [lax.ppermute(x, "expert", [(i, i ^ 1) for i in range(count)]) for x in others]
    return [*came, *swapped]


def spread_block(chips, refs, offset):
    if offset % 2 == 0:
        return refs[offset // 2].at[0]
    blocks = [ref.at[k] for ref in refs[chips:] for k in range(ref.shape[0])]
    return blocks[offset // 2]


def exchange(parts):
    return [parts[0]] + [from_peer(part, k) for k, part in enumerate(parts) if k]


def split_kernel(rep_ref, matrix_ref, *out_refs):
    for offset, out_ref in enumerate(out_refs):
        out_ref[...] = matrix_ref[:, segment(rep_ref, offset, out_ref.shape[1])]


def payload_kernel(rep_ref, weights_ref, inputs_ref, *out_refs):
    seg_rows = weights_ref.shape[2]
    slot_count = inputs_ref.shape[0]
    half = slot_count // 2
    for part, out_ref in enumerate(out_refs):
        out_ref[pl.ds(0, seg_rows), :] = weights_ref[0, 0]
        out_ref[pl.ds(seg_rows, seg_rows), :] = weights_ref[0, 1]
        columns = segment(rep_ref, part + 1, seg_rows)
        out_ref[pl.ds(2 * seg_rows, slot_count), :] = inputs_ref[:, columns]
        columns = segment(rep_ref, 3, seg_rows)
        out_ref[pl.ds(2 * seg_rows + slot_count, half), :] = inputs_ref[
            pl.ds(part * half, half), columns
        ]


def pass_kernel(from_two_ref, from_one_ref, *out_refs):
    for part, (near_ref, out_ref) in enumerate(zip((from_two_ref, from_one_ref), out_refs)):
        seg_rows = near_ref.shape[1]
        half = out_ref.shape[0] - seg_rows
        out_ref[pl.ds(0, seg_rows), :] = near_ref[pl.ds(part * seg_rows, seg_rows), :]
        out_ref[pl.ds(seg_rows, half), :] = near_ref[pl.ds(near_ref.shape[0] - half, half), :]


def projection_rows(refs):
    if len(refs) == 1 and len(refs[0].shape) > 2:
        ref = refs[0] if len(refs[0].shape) == 3 else refs[0].at[0]
        return ref.at[0], ref.at[1]
    seg_rows = refs[0].shape[1]
    start = 0 if len(refs) == 2 else seg_rows
    return refs[0].at[pl.ds(0, seg_rows)], refs[-1].at[pl.ds(start, seg_rows)]


def input_rows(rep_ref, refs, slot_count, seg_rows):
    if len(refs) == 2:
        rows = pl.ds(seg_rows, slot_count // 2)
        return jnp.concatenate([refs[1][rows], refs[0][rows]], axis=0)
    (ref,) = refs
    if ref.shape[0] > slot_count:
        return ref[pl.ds(2 * seg_rows, slot_count), :]
    return ref[...] if ref.shape[1] == seg_rows else ref[:, segment(rep_ref, 0, seg_rows)]


def cut_kernel(from_two_ref, from_one_ref, first_ref, second_ref):
    first_ref[...] = from_two_ref[0]
    second_ref[...] = from_one_ref[1]


def gather_near(payload):
    count = lax.axis_size("replica")
    if count != 4:
        return exchange([payload] * count)
    from_two = from_peer(payload, 2)
    return [payload, from_peer(payload, 1), from_two]


def gather_rest(near, after):
    whole = [(part,) for part in near]
    if lax.axis_size("replica") != 4:
        return whole
    half = jax.ShapeDtypeStruct(near[0].shape[1:], near[0].dtype)
    first, second = call(
        cut_kernel, "cut", [near[2], near[1]], [VMEM, VMEM], [half, half], after=after
    )
    return whole + [(from_peer(first, 1), from_peer(second, 2))]


def halves(refs):
    return refs if len(refs) == 2 else (refs[0].at[0], refs[0].at[1])


def regroup(refs, lengths):
    groups, at = [], 0
    for length in lengths:
        groups.append(refs[at : at + length])
        at += length
    return groups


def flatten(groups):
    return [array for group in groups for array in group]


def pair_list(count):
    return [(i, j) for i in range(count) for j in range(i, count)]


SMEM = pl.BlockSpec(memory_space=pltpu.SMEM)
VMEM = pl.BlockSpec(memory_space=pltpu.VMEM)


def call(
    kernel, name, operands, specs, outs, out_specs=None, grid=(), scratch=(), after=(), cost=0, room=0
):
    size = sum(x.size * x.dtype.itemsize for x in list(operands) + list(outs))
    taken = len(operands)

    def body(*refs):
        kernel(*refs[:taken], *refs[taken + len(after) :])

    return pl.pallas_call(
        body,
        grid=grid,
        in_specs=list(specs) + [VMEM] * len(after),
        out_specs=out_specs if out_specs is not None else [VMEM for _ in outs],
        out_shape=outs,
        scratch_shapes=list(scratch),
        compiler_params=pltpu.CompilerParams(
            dimension_semantics=("arbitrary",) * len(grid),
            vmem_limit_bytes=max(room, min(56 * MIB, size + 8 * MIB)),
        ),
        cost_estimate=pl.CostEstimate(flops=0, bytes_accessed=cost, transcendentals=0),
        name=name,
    )(*operands, *after)


def segment(rep_ref, offset, width):
    return pl.ds(pl.multiple_of((rep_ref[0] ^ offset) * width, width), width)


def rows_kernel(expert_count, rep_ref, ids_ref, task_ref, row_ref, grads_ref, *out_refs):
    row_count = grads_ref.shape[0]
    seg_rows = out_refs[0].shape[1]
    block_count = ids_ref.shape[1]
    block_rows = row_count // block_count
    square = (row_count, row_count)
    earlier = lax.broadcasted_iota(jnp.int32, square, 0) < lax.broadcasted_iota(
        jnp.int32, square, 1
    )
    experts = lax.broadcasted_iota(jnp.int32, (expert_count, row_count), 0)
    chosen = jnp.where(experts == row_ref[...], 1.0, 0.0)
    before = multiply(
        chosen.astype(jnp.bfloat16), jnp.where(earlier, 1.0, 0.0).astype(jnp.bfloat16)
    )
    rank = jnp.sum(chosen * before, axis=0, keepdims=True)
    line = lax.broadcasted_iota(jnp.int32, (LABEL_ROWS, row_count), 0)
    labels = jnp.where(line == 0, row_ref[...].astype(jnp.float32), 0.0)
    labels = jnp.where(line == 1, rank, labels).astype(jnp.bfloat16)
    for offset, out_ref in enumerate(out_refs):
        columns = segment(rep_ref, offset, seg_rows)
        for block in range(block_count):
            rows = pl.ds(block * block_rows, block_rows)
            weight = task_ref[ids_ref[0, block]]
            out_ref[rows, :] = (grads_ref[rows, columns].astype(jnp.float32) * weight).astype(
                jnp.bfloat16
            )
        if row_count < seg_rows:
            out_ref[pl.ds(row_count, LABEL_ROWS), :] = jnp.zeros(
                (LABEL_ROWS, seg_rows), jnp.bfloat16
            )
        out_ref[pl.ds(row_count, LABEL_ROWS), pl.ds(0, row_count)] = labels


def one_hot(block_ref, row_count, slot_count, capacity):
    labels = block_ref[pl.ds(row_count, LABEL_ROWS), pl.ds(0, row_count)].astype(jnp.float32)
    slot = (labels[0:1] * capacity + labels[1:2]).astype(jnp.int32)
    places = lax.broadcasted_iota(jnp.int32, (slot_count, row_count), 0)
    return jnp.where(places == slot, 1.0, 0.0).astype(jnp.bfloat16)


def place_kernel(count, row_count, spot_ref, *refs):
    block_refs, out_refs, placed_ref = refs[:count], refs[count:-1], refs[-1]
    _, expert_count, capacity, seg_rows = placed_ref.shape
    slot_count = expert_count * capacity
    for offset, block_ref in enumerate(block_refs):
        placing = one_hot(block_ref, row_count, slot_count, capacity)
        placed = multiply(placing, block_ref[pl.ds(0, row_count), :])
        placed = placed.reshape(expert_count, capacity, seg_rows)
        placed_ref[offset] = placed.astype(jnp.bfloat16)
        for expert in range(expert_count):
            out_refs[expert // 2][expert % 2, offset] = placed_ref[offset, spot_ref[0] ^ expert]


def unplace_kernel(spot_ref, block_ref, *refs):
    returned_refs, out_ref, slots_ref = refs[:-2], refs[-2], refs[-1]
    expert_count, capacity, _ = slots_ref.shape
    slot_count = expert_count * capacity
    row_count = out_ref.shape[1]
    placing = one_hot(block_ref, row_count, slot_count, capacity)
    for expert in range(expert_count):
        block_ref = spread_block(expert_count // 2, returned_refs, expert)
        slots_ref[spot_ref[0] ^ expert] = block_ref[...]
    out_ref[0] = contract_first(placing, flat_rows(slots_ref[...])).astype(jnp.bfloat16)


def flat_rows(blocks):
    rows = blocks.shape[0] * blocks.shape[1]
    if blocks.shape[1] % 16:
        wide = blocks.astype(jnp.float32).reshape(rows, blocks.shape[2])
        return wide.astype(jnp.bfloat16)
    return blocks.reshape(rows, blocks.shape[2])


def back_kernel(chips, arrays, spot_ref, weight_ref, *refs):
    came_refs, incoming_ref, out_refs = refs[:arrays], refs[arrays], refs[arrays + 1 :]
    for offset, out_ref in enumerate(out_refs):
        for expert in range(2 * chips):
            block_ref = spread_block(chips, came_refs, expert)
            incoming_ref[offset, spot_ref[0] ^ expert] = block_ref[offset]
        rows = flat_rows(incoming_ref[offset])
        out_ref[...] = multiply(rows, weight_ref[0, 2]).astype(out_ref.dtype)


def forward_kernel(offsets, lengths, has_start, rep_ref, inputs_ref, *refs):
    out_ref = refs[-1]
    weight_refs = refs[:-1]
    gate = up = None
    if has_start:
        gate, up = weight_refs[0][0], weight_refs[0][1]
        weight_refs = weight_refs[1:]
    for offset, group in zip(offsets, regroup(weight_refs, lengths)):
        gate_ref, up_ref = projection_rows(group)
        rows = inputs_ref[:, segment(rep_ref, offset, gate_ref.shape[0])]
        gate_part, up_part = multiply(rows, gate_ref[...]), multiply(rows, up_ref[...])
        gate = gate_part if gate is None else gate + gate_part
        up = up_part if up is None else up + up_part
    out_ref[0] = gate
    out_ref[1] = up


def factor_kernel(forward_ref, *refs):
    back_refs, out_ref = refs[:-1], refs[-1]
    slot_count = forward_ref.shape[1]
    half = slot_count // 2
    hidden_grad = back_refs[0][...]
    for back_ref in back_refs[1:]:
        hidden_grad = hidden_grad + back_ref[...].astype(jnp.float32)
    gate_pre, up_pre = forward_ref[0], forward_ref[1]
    sigmoid_gate = jax.nn.sigmoid(gate_pre)
    gate_act = gate_pre * sigmoid_gate
    hidden = (gate_act * up_pre).astype(jnp.bfloat16)
    gate_grad = hidden_grad * up_pre * sigmoid_gate * (1.0 + gate_pre * (1.0 - sigmoid_gate))
    out_ref[0, pl.ds(0, slot_count)] = gate_grad.astype(jnp.bfloat16)
    out_ref[1, pl.ds(0, slot_count)] = (hidden_grad * gate_act).astype(jnp.bfloat16)
    for part in range(2):
        out_ref[part, pl.ds(slot_count, half)] = hidden[part * half : (part + 1) * half]


def slot_kernel(lengths, rep_ref, spot_ref, factor_ref, *refs):
    chips = refs[-1].shape[1] // 2
    weight_refs, out_refs, slots_ref = refs[: -chips - 1], refs[-chips - 1 : -1], refs[-1]
    _, expert_count, capacity, seg_rows = slots_ref.shape
    rows = pl.ds(0, expert_count * capacity)
    gate_grad, up_grad = factor_ref[0, rows], factor_ref[1, rows]
    for offset, group in enumerate(regroup(weight_refs, lengths)):
        gate_ref, up_ref = projection_rows(group)
        total = contract_last(gate_grad, gate_ref[...]) + contract_last(up_grad, up_ref[...])
        total = total.reshape(expert_count, capacity, seg_rows)
        slots_ref[offset] = total.astype(jnp.bfloat16)
        columns = segment(rep_ref, offset, seg_rows)
        for expert in range(expert_count):
            out_ref = out_refs[expert // 2]
            out_ref[expert % 2, :, columns] = slots_ref[offset, spot_ref[0] ^ expert]


def gram_kernel(count, offsets, lengths, place, rep_ref, *refs):
    if place:
        before_ref, earlier_ref, refs = refs[0], refs[1], refs[2:]
    incoming_ref, operand_refs, grads_ref, gram_ref = refs[0], refs[1:-2], refs[-2], refs[-1]
    middle = incoming_ref.shape[1] // 2
    seg_rows, hidden_width = grads_ref.shape[2:]
    slot_count = incoming_ref.shape[1] * incoming_ref.shape[2]
    groups = regroup(operand_refs, lengths)
    known = list(range(place)) + list(offsets)
    pairs = [(i, j) for i, j in pair_list(len(known)) if j >= place]
    lines = 8
    tile = min(seg_rows, 256)
    sums = [jnp.zeros((lines, hidden_width), jnp.float32) for _ in pairs]
    operands = []
    for at, offset in enumerate(offsets):
        input_refs, factor_refs = groups[2 * at : 2 * at + 2]
        rest = pl.ds(slot_count, slot_count // 2)
        columns = input_rows(rep_ref, input_refs, slot_count, seg_rows)
        gate_ref, up_ref = (ref.at[pl.ds(0, slot_count)] for ref in halves(factor_refs))
        first_ref, second_ref = (ref.at[rest] for ref in halves(factor_refs))
        upper = flat_rows(incoming_ref[offset, :middle])
        lower = flat_rows(incoming_ref[offset, middle:])
        operands.append(
            [
                [(columns, gate_ref)],
                [(columns, up_ref)],
                [(upper, first_ref), (lower, second_ref)],
            ]
        )
    for matrix in range(3):
        for start in range(0, seg_rows, tile):
            rows = pl.ds(start, tile)
            blocks = [earlier_ref[at, matrix, rows] for at in range(place)]
            for at in range(len(offsets)):
                block = None
                for left, right_ref in operands[at][matrix]:
                    part = contract_first(left[:, start : start + tile], right_ref[...])
                    block = part if block is None else block + part
                grads_ref[at, matrix, rows] = block
                blocks.append(block)
            for place_of, (i, j) in enumerate(pairs):
                products = (blocks[i] * blocks[j]).reshape(tile // lines, lines, hidden_width)
                sums[place_of] = sums[place_of] + jnp.sum(products, axis=0)
    gram_ref[...] = before_ref[...] if place else jnp.zeros_like(gram_ref)
    for total, (i, j) in zip(sums, pairs):
        total = jnp.sum(total, axis=0, keepdims=True)
        part = total[:, :128]
        for lane in range(128, hidden_width, 128):
            part = part + total[:, lane : lane + 128]
        first, second = rep_ref[0] ^ known[i], rep_ref[0] ^ known[j]
        row = jnp.minimum(first, second) * count + jnp.maximum(first, second)
        gram_ref[pl.ds(row, 1), :] = part


def merge_coefs(gram, count):
    vectors = [{rep: None} for rep in range(count)]

    def term(coef, value):
        return value if coef is None else coef * value

    def inner(left, right):
        total = None
        for i, left_coef in left.items():
            for j, right_coef in right.items():
                value = term(left_coef, term(right_coef, gram[min(i, j), max(i, j)]))
                total = value if total is None else total + value
        return total

    while len(vectors) > 1:
        merged = []
        for first, second in zip(vectors[0::2], vectors[1::2]):
            norm_first = jnp.maximum(inner(first, first), 0.0)
            norm_second = jnp.maximum(inner(second, second), 0.0)
            bound = jnp.sqrt(norm_first) * jnp.sqrt(norm_second)
            cross = jnp.minimum(jnp.maximum(inner(first, second), -bound), bound)
            coef_first = 1.0 - cross / (2.0 * (norm_first + norm_eps))
            coef_second = 1.0 - cross / (2.0 * (norm_second + norm_eps))
            joined = {rep: term(coef, coef_first) for rep, coef in first.items()}
            joined.update({rep: term(coef, coef_second) for rep, coef in second.items()})
            merged.append(joined)
        vectors = merged
    return [vectors[0][rep] for rep in range(count)]


def adam_kernel(count, places, rep_ref, *refs):
    gram_refs, grads_refs = refs[:count], refs[count : count + len(places)]
    first_ref, second_ref, step_ref, coef_ref = refs[count + len(places) :]
    block_rows, hidden_width = step_ref.shape[2:]
    lines = coef_ref.shape[1]

    @pl.when((pl.program_id(0) == 0) & (pl.program_id(1) == 0))
    def _():
        sums = gram_refs[0][...]
        for gram_ref in gram_refs[1:]:
            sums = sums + gram_ref[...]
        sums = jnp.sum(sums, axis=1, keepdims=True)
        gram = {(i, j): sums[i * count + j : i * count + j + 1] for i, j in pair_list(count)}
        for rep, coef in enumerate(merge_coefs(gram, count)):
            coef_ref[rep] = jnp.broadcast_to(coef, coef_ref.shape[1:])

    matrix = pl.program_id(0)
    block = pl.program_id(1) * block_rows
    coefs = [[coef_ref[rep_ref[0] ^ offset] for offset in offsets] for offsets in places]

    def step(index, _):
        rows = pl.ds(pl.multiple_of(index * lines, lines), lines)
        all_rows = pl.ds(pl.multiple_of(block + index * lines, lines), lines)
        for lane in range(0, hidden_width, 128):
            columns = pl.ds(lane, 128)
            merged = None
            for grads_ref, group in zip(grads_refs, coefs):
                for at, coef in enumerate(group):
                    part = grads_ref[at, matrix, all_rows, columns] * coef
                    merged = part if merged is None else merged + part
            first_new = (beta_first / first_fix) * first_ref[0, matrix, all_rows, columns] + (
                (1.0 - beta_first) / first_fix
            ) * merged
            second_new = (beta_second / second_fix) * second_ref[0, matrix, all_rows, columns] + (
                (1.0 - beta_second) / second_fix
            ) * (merged * merged)
            root = second_new * lax.rsqrt(second_new)
            step_ref[0, 0, rows, columns] = first_new / (root + adam_eps)
        return 0

    lax.fori_loop(0, block_rows // lines, step, 0, unroll=2)


def adasum_adam_many(rep, inputs, incoming, factors, first_moment, second_moment):
    count = len(inputs)
    half = inputs[0].shape[0] // 2
    grads = []
    for offset in range(count):
        (payload,) = factors[offset]
        gate_grad, up_grad = payload[:, : 2 * half]
        hidden = payload[:, 2 * half :].reshape(2 * half, -1)
        received = incoming[offset].reshape(2 * half, incoming.shape[3])
        grads.append(
            jnp.stack(
                [
                    contract_first(inputs[offset], gate_grad),
                    contract_first(inputs[offset], up_grad),
                    contract_first(received, hidden),
                ]
            )
        )
    grads = jnp.stack(grads)[rep[0] ^ jnp.arange(count)]
    flat = grads.reshape(count, -1)
    gram = lax.psum(jnp.matmul(flat, flat.T, precision=lax.Precision.HIGHEST), "replica")
    coefs = jnp.eye(count, dtype=jnp.float32)
    while coefs.shape[0] > 1:
        inner = jnp.matmul(
            jnp.matmul(coefs, gram, precision=lax.Precision.HIGHEST),
            coefs.T,
            precision=lax.Precision.HIGHEST,
        )
        norms = jnp.maximum(jnp.diagonal(inner), 0.0)
        norm_first, norm_second = norms[0::2], norms[1::2]
        bound = jnp.sqrt(norm_first) * jnp.sqrt(norm_second)
        cross = jnp.clip(jnp.diagonal(inner, offset=1)[0::2], -bound, bound)
        coef_first = 1.0 - cross / (2.0 * (norm_first + norm_eps))
        coef_second = 1.0 - cross / (2.0 * (norm_second + norm_eps))
        coefs = coef_first[:, None] * coefs[0::2] + coef_second[:, None] * coefs[1::2]
    merged = jnp.sum(coefs[0][:, None, None, None] * grads, axis=0)
    first_new = beta_first * first_moment[0] + (1.0 - beta_first) * merged
    second_new = beta_second * second_moment[0] + (1.0 - beta_second) * merged * merged
    return ((first_new / first_fix) / (jnp.sqrt(second_new / second_fix) + adam_eps))[None]


def adasum(rep, inputs, incoming, factors):
    count = len(inputs)
    seg_rows, hidden_width = incoming.shape[3], factors[0][0].shape[2]
    shape = jax.ShapeDtypeStruct
    groups = [[k for k in range(count) if k < 3], [k for k in range(count) if k == 3]]
    groups = [group for group in groups if group]
    grads, gram, first_gram, place = [], None, None, 0
    for group in groups:
        operands = [rep] if gram is None else [rep, gram, grads[0]]
        parts = [x for k in group for x in (inputs[k], factors[k])]
        operands += [incoming] + flatten(parts)
        more, gram = call(
            functools.partial(gram_kernel, count, group, [len(x) for x in parts], place),
            "gram_late" if place else "gram",
            operands,
            [SMEM] + [VMEM] * (len(operands) - 1),
            [
                shape((len(group), 3, seg_rows, hidden_width), jnp.float32),
                shape((max(8, count * count), 128), jnp.float32),
            ],
            cost=0 if place else 0,
        )
        first_gram = gram if first_gram is None else first_gram
        grads.append(more)
        place += len(group)
    return groups, grads, gram, first_gram


def adam(rep, groups, grads, gram, first_moment, second_moment, after):
    count = sum(len(group) for group in groups)
    seg_rows, hidden_width = first_moment.shape[2:]
    grams = exchange([gram] * count)
    tile = min(seg_rows, 256)
    moment_spec = pl.BlockSpec((1, 1, tile, hidden_width), lambda m, d: (0, m, d, 0))
    (adam_step,) = call(
        functools.partial(adam_kernel, count, groups),
        "adam",
        [rep, *grams, *grads, first_moment, second_moment],
        [SMEM] + [VMEM] * (len(grams) + len(grads) + 2),
        [jax.ShapeDtypeStruct(first_moment.shape, jnp.float32)],
        out_specs=[moment_spec],
        grid=(3, seg_rows // tile),
        scratch=[pltpu.VMEM((count, 16, 128), jnp.float32)],
        after=after,
    )
    return adam_step


def shards(
    weights, first_moment, second_moment, out_grads, routes, task_ids, task_weights, saved_inputs
):
    expert_count = lax.axis_size("expert")
    rep_count = lax.axis_size("replica")
    row_count = out_grads.shape[1]
    model_width = out_grads.shape[2]
    hidden_width = weights.shape[3]
    slot_count = saved_inputs.shape[2]
    capacity = slot_count // expert_count
    seg_rows = model_width // rep_count
    half = slot_count // 2
    offsets = range(rep_count)
    chips = expert_count // 2
    rep = lax.axis_index("replica").astype(jnp.int32).reshape(1)
    spot = lax.axis_index("expert").astype(jnp.int32).reshape(1)
    shape = jax.ShapeDtypeStruct

    block = shape((row_count + LABEL_ROWS, seg_rows), jnp.bfloat16)
    small = [routes[0].reshape(1, row_count), out_grads[0]]
    row_blocks = call(
        functools.partial(rows_kernel, expert_count),
        "rows",
        [rep, task_ids, task_weights, *small],
        [SMEM] * 3 + [pl.BlockSpec(x.shape, lambda i: (0, 0)) for x in small],
        [block for _ in offsets],
        grid=(1,),
        room=56 * MIB,
    )
    routed = exchange(row_blocks)

    inputs_home = saved_inputs[0, 0]
    packed = rep_count == 4 and seg_rows == hidden_width
    if packed:
        payload = shape((2 * seg_rows + slot_count + half, seg_rows), jnp.bfloat16)
        to_one, to_two = call(
            payload_kernel,
            "payload",
            [rep, weights, inputs_home],
            [SMEM, VMEM, VMEM],
            [payload, payload],
            after=routed[1:],
        )
        from_two, from_one = from_peer(to_two, 2), from_peer(to_one, 1)
        projections = [(weights,), (from_one,), (from_two,)]
        inputs = [(inputs_home,), (from_one,), (from_two,)]
    else:
        projections = [(x,) for x in exchange([weights[0, :2]] * rep_count)]
        pieces = [shape((slot_count, seg_rows), jnp.bfloat16) for _ in offsets]
        pieces = call(split_kernel, "split", [rep, inputs_home], [SMEM, VMEM], pieces)
        inputs = [(x,) for x in exchange(pieces)]

    part = shape((2, rep_count, capacity, seg_rows), jnp.bfloat16)
    placed = (
        call(
            functools.partial(place_kernel, rep_count, row_count),
            "place",
            [spot, *routed],
            [SMEM] + [VMEM] * len(routed),
            [part] * chips,
            scratch=[
                pltpu.VMEM((rep_count, expert_count, capacity, seg_rows), jnp.bfloat16)
            ],
        )
    )

    came = across_chips(placed)

    came = finish_spread(came)

    back_shape = (slot_count, hidden_width)
    incoming, *back = call(
        functools.partial(back_kernel, chips, len(came)),
        "back",
        [spot, weights, *came],
        [SMEM] + [VMEM] * (1 + len(came)),
        [shape((rep_count, expert_count, capacity, seg_rows), jnp.bfloat16)]
        + [shape(back_shape, jnp.bfloat16 if k else jnp.float32) for k in offsets],
    )
    own_back = back[:1]
    back = exchange(back)
    if packed:
        passed = shape((seg_rows + half, seg_rows), jnp.bfloat16)
        first, second = call(
            pass_kernel,
            "pass",
            [from_two, from_one],
            [VMEM, VMEM],
            [passed, passed],
            after=own_back,
        )
        last = (from_peer(first, 1), from_peer(second, 2))
        projections.append(last)
        inputs.append(last)

    forward = None
    late = [3] if packed else []
    for name, group in (("forward", [k for k in offsets if k not in late]), ("rest", late)):
        if not group:
            continue
        operands = [rep, inputs_home] + ([] if forward is None else [forward])
        operands += flatten(projections[k] for k in group)
        lengths = [len(projections[k]) for k in group]
        (forward,) = call(
            functools.partial(forward_kernel, group, lengths, forward is not None),
            name,
            operands,
            [SMEM] + [VMEM] * (len(operands) - 1),
            [shape((2, slot_count, hidden_width), jnp.float32)],
            cost=0 if name == "rest" else 0,
        )

    (own_factors,) = call(
        factor_kernel,
        "factors",
        [forward, *back],
        [VMEM] * (1 + len(back)),
        [shape((2, slot_count + half, hidden_width), jnp.bfloat16)],
    )
    near_factors = gather_near(own_factors)

    operands = [rep, spot, own_factors] + flatten(projections)
    returning = across_chips(
        call(
            functools.partial(slot_kernel, [len(group) for group in projections]),
            "slots",
            operands,
            [SMEM] * 2 + [VMEM] * (len(operands) - 2),
            [shape((2, capacity, model_width), jnp.bfloat16)] * chips,
            scratch=[
                pltpu.VMEM((rep_count, expert_count, capacity, seg_rows), jnp.bfloat16)
            ],
        )
    )
    factors = gather_rest(near_factors, after=returning[:1])
    if rep_count <= 4:
        *merging, first_gram = adasum(rep, inputs, incoming, factors)
        returned = finish_spread(returning, [first_gram], pieces=2)
        unplace_after = merging[2:]
    else:
        returned, unplace_after = finish_spread(returning), ()
    (input_grads,) = call(
        unplace_kernel,
        "unplace",
        [spot, routed[0], *returned],
        [SMEM] + [VMEM] * (1 + len(returned)),
        [shape((1, row_count, model_width), jnp.bfloat16)],
        scratch=[pltpu.VMEM((expert_count, capacity, model_width), jnp.bfloat16)],
        after=unplace_after,
    )
    if rep_count <= 4:
        adam_step = adam(rep, *merging, first_moment, second_moment, ())
    else:
        adam_step = adasum_adam_many(
            rep, [x for (x,) in inputs], incoming, factors, first_moment, second_moment
        )
    return (input_grads, adam_step)


def solution(mesh):
    return jax.shard_map(
        shards,
        mesh=mesh,
        in_specs=(
            P("expert", None, "replica", None),
            P("expert", None, "replica", None),
            P("expert", None, "replica", None),
            P("replica", "expert", None),
            P("replica", "expert", None),
            P("replica", "expert"),
            P(),
            P("replica", "expert", None, None),
        ),
        out_specs=(P("replica", "expert", None), P("expert", None, "replica", None)),
        check_vma=False,
    )
```

```python
import functools

import jax
import jax.numpy as jnp
from jax import lax
from jax.experimental import pallas as pl
from jax.experimental.pallas import tpu as pltpu
from jax.sharding import PartitionSpec as P

beta_first = 0.9
beta_second = 0.95
adam_eps = 1e-08
norm_eps = 1e-06
first_fix = 1.0 - (0.9**50) ** 2
second_fix = 1.0 - (0.95**50) ** 2
MIB = 1024 * 1024
LABEL_ROWS = 16


def contract_first(left, right):
    return lax.dot_general(
        left, right, (((0,), (0,)), ((), ())), preferred_element_type=jnp.float32
    )


def contract_last(left, right):
    return lax.dot_general(
        left, right, (((1,), (1,)), ((), ())), preferred_element_type=jnp.float32
    )


def multiply(left, right):
    return jnp.dot(left, right, preferred_element_type=jnp.float32)


def from_peer(array, offset):
    count = lax.axis_size("replica")
    return lax.ppermute(array, "replica", [(i, i ^ offset) for i in range(count)])


def across_chips(parts):
    count = lax.axis_size("expert")
    return [parts[0]] + [
        lax.ppermute(part, "expert", [(i, i ^ 2 * k) for i in range(count)])
        for k, part in enumerate(parts)
        if k
    ]


def pick_kernel(chips, *refs):
    block_refs = [ref.at[k] for ref in refs[chips:] for k in range(ref.shape[0])]
    for part_ref, block_ref in zip(refs[:chips], block_refs):
        block_ref[...] = part_ref[1]


def finish_spread(came, after=(), pieces=1):
    count = lax.axis_size("expert")
    chips = len(came)
    block = jax.ShapeDtypeStruct((chips // pieces,) + came[0].shape[1:], came[0].dtype)
    others = call(
        functools.partial(pick_kernel, chips),
        "pick",
        came,
        [VMEM] * chips,
        [block] * pieces,
        after=after,
    )
    swapped = [lax.ppermute(x, "expert", [(i, i ^ 1) for i in range(count)]) for x in others]
    return [*came, *swapped]


def spread_block(chips, refs, offset):
    if offset % 2 == 0:
        return refs[offset // 2].at[0]
    blocks = [ref.at[k] for ref in refs[chips:] for k in range(ref.shape[0])]
    return blocks[offset // 2]


def exchange(parts):
    return [parts[0]] + [from_peer(part, k) for k, part in enumerate(parts) if k]


def split_kernel(rep_ref, matrix_ref, *out_refs):
    for offset, out_ref in enumerate(out_refs):
        out_ref[...] = matrix_ref[:, segment(rep_ref, offset, out_ref.shape[1])]


def first_kernel(pair_ref, *out_refs):
    for part, out_ref in enumerate(out_refs):
        out_ref[...] = pair_ref[1 - part]


def second_kernel(pos_ref, pair_ref, inputs_ref, *out_refs):
    seg_rows = pair_ref.shape[1]
    slot_count = inputs_ref.shape[0]
    half = slot_count // 2
    for part, out_ref in enumerate(out_refs):
        out_ref[pl.ds(0, seg_rows), :] = pair_ref[part]
        columns = segment(pos_ref, part + 1, seg_rows)
        out_ref[pl.ds(seg_rows, slot_count), :] = inputs_ref[:, columns]
        columns = segment(pos_ref, 3, seg_rows)
        out_ref[pl.ds(seg_rows + slot_count, half), :] = inputs_ref[
            pl.ds(part * half, half), columns
        ]


def pass_kernel(from_two_ref, from_one_ref, first_ref, second_ref):
    first_ref[...] = from_two_ref[...]
    second_ref[...] = from_one_ref[...]


def projection_rows(refs):
    if len(refs) == 1:
        return refs[0].at[0], refs[0].at[1]
    return tuple(ref.at[pl.ds(0, ref.shape[1])] for ref in refs)


def input_rows(rep_ref, refs, slot_count, seg_rows):
    if len(refs) == 2:
        rows = pl.ds(slot_count + slot_count // 2, slot_count // 2)
        return jnp.concatenate([refs[1][rows], refs[0][rows]], axis=0)
    (ref,) = refs
    if ref.shape[0] > slot_count:
        return ref[pl.ds(seg_rows, slot_count), :]
    return ref[...] if ref.shape[1] == seg_rows else ref[:, segment(rep_ref, 0, seg_rows)]


def cut_kernel(from_two_ref, from_one_ref, *refs):
    tail_refs, out_refs = refs[:-2], refs[-2:]
    for part, (near_ref, out_ref) in enumerate(zip((from_two_ref, from_one_ref), out_refs)):
        rows = near_ref.shape[1]
        out_ref[pl.ds(0, rows), :] = near_ref[part]
        if tail_refs:
            tail = out_ref.shape[0] - rows
            tail_ref = tail_refs[part]
            out_ref[pl.ds(rows, tail), :] = tail_ref[pl.ds(tail_ref.shape[0] - tail, tail), :]


def gather_near(payload):
    count = lax.axis_size("replica")
    if count != 4:
        return exchange([payload] * count)
    from_two = from_peer(payload, 2)
    return [payload, from_peer(payload, 1), from_two]


def gather_rest(near, after, tails=(), rows=0):
    whole = [(part,) for part in near]
    if lax.axis_size("replica") != 4:
        return whole
    half = jax.ShapeDtypeStruct((near[0].shape[1] + rows, near[0].shape[2]), near[0].dtype)
    operands = [near[2], near[1], *tails]
    first, second = call(
        cut_kernel, "cut", operands, [VMEM] * len(operands), [half, half], after=after
    )
    return whole + [(from_peer(first, 1), from_peer(second, 2))]


def halves(refs):
    return refs if len(refs) == 2 else (refs[0].at[0], refs[0].at[1])


def regroup(refs, lengths):
    groups, at = [], 0
    for length in lengths:
        groups.append(refs[at : at + length])
        at += length
    return groups


def flatten(groups):
    return [array for group in groups for array in group]


def pair_list(count):
    return [(i, j) for i in range(count) for j in range(i, count)]


SMEM = pl.BlockSpec(memory_space=pltpu.SMEM)
VMEM = pl.BlockSpec(memory_space=pltpu.VMEM)


def call(
    kernel, name, operands, specs, outs, out_specs=None, grid=(), scratch=(), after=(), cost=0, room=0
):
    size = sum(x.size * x.dtype.itemsize for x in list(operands) + list(outs))
    taken = len(operands)

    def body(*refs):
        kernel(*refs[:taken], *refs[taken + len(after) :])

    return pl.pallas_call(
        body,
        grid=grid,
        in_specs=list(specs) + [VMEM] * len(after),
        out_specs=out_specs if out_specs is not None else [VMEM for _ in outs],
        out_shape=outs,
        scratch_shapes=list(scratch),
        compiler_params=pltpu.CompilerParams(
            dimension_semantics=("arbitrary",) * len(grid),
            vmem_limit_bytes=max(room, min(56 * MIB, size + 8 * MIB)),
        ),
        cost_estimate=pl.CostEstimate(flops=0, bytes_accessed=cost, transcendentals=0),
        name=name,
    )(*operands, *after)


def segment(pos_ref, offset, width):
    return pl.ds(pl.multiple_of((pos_ref[0] ^ offset) * width, width), width)


def rows_kernel(expert_count, pos_ref, ids_ref, task_ref, row_ref, grads_ref, *out_refs):
    row_count = grads_ref.shape[0]
    seg_rows = out_refs[0].shape[1]
    block_count = ids_ref.shape[1]
    block_rows = row_count // block_count
    square = (row_count, row_count)
    earlier = lax.broadcasted_iota(jnp.int32, square, 0) < lax.broadcasted_iota(
        jnp.int32, square, 1
    )
    experts = lax.broadcasted_iota(jnp.int32, (expert_count, row_count), 0)
    chosen = jnp.where(experts == row_ref[...], 1.0, 0.0)
    before = multiply(
        chosen.astype(jnp.bfloat16), jnp.where(earlier, 1.0, 0.0).astype(jnp.bfloat16)
    )
    rank = jnp.sum(chosen * before, axis=0, keepdims=True)
    line = lax.broadcasted_iota(jnp.int32, (LABEL_ROWS, row_count), 0)
    labels = jnp.where(line == 0, row_ref[...].astype(jnp.float32), 0.0)
    labels = jnp.where(line == 1, rank, labels).astype(jnp.bfloat16)
    for offset, out_ref in enumerate(out_refs):
        columns = segment(pos_ref, offset, seg_rows)
        for block in range(block_count):
            rows = pl.ds(block * block_rows, block_rows)
            weight = task_ref[ids_ref[0, block]]
            out_ref[rows, :] = (grads_ref[rows, columns].astype(jnp.float32) * weight).astype(
                jnp.bfloat16
            )
        if row_count < seg_rows:
            out_ref[pl.ds(row_count, LABEL_ROWS), :] = jnp.zeros(
                (LABEL_ROWS, seg_rows), jnp.bfloat16
            )
        out_ref[pl.ds(row_count, LABEL_ROWS), pl.ds(0, row_count)] = labels


def one_hot(block_ref, row_count, slot_count, capacity):
    labels = block_ref[pl.ds(row_count, LABEL_ROWS), pl.ds(0, row_count)].astype(jnp.float32)
    slot = (labels[0:1] * capacity + labels[1:2]).astype(jnp.int32)
    places = lax.broadcasted_iota(jnp.int32, (slot_count, row_count), 0)
    return jnp.where(places == slot, 1.0, 0.0).astype(jnp.bfloat16)


def place_kernel(count, row_count, pos_ref, *refs):
    block_refs, out_refs, placed_ref = refs[:count], refs[count:-1], refs[-1]
    _, expert_count, capacity, seg_rows = placed_ref.shape
    slot_count = expert_count * capacity
    for offset, block_ref in enumerate(block_refs):
        placing = one_hot(block_ref, row_count, slot_count, capacity)
        placed = multiply(placing, block_ref[pl.ds(0, row_count), :])
        placed = placed.reshape(expert_count, capacity, seg_rows)
        placed_ref[offset] = placed.astype(jnp.bfloat16)
        for expert in range(expert_count):
            out_refs[expert // 2][expert % 2, offset] = placed_ref[offset, pos_ref[1] ^ expert]


def unplace_kernel(pos_ref, block_ref, *refs):
    returned_refs, out_ref, slots_ref = refs[:-2], refs[-2], refs[-1]
    expert_count, capacity, _ = slots_ref.shape
    slot_count = expert_count * capacity
    row_count = out_ref.shape[1]
    placing = one_hot(block_ref, row_count, slot_count, capacity)
    for expert in range(expert_count):
        block_ref = spread_block(expert_count // 2, returned_refs, expert)
        slots_ref[pos_ref[1] ^ expert] = block_ref[...]
    out_ref[0] = contract_first(placing, flat_rows(slots_ref[...])).astype(jnp.bfloat16)


def flat_rows(blocks):
    rows = blocks.shape[0] * blocks.shape[1]
    if blocks.shape[1] % 16:
        wide = blocks.astype(jnp.float32).reshape(rows, blocks.shape[2])
        return wide.astype(jnp.bfloat16)
    return blocks.reshape(rows, blocks.shape[2])


def back_kernel(chips, arrays, pos_ref, weight_ref, *refs):
    came_refs, incoming_ref, out_refs = refs[:arrays], refs[arrays], refs[arrays + 1 :]
    for offset, out_ref in enumerate(out_refs):
        for expert in range(2 * chips):
            block_ref = spread_block(chips, came_refs, expert)
            incoming_ref[offset, pos_ref[1] ^ expert] = block_ref[offset]
        rows = flat_rows(incoming_ref[offset])
        out_ref[...] = multiply(rows, weight_ref[...]).astype(out_ref.dtype)


def forward_kernel(terms, count, has_start, pos_ref, inputs_ref, *refs):
    weight_refs, out_ref = refs[:-1], refs[-1]
    totals = [None, None]
    if has_start:
        totals = [weight_refs[0][0], weight_refs[0][1]]
        weight_refs = weight_refs[1:]
    for (offset, which), weight_ref in zip(terms, weight_refs):
        if len(weight_ref.shape) == 3:
            weight_ref = weight_ref.at[which]
        seg_rows = inputs_ref.shape[1] // count
        rows = inputs_ref[:, segment(pos_ref, offset, seg_rows)]
        part = multiply(rows, weight_ref[pl.ds(0, seg_rows), :])
        totals[which] = part if totals[which] is None else totals[which] + part
    for which, total in enumerate(totals):
        out_ref[which] = total


def factor_kernel(forward_ref, *refs):
    back_refs, out_ref = refs[:-1], refs[-1]
    slot_count = forward_ref.shape[1]
    half = slot_count // 2
    hidden_grad = back_refs[0][...]
    for back_ref in back_refs[1:]:
        hidden_grad = hidden_grad + back_ref[...].astype(jnp.float32)
    gate_pre, up_pre = forward_ref[0], forward_ref[1]
    sigmoid_gate = jax.nn.sigmoid(gate_pre)
    gate_act = gate_pre * sigmoid_gate
    hidden = (gate_act * up_pre).astype(jnp.bfloat16)
    gate_grad = hidden_grad * up_pre * sigmoid_gate * (1.0 + gate_pre * (1.0 - sigmoid_gate))
    out_ref[0, pl.ds(0, slot_count)] = gate_grad.astype(jnp.bfloat16)
    out_ref[1, pl.ds(0, slot_count)] = (hidden_grad * gate_act).astype(jnp.bfloat16)
    for part in range(2):
        out_ref[part, pl.ds(slot_count, half)] = hidden[part * half : (part + 1) * half]


def slot_kernel(lengths, pos_ref, factor_ref, *refs):
    chips = refs[-1].shape[1] // 2
    weight_refs, out_refs, slots_ref = refs[: -chips - 1], refs[-chips - 1 : -1], refs[-1]
    _, expert_count, capacity, seg_rows = slots_ref.shape
    rows = pl.ds(0, expert_count * capacity)
    gate_grad, up_grad = factor_ref[0, rows], factor_ref[1, rows]
    for offset, group in enumerate(regroup(weight_refs, lengths)):
        gate_ref, up_ref = projection_rows(group)
        total = contract_last(gate_grad, gate_ref[...]) + contract_last(up_grad, up_ref[...])
        total = total.reshape(expert_count, capacity, seg_rows)
        slots_ref[offset] = total.astype(jnp.bfloat16)
        columns = segment(pos_ref, offset, seg_rows)
        for expert in range(expert_count):
            out_ref = out_refs[expert // 2]
            out_ref[expert % 2, :, columns] = slots_ref[offset, pos_ref[1] ^ expert]


def gram_kernel(count, offsets, lengths, place, rep_ref, *refs):
    if place:
        before_ref, earlier_ref, refs = refs[0], refs[1], refs[2:]
    incoming_ref, operand_refs, grads_ref, gram_ref = refs[0], refs[1:-2], refs[-2], refs[-1]
    middle = incoming_ref.shape[1] // 2
    seg_rows, hidden_width = grads_ref.shape[2:]
    slot_count = incoming_ref.shape[1] * incoming_ref.shape[2]
    groups = regroup(operand_refs, lengths)
    known = list(range(place)) + list(offsets)
    pairs = [(i, j) for i, j in pair_list(len(known)) if j >= place]
    lines = 8
    tile = min(seg_rows, 256)
    sums = [jnp.zeros((lines, hidden_width), jnp.float32) for _ in pairs]
    operands = []
    for at, offset in enumerate(offsets):
        input_refs, factor_refs = groups[2 * at : 2 * at + 2]
        rest = pl.ds(slot_count, slot_count // 2)
        columns = input_rows(rep_ref, input_refs, slot_count, seg_rows)
        gate_ref, up_ref = (ref.at[pl.ds(0, slot_count)] for ref in halves(factor_refs))
        first_ref, second_ref = (ref.at[rest] for ref in halves(factor_refs))
        upper = flat_rows(incoming_ref[offset, :middle])
        lower = flat_rows(incoming_ref[offset, middle:])
        operands.append(
            [
                [(columns, gate_ref)],
                [(columns, up_ref)],
                [(upper, first_ref), (lower, second_ref)],
            ]
        )
    for matrix in range(3):
        for start in range(0, seg_rows, tile):
            rows = pl.ds(start, tile)
            blocks = [earlier_ref[at, matrix, rows] for at in range(place)]
            for at in range(len(offsets)):
                block = None
                for left, right_ref in operands[at][matrix]:
                    part = contract_first(left[:, start : start + tile], right_ref[...])
                    block = part if block is None else block + part
                grads_ref[at, matrix, rows] = block
                blocks.append(block)
            for place_of, (i, j) in enumerate(pairs):
                products = (blocks[i] * blocks[j]).reshape(tile // lines, lines, hidden_width)
                sums[place_of] = sums[place_of] + jnp.sum(products, axis=0)
    gram_ref[...] = before_ref[...] if place else jnp.zeros_like(gram_ref)
    for total, (i, j) in zip(sums, pairs):
        total = jnp.sum(total, axis=0, keepdims=True)
        part = total[:, :128]
        for lane in range(128, hidden_width, 128):
            part = part + total[:, lane : lane + 128]
        first, second = rep_ref[0] ^ known[i], rep_ref[0] ^ known[j]
        row = jnp.minimum(first, second) * count + jnp.maximum(first, second)
        gram_ref[pl.ds(row, 1), :] = part


def merge_coefs(gram, count):
    vectors = [{rep: None} for rep in range(count)]

    def term(coef, value):
        return value if coef is None else coef * value

    def inner(left, right):
        total = None
        for i, left_coef in left.items():
            for j, right_coef in right.items():
                value = term(left_coef, term(right_coef, gram[min(i, j), max(i, j)]))
                total = value if total is None else total + value
        return total

    while len(vectors) > 1:
        merged = []
        for first, second in zip(vectors[0::2], vectors[1::2]):
            norm_first = jnp.maximum(inner(first, first), 0.0)
            norm_second = jnp.maximum(inner(second, second), 0.0)
            bound = jnp.sqrt(norm_first) * jnp.sqrt(norm_second)
            cross = jnp.minimum(jnp.maximum(inner(first, second), -bound), bound)
            coef_first = 1.0 - cross / (2.0 * (norm_first + norm_eps))
            coef_second = 1.0 - cross / (2.0 * (norm_second + norm_eps))
            joined = {rep: term(coef, coef_first) for rep, coef in first.items()}
            joined.update({rep: term(coef, coef_second) for rep, coef in second.items()})
            merged.append(joined)
        vectors = merged
    return [vectors[0][rep] for rep in range(count)]


def adam_kernel(count, places, rep_ref, *refs):
    gram_refs, grads_refs = refs[:count], refs[count : count + len(places)]
    first_ref, second_ref, step_ref, coef_ref = refs[count + len(places) :]
    block_rows, hidden_width = step_ref.shape[2:]
    lines = coef_ref.shape[1]

    @pl.when((pl.program_id(0) == 0) & (pl.program_id(1) == 0))
    def _():
        sums = gram_refs[0][...]
        for gram_ref in gram_refs[1:]:
            sums = sums + gram_ref[...]
        sums = jnp.sum(sums, axis=1, keepdims=True)
        gram = {(i, j): sums[i * count + j : i * count + j + 1] for i, j in pair_list(count)}
        for rep, coef in enumerate(merge_coefs(gram, count)):
            coef_ref[rep] = jnp.broadcast_to(coef, coef_ref.shape[1:])

    matrix = pl.program_id(0)
    block = pl.program_id(1) * block_rows
    coefs = [[coef_ref[rep_ref[0] ^ offset] for offset in offsets] for offsets in places]

    def step(index, _):
        rows = pl.ds(pl.multiple_of(index * lines, lines), lines)
        all_rows = pl.ds(pl.multiple_of(block + index * lines, lines), lines)
        for lane in range(0, hidden_width, 128):
            columns = pl.ds(lane, 128)
            merged = None
            for grads_ref, group in zip(grads_refs, coefs):
                for at, coef in enumerate(group):
                    part = grads_ref[at, matrix, all_rows, columns] * coef
                    merged = part if merged is None else merged + part
            first_new = (beta_first / first_fix) * first_ref[0, matrix, all_rows, columns] + (
                (1.0 - beta_first) / first_fix
            ) * merged
            second_new = (beta_second / second_fix) * second_ref[0, matrix, all_rows, columns] + (
                (1.0 - beta_second) / second_fix
            ) * (merged * merged)
            root = second_new * lax.rsqrt(second_new)
            step_ref[0, 0, rows, columns] = first_new / (root + adam_eps)
        return 0

    lax.fori_loop(0, block_rows // lines, step, 0, unroll=2)


def adasum_adam_many(rep, inputs, incoming, factors, first_moment, second_moment):
    count = len(inputs)
    half = inputs[0].shape[0] // 2
    grads = []
    for offset in range(count):
        (payload,) = factors[offset]
        gate_grad, up_grad = payload[:, : 2 * half]
        hidden = payload[:, 2 * half :].reshape(2 * half, -1)
        received = incoming[offset].reshape(2 * half, incoming.shape[3])
        grads.append(
            jnp.stack(
                [
                    contract_first(inputs[offset], gate_grad),
                    contract_first(inputs[offset], up_grad),
                    contract_first(received, hidden),
                ]
            )
        )
    grads = jnp.stack(grads)[rep[0] ^ jnp.arange(count)]
    flat = grads.reshape(count, -1)
    gram = lax.psum(jnp.matmul(flat, flat.T, precision=lax.Precision.HIGHEST), "replica")
    coefs = jnp.eye(count, dtype=jnp.float32)
    while coefs.shape[0] > 1:
        inner = jnp.matmul(
            jnp.matmul(coefs, gram, precision=lax.Precision.HIGHEST),
            coefs.T,
            precision=lax.Precision.HIGHEST,
        )
        norms = jnp.maximum(jnp.diagonal(inner), 0.0)
        norm_first, norm_second = norms[0::2], norms[1::2]
        bound = jnp.sqrt(norm_first) * jnp.sqrt(norm_second)
        cross = jnp.clip(jnp.diagonal(inner, offset=1)[0::2], -bound, bound)
        coef_first = 1.0 - cross / (2.0 * (norm_first + norm_eps))
        coef_second = 1.0 - cross / (2.0 * (norm_second + norm_eps))
        coefs = coef_first[:, None] * coefs[0::2] + coef_second[:, None] * coefs[1::2]
    merged = jnp.sum(coefs[0][:, None, None, None] * grads, axis=0)
    first_new = beta_first * first_moment[0] + (1.0 - beta_first) * merged
    second_new = beta_second * second_moment[0] + (1.0 - beta_second) * merged * merged
    return ((first_new / first_fix) / (jnp.sqrt(second_new / second_fix) + adam_eps))[None]


def adasum(rep, inputs, incoming, factors):
    count = len(inputs)
    seg_rows, hidden_width = incoming.shape[3], factors[0][0].shape[2]
    shape = jax.ShapeDtypeStruct
    groups = [[k for k in range(count) if k < 3], [k for k in range(count) if k == 3]]
    groups = [group for group in groups if group]
    grads, gram, first_gram, place = [], None, None, 0
    for group in groups:
        operands = [rep] if gram is None else [rep, gram, grads[0]]
        parts = [x for k in group for x in (inputs[k], factors[k])]
        operands += [incoming] + flatten(parts)
        more, gram = call(
            functools.partial(gram_kernel, count, group, [len(x) for x in parts], place),
            "gram_late" if place else "gram",
            operands,
            [SMEM] + [VMEM] * (len(operands) - 1),
            [
                shape((len(group), 3, seg_rows, hidden_width), jnp.float32),
                shape((max(8, count * count), 128), jnp.float32),
            ],
            cost=0 if place else 0,
        )
        first_gram = gram if first_gram is None else first_gram
        grads.append(more)
        place += len(group)
    return groups, grads, gram, first_gram


def adam(rep, groups, grads, gram, first_moment, second_moment, after):
    count = sum(len(group) for group in groups)
    seg_rows, hidden_width = first_moment.shape[2:]
    grams = exchange([gram] * count)
    tile = min(seg_rows, 256)
    moment_spec = pl.BlockSpec((1, 1, tile, hidden_width), lambda m, d: (0, m, d, 0))
    (adam_step,) = call(
        functools.partial(adam_kernel, count, groups),
        "adam",
        [rep, *grams, *grads, first_moment, second_moment],
        [SMEM] + [VMEM] * (len(grams) + len(grads) + 2),
        [jax.ShapeDtypeStruct(first_moment.shape, jnp.float32)],
        out_specs=[moment_spec],
        grid=(3, seg_rows // tile),
        scratch=[pltpu.VMEM((count, 16, 128), jnp.float32)],
        after=after,
    )
    return adam_step


def shards(
    weights, first_moment, second_moment, out_grads, routes, task_ids, task_weights, saved_inputs
):
    expert_count = lax.axis_size("expert")
    rep_count = lax.axis_size("replica")
    row_count = out_grads.shape[1]
    model_width = out_grads.shape[2]
    hidden_width = weights.shape[3]
    slot_count = saved_inputs.shape[2]
    capacity = slot_count // expert_count
    seg_rows = model_width // rep_count
    half = slot_count // 2
    offsets = range(rep_count)
    chips = expert_count // 2
    rep = jnp.stack([lax.axis_index("replica"), lax.axis_index("expert")]).astype(jnp.int32)
    shape = jax.ShapeDtypeStruct

    block = shape((row_count + LABEL_ROWS, seg_rows), jnp.bfloat16)
    small = [routes[0].reshape(1, row_count), out_grads[0]]
    row_blocks = call(
        functools.partial(rows_kernel, expert_count),
        "rows",
        [lax.axis_index("replica").astype(jnp.int32).reshape(1), task_ids, task_weights, *small],
        [SMEM] * 3 + [pl.BlockSpec(x.shape, lambda i: (0, 0)) for x in small],
        [block for _ in offsets],
        grid=(1,),
        room=56 * MIB,
    )
    routed = exchange(row_blocks)

    inputs_home = saved_inputs[0, 0]
    pair = weights[0, :2]
    packed = rep_count == 4 and seg_rows == hidden_width
    if packed:
        part = shape((seg_rows, hidden_width), jnp.bfloat16)
        to_one, to_two = call(first_kernel, "first", [pair], [VMEM], [part, part])
        up_one, gate_two = from_peer(to_one, 1), from_peer(to_two, 2)
        to_one, to_two = call(
            pass_kernel,
            "pass",
            [gate_two, up_one],
            [VMEM, VMEM],
            [part, part],
            after=routed[1:],
        )
        last = (from_peer(to_one, 1), from_peer(to_two, 2))
        part = shape((seg_rows + slot_count + half, seg_rows), jnp.bfloat16)
        to_one, to_two = call(
            second_kernel,
            "second",
            [rep, pair, inputs_home],
            [SMEM, VMEM, VMEM],
            [part, part],
            after=last,
        )
        gate_one, up_two = from_peer(to_one, 1), from_peer(to_two, 2)
        projections = [(pair,), (gate_one, up_one), (gate_two, up_two), last]
        inputs = [(inputs_home,), (gate_one,), (up_two,)]
        late = [(1, 0), (2, 1)]
        tails = [up_two, gate_one]
    else:
        projections = [(x,) for x in exchange([pair] * rep_count)]
        pieces = [shape((slot_count, seg_rows), jnp.bfloat16) for _ in offsets]
        pieces = call(split_kernel, "split", [rep, inputs_home], [SMEM, VMEM], pieces)
        inputs = [(x,) for x in exchange(pieces)]
        late, tails = [], []

    part = shape((2, rep_count, capacity, seg_rows), jnp.bfloat16)
    placed = (
        call(
            functools.partial(place_kernel, rep_count, row_count),
            "place",
            [rep, *routed],
            [SMEM] + [VMEM] * len(routed),
            [part] * chips,
            scratch=[
                pltpu.VMEM((rep_count, expert_count, capacity, seg_rows), jnp.bfloat16)
            ],
        )
    )

    came = across_chips(placed)

    came = finish_spread(came)

    back_shape = (slot_count, hidden_width)
    incoming, *back = call(
        functools.partial(back_kernel, chips, len(came)),
        "back",
        [rep, weights[0, 2], *came],
        [SMEM] + [VMEM] * (1 + len(came)),
        [shape((rep_count, expert_count, capacity, seg_rows), jnp.bfloat16)]
        + [shape(back_shape, jnp.bfloat16 if k else jnp.float32) for k in offsets],
    )
    own_back = back[:1]
    back = exchange(back)
    forward = None
    terms = [(k, which) for k in offsets for which in range(2)]
    for name, group in (("forward", [x for x in terms if x not in late]), ("rest", late)):
        if not group:
            continue
        operands = [rep, inputs_home] + ([] if forward is None else [forward])
        operands += [(projections[k] * 2)[which] if k else pair for k, which in group]
        (forward,) = call(
            functools.partial(forward_kernel, group, rep_count, forward is not None),
            name,
            operands,
            [SMEM] + [VMEM] * (len(operands) - 1),
            [shape((2, slot_count, hidden_width), jnp.float32)],
        )
    (own_factors,) = call(
        factor_kernel,
        "factors",
        [forward, *back],
        [VMEM] * (1 + len(back)),
        [shape((2, slot_count + half, hidden_width), jnp.bfloat16)],
    )
    near_factors = gather_near(own_factors)

    operands = [rep, own_factors] + flatten(projections)
    returning = across_chips(
        call(
            functools.partial(slot_kernel, [len(group) for group in projections]),
            "slots",
            operands,
            [SMEM] + [VMEM] * (len(operands) - 1),
            [shape((2, capacity, model_width), jnp.bfloat16)] * chips,
            scratch=[
                pltpu.VMEM((rep_count, expert_count, capacity, seg_rows), jnp.bfloat16)
            ],
        )
    )
    factors = gather_rest(near_factors, returning[:1], tails, half if tails else 0)
    inputs += factors[3:] if tails else []
    if rep_count <= 4:
        *merging, first_gram = adasum(rep, inputs, incoming, factors)
        returned = finish_spread(returning, [first_gram])
        unplace_after = merging[2:]
    else:
        returned, unplace_after = finish_spread(returning), ()
    (input_grads,) = call(
        unplace_kernel,
        "unplace",
        [rep, routed[0], *returned],
        [SMEM] + [VMEM] * (1 + len(returned)),
        [shape((1, row_count, model_width), jnp.bfloat16)],
        scratch=[pltpu.VMEM((expert_count, capacity, model_width), jnp.bfloat16)],
        after=unplace_after,
    )
    if rep_count <= 4:
        adam_step = adam(rep, *merging, first_moment, second_moment, ())
    else:
        adam_step = adasum_adam_many(
            rep, [x for (x,) in inputs], incoming, factors, first_moment, second_moment
        )
    return (input_grads, adam_step)


def solution(mesh):
    return jax.shard_map(
        shards,
        mesh=mesh,
        in_specs=(
            P("expert", None, "replica", None),
            P("expert", None, "replica", None),
            P("expert", None, "replica", None),
            P("replica", "expert", None),
            P("replica", "expert", None),
            P("replica", "expert"),
            P(),
            P("replica", "expert", None, None),
        ),
        out_specs=(P("replica", "expert", None), P("expert", None, "replica", None)),
        check_vma=False,
    )
```

```python
import functools

import jax
import jax.numpy as jnp
from jax import lax
from jax.experimental import pallas as pl
from jax.experimental.pallas import tpu as pltpu
from jax.sharding import PartitionSpec as P

beta_first = 0.9
beta_second = 0.95
adam_eps = 1e-08
norm_eps = 1e-06
first_fix = 1.0 - (0.9**50) ** 2
second_fix = 1.0 - (0.95**50) ** 2
MIB = 1024 * 1024
LABEL_ROWS = 16


def contract_first(left, right):
    return lax.dot_general(
        left, right, (((0,), (0,)), ((), ())), preferred_element_type=jnp.float32
    )


def contract_last(left, right):
    return lax.dot_general(
        left, right, (((1,), (1,)), ((), ())), preferred_element_type=jnp.float32
    )


def multiply(left, right):
    return jnp.dot(left, right, preferred_element_type=jnp.float32)


def from_peer(array, offset):
    count = lax.axis_size("replica")
    return lax.ppermute(array, "replica", [(i, i ^ offset) for i in range(count)])


def across_chips(parts):
    count = lax.axis_size("expert")
    return [parts[0]] + [
        lax.ppermute(part, "expert", [(i, i ^ 2 * k) for i in range(count)])
        for k, part in enumerate(parts)
        if k
    ]


def pick_kernel(chips, *refs):
    block_refs = [ref.at[k] for ref in refs[chips:] for k in range(ref.shape[0])]
    for part_ref, block_ref in zip(refs[:chips], block_refs):
        block_ref[...] = part_ref[1]


def finish_spread(came, after=(), pieces=1):
    count = lax.axis_size("expert")
    chips = len(came)
    block = jax.ShapeDtypeStruct((chips // pieces,) + came[0].shape[1:], came[0].dtype)
    others = call(
        functools.partial(pick_kernel, chips),
        "pick",
        came,
        [VMEM] * chips,
        [block] * pieces,
        after=after,
    )
    swapped = [lax.ppermute(x, "expert", [(i, i ^ 1) for i in range(count)]) for x in others]
    return [*came, *swapped]


def spread_block(chips, refs, offset):
    if offset % 2 == 0:
        return refs[offset // 2].at[0]
    blocks = [ref.at[k] for ref in refs[chips:] for k in range(ref.shape[0])]
    return blocks[offset // 2]


def exchange(parts):
    return [parts[0]] + [from_peer(part, k) for k, part in enumerate(parts) if k]


def split_kernel(rep_ref, matrix_ref, *out_refs):
    for offset, out_ref in enumerate(out_refs):
        out_ref[...] = matrix_ref[:, segment(rep_ref, offset, out_ref.shape[1])]


def payload_kernel(rep_ref, pair_ref, inputs_ref, *out_refs):
    seg_rows = pair_ref.shape[1]
    slot_count = inputs_ref.shape[0]
    half = slot_count // 2
    for part, out_ref in enumerate(out_refs):
        out_ref[pl.ds(0, seg_rows), :] = pair_ref[0]
        out_ref[pl.ds(seg_rows, seg_rows), :] = pair_ref[1]
        columns = segment(rep_ref, part + 1, seg_rows)
        out_ref[pl.ds(2 * seg_rows, slot_count), :] = inputs_ref[:, columns]
        columns = segment(rep_ref, 3, seg_rows)
        out_ref[pl.ds(2 * seg_rows + slot_count, half), :] = inputs_ref[
            pl.ds(part * half, half), columns
        ]


def pass_kernel(from_two_ref, from_one_ref, *out_refs):
    for part, (near_ref, out_ref) in enumerate(zip((from_two_ref, from_one_ref), out_refs)):
        seg_rows = near_ref.shape[1]
        half = out_ref.shape[0] - seg_rows
        out_ref[pl.ds(0, seg_rows), :] = near_ref[pl.ds(part * seg_rows, seg_rows), :]
        out_ref[pl.ds(seg_rows, half), :] = near_ref[pl.ds(near_ref.shape[0] - half, half), :]


def projection_rows(refs):
    if len(refs) == 1 and len(refs[0].shape) == 3:
        return refs[0].at[0], refs[0].at[1]
    seg_rows = refs[0].shape[1]
    start = 0 if len(refs) == 2 else seg_rows
    return refs[0].at[pl.ds(0, seg_rows)], refs[-1].at[pl.ds(start, seg_rows)]


def input_rows(rep_ref, refs, slot_count, seg_rows):
    if len(refs) == 2:
        rows = pl.ds(seg_rows, slot_count // 2)
        return jnp.concatenate([refs[1][rows], refs[0][rows]], axis=0)
    (ref,) = refs
    if ref.shape[0] > slot_count:
        return ref[pl.ds(2 * seg_rows, slot_count), :]
    return ref[...] if ref.shape[1] == seg_rows else ref[:, segment(rep_ref, 0, seg_rows)]


def cut_kernel(from_two_ref, from_one_ref, first_ref, second_ref):
    first_ref[...] = from_two_ref[0]
    second_ref[...] = from_one_ref[1]


def gather_near(payload):
    count = lax.axis_size("replica")
    if count != 4:
        return exchange([payload] * count)
    from_two = from_peer(payload, 2)
    return [payload, from_peer(payload, 1), from_two]


def gather_rest(near, after):
    whole = [(part,) for part in near]
    if lax.axis_size("replica") != 4:
        return whole
    half = jax.ShapeDtypeStruct(near[0].shape[1:], near[0].dtype)
    first, second = call(
        cut_kernel, "cut", [near[2], near[1]], [VMEM, VMEM], [half, half], after=after
    )
    return whole + [(from_peer(first, 1), from_peer(second, 2))]


def halves(refs):
    return refs if len(refs) == 2 else (refs[0].at[0], refs[0].at[1])


def regroup(refs, lengths):
    groups, at = [], 0
    for length in lengths:
        groups.append(refs[at : at + length])
        at += length
    return groups


def flatten(groups):
    return [array for group in groups for array in group]


def pair_list(count):
    return [(i, j) for i in range(count) for j in range(i, count)]


SMEM = pl.BlockSpec(memory_space=pltpu.SMEM)
VMEM = pl.BlockSpec(memory_space=pltpu.VMEM)


def call(
    kernel, name, operands, specs, outs, out_specs=None, grid=(), scratch=(), after=(), cost=0, room=0
):
    size = sum(x.size * x.dtype.itemsize for x in list(operands) + list(outs))
    taken = len(operands)

    def body(*refs):
        kernel(*refs[:taken], *refs[taken + len(after) :])

    return pl.pallas_call(
        body,
        grid=grid,
        in_specs=list(specs) + [VMEM] * len(after),
        out_specs=out_specs if out_specs is not None else [VMEM for _ in outs],
        out_shape=outs,
        scratch_shapes=list(scratch),
        compiler_params=pltpu.CompilerParams(
            dimension_semantics=("arbitrary",) * len(grid),
            vmem_limit_bytes=max(room, min(56 * MIB, size + 8 * MIB)),
        ),
        cost_estimate=pl.CostEstimate(flops=0, bytes_accessed=cost, transcendentals=0),
        name=name,
    )(*operands, *after)


def segment(rep_ref, offset, width):
    return pl.ds(pl.multiple_of((rep_ref[0] ^ offset) * width, width), width)


def rows_kernel(expert_count, rep_ref, ids_ref, task_ref, row_ref, grads_ref, *out_refs):
    row_count = grads_ref.shape[0]
    seg_rows = out_refs[0].shape[1]
    block_count = ids_ref.shape[1]
    block_rows = row_count // block_count
    square = (row_count, row_count)
    earlier = lax.broadcasted_iota(jnp.int32, square, 0) < lax.broadcasted_iota(
        jnp.int32, square, 1
    )
    experts = lax.broadcasted_iota(jnp.int32, (expert_count, row_count), 0)
    chosen = jnp.where(experts == row_ref[...], 1.0, 0.0)
    before = multiply(
        chosen.astype(jnp.bfloat16), jnp.where(earlier, 1.0, 0.0).astype(jnp.bfloat16)
    )
    rank = jnp.sum(chosen * before, axis=0, keepdims=True)
    line = lax.broadcasted_iota(jnp.int32, (LABEL_ROWS, row_count), 0)
    labels = jnp.where(line == 0, row_ref[...].astype(jnp.float32), 0.0)
    labels = jnp.where(line == 1, rank, labels).astype(jnp.bfloat16)
    for offset, out_ref in enumerate(out_refs):
        columns = segment(rep_ref, offset, seg_rows)
        for block in range(block_count):
            rows = pl.ds(block * block_rows, block_rows)
            weight = task_ref[ids_ref[0, block]]
            out_ref[rows, :] = (grads_ref[rows, columns].astype(jnp.float32) * weight).astype(
                jnp.bfloat16
            )
        if row_count < seg_rows:
            out_ref[pl.ds(row_count, LABEL_ROWS), :] = jnp.zeros(
                (LABEL_ROWS, seg_rows), jnp.bfloat16
            )
        out_ref[pl.ds(row_count, LABEL_ROWS), pl.ds(0, row_count)] = labels


def one_hot(block_ref, row_count, slot_count, capacity):
    labels = block_ref[pl.ds(row_count, LABEL_ROWS), pl.ds(0, row_count)].astype(jnp.float32)
    slot = (labels[0:1] * capacity + labels[1:2]).astype(jnp.int32)
    places = lax.broadcasted_iota(jnp.int32, (slot_count, row_count), 0)
    return jnp.where(places == slot, 1.0, 0.0).astype(jnp.bfloat16)


def place_kernel(count, row_count, spot_ref, *refs):
    block_refs, out_refs, placed_ref = refs[:count], refs[count:-1], refs[-1]
    _, expert_count, capacity, seg_rows = placed_ref.shape
    slot_count = expert_count * capacity
    for offset, block_ref in enumerate(block_refs):
        placing = one_hot(block_ref, row_count, slot_count, capacity)
        placed = multiply(placing, block_ref[pl.ds(0, row_count), :])
        placed = placed.reshape(expert_count, capacity, seg_rows)
        placed_ref[offset] = placed.astype(jnp.bfloat16)
        for expert in range(expert_count):
            out_refs[expert // 2][expert % 2, offset] = placed_ref[offset, spot_ref[0] ^ expert]


def unplace_kernel(spot_ref, block_ref, *refs):
    returned_refs, out_ref, slots_ref = refs[:-2], refs[-2], refs[-1]
    expert_count, capacity, _ = slots_ref.shape
    slot_count = expert_count * capacity
    row_count = out_ref.shape[1]
    placing = one_hot(block_ref, row_count, slot_count, capacity)
    for expert in range(expert_count):
        block_ref = spread_block(expert_count // 2, returned_refs, expert)
        slots_ref[spot_ref[0] ^ expert] = block_ref[...]
    out_ref[0] = contract_first(placing, flat_rows(slots_ref[...])).astype(jnp.bfloat16)


def flat_rows(blocks):
    rows = blocks.shape[0] * blocks.shape[1]
    if blocks.shape[1] % 16:
        wide = blocks.astype(jnp.float32).reshape(rows, blocks.shape[2])
        return wide.astype(jnp.bfloat16)
    return blocks.reshape(rows, blocks.shape[2])


def back_kernel(chips, arrays, spot_ref, weight_ref, *refs):
    came_refs, incoming_ref, out_refs = refs[:arrays], refs[arrays], refs[arrays + 1 :]
    for offset, out_ref in enumerate(out_refs):
        for expert in range(2 * chips):
            block_ref = spread_block(chips, came_refs, expert)
            incoming_ref[offset, spot_ref[0] ^ expert] = block_ref[offset]
        rows = flat_rows(incoming_ref[offset])
        out_ref[...] = multiply(rows, weight_ref[...]).astype(out_ref.dtype)


def forward_kernel(offsets, lengths, has_start, rep_ref, inputs_ref, *refs):
    out_ref = refs[-1]
    weight_refs = refs[:-1]
    gate = up = None
    if has_start:
        gate, up = weight_refs[0][0], weight_refs[0][1]
        weight_refs = weight_refs[1:]
    for offset, group in zip(offsets, regroup(weight_refs, lengths)):
        gate_ref, up_ref = projection_rows(group)
        rows = inputs_ref[:, segment(rep_ref, offset, gate_ref.shape[0])]
        gate_part, up_part = multiply(rows, gate_ref[...]), multiply(rows, up_ref[...])
        gate = gate_part if gate is None else gate + gate_part
        up = up_part if up is None else up + up_part
    out_ref[0] = gate
    out_ref[1] = up


def factor_kernel(forward_ref, *refs):
    back_refs, out_ref = refs[:-1], refs[-1]
    slot_count = forward_ref.shape[1]
    half = slot_count // 2
    hidden_grad = back_refs[0][...]
    for back_ref in back_refs[1:]:
        hidden_grad = hidden_grad + back_ref[...].astype(jnp.float32)
    gate_pre, up_pre = forward_ref[0], forward_ref[1]
    sigmoid_gate = jax.nn.sigmoid(gate_pre)
    gate_act = gate_pre * sigmoid_gate
    hidden = (gate_act * up_pre).astype(jnp.bfloat16)
    gate_grad = hidden_grad * up_pre * sigmoid_gate * (1.0 + gate_pre * (1.0 - sigmoid_gate))
    out_ref[0, pl.ds(0, slot_count)] = gate_grad.astype(jnp.bfloat16)
    out_ref[1, pl.ds(0, slot_count)] = (hidden_grad * gate_act).astype(jnp.bfloat16)
    for part in range(2):
        out_ref[part, pl.ds(slot_count, half)] = hidden[part * half : (part + 1) * half]


def slot_kernel(lengths, rep_ref, spot_ref, factor_ref, *refs):
    chips = refs[-1].shape[1] // 2
    weight_refs, out_refs, slots_ref = refs[: -chips - 1], refs[-chips - 1 : -1], refs[-1]
    _, expert_count, capacity, seg_rows = slots_ref.shape
    rows = pl.ds(0, expert_count * capacity)
    gate_grad, up_grad = factor_ref[0, rows], factor_ref[1, rows]
    for offset, group in enumerate(regroup(weight_refs, lengths)):
        gate_ref, up_ref = projection_rows(group)
        total = contract_last(gate_grad, gate_ref[...]) + contract_last(up_grad, up_ref[...])
        total = total.reshape(expert_count, capacity, seg_rows)
        slots_ref[offset] = total.astype(jnp.bfloat16)
        columns = segment(rep_ref, offset, seg_rows)
        for expert in range(expert_count):
            out_ref = out_refs[expert // 2]
            out_ref[expert % 2, :, columns] = slots_ref[offset, spot_ref[0] ^ expert]


def gram_kernel(count, offsets, lengths, place, rep_ref, *refs):
    if place:
        before_ref, earlier_ref, refs = refs[0], refs[1], refs[2:]
    incoming_ref, operand_refs, grads_ref, gram_ref = refs[0], refs[1:-2], refs[-2], refs[-1]
    middle = incoming_ref.shape[1] // 2
    seg_rows, hidden_width = grads_ref.shape[2:]
    slot_count = incoming_ref.shape[1] * incoming_ref.shape[2]
    groups = regroup(operand_refs, lengths)
    known = list(range(place)) + list(offsets)
    pairs = [(i, j) for i, j in pair_list(len(known)) if j >= place]
    lines = 8
    tile = min(seg_rows, 256)
    sums = [jnp.zeros((lines, hidden_width), jnp.float32) for _ in pairs]
    operands = []
    for at, offset in enumerate(offsets):
        input_refs, factor_refs = groups[2 * at : 2 * at + 2]
        rest = pl.ds(slot_count, slot_count // 2)
        columns = input_rows(rep_ref, input_refs, slot_count, seg_rows)
        gate_ref, up_ref = (ref.at[pl.ds(0, slot_count)] for ref in halves(factor_refs))
        first_ref, second_ref = (ref.at[rest] for ref in halves(factor_refs))
        upper = flat_rows(incoming_ref[offset, :middle])
        lower = flat_rows(incoming_ref[offset, middle:])
        operands.append(
            [
                [(columns, gate_ref)],
                [(columns, up_ref)],
                [(upper, first_ref), (lower, second_ref)],
            ]
        )
    for matrix in range(3):
        for start in range(0, seg_rows, tile):
            rows = pl.ds(start, tile)
            blocks = [earlier_ref[at, matrix, rows] for at in range(place)]
            for at in range(len(offsets)):
                block = None
                for left, right_ref in operands[at][matrix]:
                    part = contract_first(left[:, start : start + tile], right_ref[...])
                    block = part if block is None else block + part
                grads_ref[at, matrix, rows] = block
                blocks.append(block)
            for place_of, (i, j) in enumerate(pairs):
                products = (blocks[i] * blocks[j]).reshape(tile // lines, lines, hidden_width)
                sums[place_of] = sums[place_of] + jnp.sum(products, axis=0)
    gram_ref[...] = before_ref[...] if place else jnp.zeros_like(gram_ref)
    for total, (i, j) in zip(sums, pairs):
        total = jnp.sum(total, axis=0, keepdims=True)
        part = total[:, :128]
        for lane in range(128, hidden_width, 128):
            part = part + total[:, lane : lane + 128]
        first, second = rep_ref[0] ^ known[i], rep_ref[0] ^ known[j]
        row = jnp.minimum(first, second) * count + jnp.maximum(first, second)
        gram_ref[pl.ds(row, 1), :] = part


def merge_coefs(gram, count):
    vectors = [{rep: None} for rep in range(count)]

    def term(coef, value):
        return value if coef is None else coef * value

    def inner(left, right):
        total = None
        for i, left_coef in left.items():
            for j, right_coef in right.items():
                value = term(left_coef, term(right_coef, gram[min(i, j), max(i, j)]))
                total = value if total is None else total + value
        return total

    while len(vectors) > 1:
        merged = []
        for first, second in zip(vectors[0::2], vectors[1::2]):
            norm_first = jnp.maximum(inner(first, first), 0.0)
            norm_second = jnp.maximum(inner(second, second), 0.0)
            bound = jnp.sqrt(norm_first) * jnp.sqrt(norm_second)
            cross = jnp.minimum(jnp.maximum(inner(first, second), -bound), bound)
            coef_first = 1.0 - cross / (2.0 * (norm_first + norm_eps))
            coef_second = 1.0 - cross / (2.0 * (norm_second + norm_eps))
            joined = {rep: term(coef, coef_first) for rep, coef in first.items()}
            joined.update({rep: term(coef, coef_second) for rep, coef in second.items()})
            merged.append(joined)
        vectors = merged
    return [vectors[0][rep] for rep in range(count)]


def adam_kernel(count, places, rep_ref, *refs):
    gram_refs, grads_refs = refs[:count], refs[count : count + len(places)]
    first_ref, second_ref, step_ref, coef_ref = refs[count + len(places) :]
    block_rows, hidden_width = step_ref.shape[2:]
    lines = coef_ref.shape[1]

    @pl.when((pl.program_id(0) == 0) & (pl.program_id(1) == 0))
    def _():
        sums = gram_refs[0][...]
        for gram_ref in gram_refs[1:]:
            sums = sums + gram_ref[...]
        sums = jnp.sum(sums, axis=1, keepdims=True)
        gram = {(i, j): sums[i * count + j : i * count + j + 1] for i, j in pair_list(count)}
        for rep, coef in enumerate(merge_coefs(gram, count)):
            coef_ref[rep] = jnp.broadcast_to(coef, coef_ref.shape[1:])

    matrix = pl.program_id(0)
    block = pl.program_id(1) * block_rows
    coefs = [[coef_ref[rep_ref[0] ^ offset] for offset in offsets] for offsets in places]

    def step(index, _):
        rows = pl.ds(pl.multiple_of(index * lines, lines), lines)
        all_rows = pl.ds(pl.multiple_of(block + index * lines, lines), lines)
        for lane in range(0, hidden_width, 128):
            columns = pl.ds(lane, 128)
            merged = None
            for grads_ref, group in zip(grads_refs, coefs):
                for at, coef in enumerate(group):
                    part = grads_ref[at, matrix, all_rows, columns] * coef
                    merged = part if merged is None else merged + part
            first_new = (beta_first / first_fix) * first_ref[0, matrix, all_rows, columns] + (
                (1.0 - beta_first) / first_fix
            ) * merged
            second_new = (beta_second / second_fix) * second_ref[0, matrix, all_rows, columns] + (
                (1.0 - beta_second) / second_fix
            ) * (merged * merged)
            root = second_new * lax.rsqrt(second_new)
            step_ref[0, 0, rows, columns] = first_new / (root + adam_eps)
        return 0

    lax.fori_loop(0, block_rows // lines, step, 0, unroll=2)


def adasum_adam_many(rep, inputs, incoming, factors, first_moment, second_moment):
    count = len(inputs)
    half = inputs[0].shape[0] // 2
    grads = []
    for offset in range(count):
        (payload,) = factors[offset]
        gate_grad, up_grad = payload[:, : 2 * half]
        hidden = payload[:, 2 * half :].reshape(2 * half, -1)
        received = incoming[offset].reshape(2 * half, incoming.shape[3])
        grads.append(
            jnp.stack(
                [
                    contract_first(inputs[offset], gate_grad),
                    contract_first(inputs[offset], up_grad),
                    contract_first(received, hidden),
                ]
            )
        )
    grads = jnp.stack(grads)[rep[0] ^ jnp.arange(count)]
    flat = grads.reshape(count, -1)
    gram = lax.psum(jnp.matmul(flat, flat.T, precision=lax.Precision.HIGHEST), "replica")
    coefs = jnp.eye(count, dtype=jnp.float32)
    while coefs.shape[0] > 1:
        inner = jnp.matmul(
            jnp.matmul(coefs, gram, precision=lax.Precision.HIGHEST),
            coefs.T,
            precision=lax.Precision.HIGHEST,
        )
        norms = jnp.maximum(jnp.diagonal(inner), 0.0)
        norm_first, norm_second = norms[0::2], norms[1::2]
        bound = jnp.sqrt(norm_first) * jnp.sqrt(norm_second)
        cross = jnp.clip(jnp.diagonal(inner, offset=1)[0::2], -bound, bound)
        coef_first = 1.0 - cross / (2.0 * (norm_first + norm_eps))
        coef_second = 1.0 - cross / (2.0 * (norm_second + norm_eps))
        coefs = coef_first[:, None] * coefs[0::2] + coef_second[:, None] * coefs[1::2]
    merged = jnp.sum(coefs[0][:, None, None, None] * grads, axis=0)
    first_new = beta_first * first_moment[0] + (1.0 - beta_first) * merged
    second_new = beta_second * second_moment[0] + (1.0 - beta_second) * merged * merged
    return ((first_new / first_fix) / (jnp.sqrt(second_new / second_fix) + adam_eps))[None]


def adasum(rep, inputs, incoming, factors):
    count = len(inputs)
    seg_rows, hidden_width = incoming.shape[3], factors[0][0].shape[2]
    shape = jax.ShapeDtypeStruct
    groups = [[k for k in range(count) if k < 3], [k for k in range(count) if k == 3]]
    groups = [group for group in groups if group]
    grads, gram, first_gram, place = [], None, None, 0
    for group in groups:
        operands = [rep] if gram is None else [rep, gram, grads[0]]
        parts = [x for k in group for x in (inputs[k], factors[k])]
        operands += [incoming] + flatten(parts)
        more, gram = call(
            functools.partial(gram_kernel, count, group, [len(x) for x in parts], place),
            "gram_late" if place else "gram",
            operands,
            [SMEM] + [VMEM] * (len(operands) - 1),
            [
                shape((len(group), 3, seg_rows, hidden_width), jnp.float32),
                shape((max(8, count * count), 128), jnp.float32),
            ],
            cost=0 if place else 0,
        )
        first_gram = gram if first_gram is None else first_gram
        grads.append(more)
        place += len(group)
    return groups, grads, gram, first_gram


def adam(rep, groups, grads, gram, first_moment, second_moment, after):
    count = sum(len(group) for group in groups)
    seg_rows, hidden_width = first_moment.shape[2:]
    grams = [gram] + [from_peer(gram, k) for k in reversed(range(1, count))]
    tile = min(seg_rows, 256)
    moment_spec = pl.BlockSpec((1, 1, tile, hidden_width), lambda m, d: (0, m, d, 0))
    (adam_step,) = call(
        functools.partial(adam_kernel, count, groups),
        "adam",
        [rep, *grams, *grads, first_moment, second_moment],
        [SMEM] + [VMEM] * (len(grams) + len(grads) + 2),
        [jax.ShapeDtypeStruct(first_moment.shape, jnp.float32)],
        out_specs=[moment_spec],
        grid=(3, seg_rows // tile),
        scratch=[pltpu.VMEM((count, 16, 128), jnp.float32)],
        after=after,
    )
    return adam_step


def shards(
    weights, first_moment, second_moment, out_grads, routes, task_ids, task_weights, saved_inputs
):
    expert_count = lax.axis_size("expert")
    rep_count = lax.axis_size("replica")
    row_count = out_grads.shape[1]
    model_width = out_grads.shape[2]
    hidden_width = weights.shape[3]
    slot_count = saved_inputs.shape[2]
    capacity = slot_count // expert_count
    seg_rows = model_width // rep_count
    half = slot_count // 2
    offsets = range(rep_count)
    chips = expert_count // 2
    rep = lax.axis_index("replica").astype(jnp.int32).reshape(1)
    spot = lax.axis_index("expert").astype(jnp.int32).reshape(1)
    shape = jax.ShapeDtypeStruct

    block = shape((row_count + LABEL_ROWS, seg_rows), jnp.bfloat16)
    small = [routes[0].reshape(1, row_count), out_grads[0]]
    row_blocks = call(
        functools.partial(rows_kernel, expert_count),
        "rows",
        [rep, task_ids, task_weights, *small],
        [SMEM] * 3 + [pl.BlockSpec(x.shape, lambda i: (0, 0)) for x in small],
        [block for _ in offsets],
        grid=(1,),
        room=56 * MIB,
    )
    routed = exchange(row_blocks)

    inputs_home = saved_inputs[0, 0]
    pair = weights[0, :2]
    packed = rep_count == 4 and seg_rows == hidden_width
    if packed:
        payload = shape((2 * seg_rows + slot_count + half, seg_rows), jnp.bfloat16)
        to_one, to_two = call(
            payload_kernel,
            "payload",
            [rep, pair, inputs_home],
            [SMEM, VMEM, VMEM],
            [payload, payload],
            after=routed[1:],
        )
        from_two, from_one = from_peer(to_two, 2), from_peer(to_one, 1)
        projections = [(to_one,), (from_one,), (from_two,)]
        inputs = [(inputs_home,), (from_one,), (from_two,)]
    else:
        projections = [(x,) for x in exchange([pair] * rep_count)]
        pieces = [shape((slot_count, seg_rows), jnp.bfloat16) for _ in offsets]
        pieces = call(split_kernel, "split", [rep, inputs_home], [SMEM, VMEM], pieces)
        inputs = [(x,) for x in exchange(pieces)]

    part = shape((2, rep_count, capacity, seg_rows), jnp.bfloat16)
    placed = (
        call(
            functools.partial(place_kernel, rep_count, row_count),
            "place",
            [spot, *routed],
            [SMEM] + [VMEM] * len(routed),
            [part] * chips,
            scratch=[
                pltpu.VMEM((rep_count, expert_count, capacity, seg_rows), jnp.bfloat16)
            ],
        )
    )

    came = across_chips(placed)

    came = finish_spread(came)

    back_shape = (slot_count, hidden_width)
    incoming, *back = call(
        functools.partial(back_kernel, chips, len(came)),
        "back",
        [spot, weights[0, 2], *came],
        [SMEM] + [VMEM] * (1 + len(came)),
        [shape((rep_count, expert_count, capacity, seg_rows), jnp.bfloat16)]
        + [shape(back_shape, jnp.bfloat16 if k else jnp.float32) for k in offsets],
    )
    own_back = back[:1]
    back = exchange(back)
    if packed:
        passed = shape((seg_rows + half, seg_rows), jnp.bfloat16)
        first, second = call(
            pass_kernel,
            "pass",
            [from_two, from_one],
            [VMEM, VMEM],
            [passed, passed],
            after=own_back,
        )
        last = (from_peer(first, 1), from_peer(second, 2))
        projections.append(last)
        inputs.append(last)

    forward = None
    late = [3] if packed else []
    for name, group in (("forward", [k for k in offsets if k not in late]), ("rest", late)):
        if not group:
            continue
        operands = [rep, inputs_home] + ([] if forward is None else [forward])
        operands += flatten(projections[k] for k in group)
        lengths = [len(projections[k]) for k in group]
        (forward,) = call(
            functools.partial(forward_kernel, group, lengths, forward is not None),
            name,
            operands,
            [SMEM] + [VMEM] * (len(operands) - 1),
            [shape((2, slot_count, hidden_width), jnp.float32)],
            cost=0 if name == "rest" else 0,
        )

    (own_factors,) = call(
        factor_kernel,
        "factors",
        [forward, *back],
        [VMEM] * (1 + len(back)),
        [shape((2, slot_count + half, hidden_width), jnp.bfloat16)],
    )
    near_factors = gather_near(own_factors)

    operands = [rep, spot, own_factors] + flatten(projections)
    returning = across_chips(
        call(
            functools.partial(slot_kernel, [len(group) for group in projections]),
            "slots",
            operands,
            [SMEM] * 2 + [VMEM] * (len(operands) - 2),
            [shape((2, capacity, model_width), jnp.bfloat16)] * chips,
            scratch=[
                pltpu.VMEM((rep_count, expert_count, capacity, seg_rows), jnp.bfloat16)
            ],
        )
    )
    factors = gather_rest(near_factors, after=returning[:1])
    if rep_count <= 4:
        *merging, first_gram = adasum(rep, inputs, incoming, factors)
        returned = finish_spread(returning, [first_gram], pieces=2)
        unplace_after = merging[2:]
    else:
        returned, unplace_after = finish_spread(returning), ()
    (input_grads,) = call(
        unplace_kernel,
        "unplace",
        [spot, routed[0], *returned],
        [SMEM] + [VMEM] * (1 + len(returned)),
        [shape((1, row_count, model_width), jnp.bfloat16)],
        scratch=[pltpu.VMEM((expert_count, capacity, model_width), jnp.bfloat16)],
        after=unplace_after,
    )
    if rep_count <= 4:
        adam_step = adam(rep, *merging, first_moment, second_moment, ())
    else:
        adam_step = adasum_adam_many(
            rep, [x for (x,) in inputs], incoming, factors, first_moment, second_moment
        )
    return (input_grads, adam_step)


def solution(mesh):
    return jax.shard_map(
        shards,
        mesh=mesh,
        in_specs=(
            P("expert", None, "replica", None),
            P("expert", None, "replica", None),
            P("expert", None, "replica", None),
            P("replica", "expert", None),
            P("replica", "expert", None),
            P("replica", "expert"),
            P(),
            P("replica", "expert", None, None),
        ),
        out_specs=(P("replica", "expert", None), P("expert", None, "replica", None)),
        check_vma=False,
    )
```

```python
import functools

import jax
import jax.numpy as jnp
from jax import lax
from jax.experimental import pallas as pl
from jax.experimental.pallas import tpu as pltpu
from jax.sharding import PartitionSpec as P

beta_first = 0.9
beta_second = 0.95
adam_eps = 1e-08
norm_eps = 1e-06
first_fix = 1.0 - (0.9**50) ** 2
second_fix = 1.0 - (0.95**50) ** 2
MIB = 1024 * 1024
LABEL_ROWS = 16


def contract_first(left, right):
    return lax.dot_general(
        left, right, (((0,), (0,)), ((), ())), preferred_element_type=jnp.float32
    )


def contract_last(left, right):
    return lax.dot_general(
        left, right, (((1,), (1,)), ((), ())), preferred_element_type=jnp.float32
    )


def multiply(left, right):
    return jnp.dot(left, right, preferred_element_type=jnp.float32)


def from_peer(array, offset):
    count = lax.axis_size("replica")
    return lax.ppermute(array, "replica", [(i, i ^ offset) for i in range(count)])


def across_chips(parts):
    count = lax.axis_size("expert")
    return [parts[0]] + [
        lax.ppermute(part, "expert", [(i, i ^ 2 * k) for i in range(count)])
        for k, part in enumerate(parts)
        if k
    ]


def pick_kernel(chips, *refs):
    block_refs = [ref.at[k] for ref in refs[chips:] for k in range(ref.shape[0])]
    for part_ref, block_ref in zip(refs[:chips], block_refs):
        block_ref[...] = part_ref[1]


def finish_spread(came, after=(), pieces=1):
    count = lax.axis_size("expert")
    chips = len(came)
    block = jax.ShapeDtypeStruct((chips // pieces,) + came[0].shape[1:], came[0].dtype)
    others = call(
        functools.partial(pick_kernel, chips),
        "pick",
        came,
        [VMEM] * chips,
        [block] * pieces,
        after=after,
    )
    swapped = [lax.ppermute(x, "expert", [(i, i ^ 1) for i in range(count)]) for x in others]
    return [*came, *swapped]


def spread_block(chips, refs, offset):
    if offset % 2 == 0:
        return refs[offset // 2].at[0]
    blocks = [ref.at[k] for ref in refs[chips:] for k in range(ref.shape[0])]
    return blocks[offset // 2]


def exchange(parts):
    return [parts[0]] + [from_peer(part, k) for k, part in enumerate(parts) if k]


def split_kernel(rep_ref, matrix_ref, *out_refs):
    for offset, out_ref in enumerate(out_refs):
        out_ref[...] = matrix_ref[:, segment(rep_ref, offset, out_ref.shape[1])]


def payload_kernel(rep_ref, pair_ref, inputs_ref, *out_refs):
    seg_rows = pair_ref.shape[1]
    slot_count = inputs_ref.shape[0]
    half = slot_count // 2
    for part, out_ref in enumerate(out_refs):
        out_ref[pl.ds(0, seg_rows), :] = pair_ref[0]
        out_ref[pl.ds(seg_rows, seg_rows), :] = pair_ref[1]
        columns = segment(rep_ref, part + 1, seg_rows)
        out_ref[pl.ds(2 * seg_rows, slot_count), :] = inputs_ref[:, columns]
        columns = segment(rep_ref, 3, seg_rows)
        out_ref[pl.ds(2 * seg_rows + slot_count, half), :] = inputs_ref[
            pl.ds(part * half, half), columns
        ]


def pass_kernel(from_two_ref, from_one_ref, *out_refs):
    for part, (near_ref, out_ref) in enumerate(zip((from_two_ref, from_one_ref), out_refs)):
        seg_rows = near_ref.shape[1]
        half = out_ref.shape[0] - seg_rows
        out_ref[pl.ds(0, seg_rows), :] = near_ref[pl.ds(part * seg_rows, seg_rows), :]
        out_ref[pl.ds(seg_rows, half), :] = near_ref[pl.ds(near_ref.shape[0] - half, half), :]


def projection_rows(refs):
    if len(refs) == 1 and len(refs[0].shape) == 3:
        return refs[0].at[0], refs[0].at[1]
    seg_rows = refs[0].shape[1]
    start = 0 if len(refs) == 2 else seg_rows
    return refs[0].at[pl.ds(0, seg_rows)], refs[-1].at[pl.ds(start, seg_rows)]


def input_rows(rep_ref, refs, slot_count, seg_rows):
    if len(refs) == 2:
        rows = pl.ds(seg_rows, slot_count // 2)
        return jnp.concatenate([refs[1][rows], refs[0][rows]], axis=0)
    (ref,) = refs
    if ref.shape[0] > slot_count:
        return ref[pl.ds(2 * seg_rows, slot_count), :]
    return ref[...] if ref.shape[1] == seg_rows else ref[:, segment(rep_ref, 0, seg_rows)]


def cut_kernel(from_two_ref, from_one_ref, first_ref, second_ref):
    first_ref[...] = from_two_ref[0]
    second_ref[...] = from_one_ref[1]


def gather_near(payload):
    count = lax.axis_size("replica")
    if count != 4:
        return exchange([payload] * count)
    from_two = from_peer(payload, 2)
    return [payload, from_peer(payload, 1), from_two]


def gather_rest(near, after):
    whole = [(part,) for part in near]
    if lax.axis_size("replica") != 4:
        return whole
    half = jax.ShapeDtypeStruct(near[0].shape[1:], near[0].dtype)
    first, second = call(
        cut_kernel, "cut", [near[2], near[1]], [VMEM, VMEM], [half, half], after=after
    )
    return whole + [(from_peer(first, 1), from_peer(second, 2))]


def halves(refs):
    return refs if len(refs) == 2 else (refs[0].at[0], refs[0].at[1])


def regroup(refs, lengths):
    groups, at = [], 0
    for length in lengths:
        groups.append(refs[at : at + length])
        at += length
    return groups


def flatten(groups):
    return [array for group in groups for array in group]


def pair_list(count):
    return [(i, j) for i in range(count) for j in range(i, count)]


SMEM = pl.BlockSpec(memory_space=pltpu.SMEM)
VMEM = pl.BlockSpec(memory_space=pltpu.VMEM)


def call(
    kernel, name, operands, specs, outs, out_specs=None, grid=(), scratch=(), after=(), cost=0, room=0
):
    size = sum(x.size * x.dtype.itemsize for x in list(operands) + list(outs))
    taken = len(operands)

    def body(*refs):
        kernel(*refs[:taken], *refs[taken + len(after) :])

    return pl.pallas_call(
        body,
        grid=grid,
        in_specs=list(specs) + [VMEM] * len(after),
        out_specs=out_specs if out_specs is not None else [VMEM for _ in outs],
        out_shape=outs,
        scratch_shapes=list(scratch),
        compiler_params=pltpu.CompilerParams(
            dimension_semantics=("arbitrary",) * len(grid),
            vmem_limit_bytes=max(room, min(56 * MIB, size + 8 * MIB)),
        ),
        cost_estimate=pl.CostEstimate(flops=0, bytes_accessed=cost, transcendentals=0),
        name=name,
    )(*operands, *after)


def segment(rep_ref, offset, width):
    return pl.ds(pl.multiple_of((rep_ref[0] ^ offset) * width, width), width)


def rows_kernel(expert_count, rep_ref, ids_ref, task_ref, row_ref, grads_ref, *out_refs):
    row_count = grads_ref.shape[0]
    seg_rows = out_refs[0].shape[1]
    block_count = ids_ref.shape[1]
    block_rows = row_count // block_count
    square = (row_count, row_count)
    earlier = lax.broadcasted_iota(jnp.int32, square, 0) < lax.broadcasted_iota(
        jnp.int32, square, 1
    )
    experts = lax.broadcasted_iota(jnp.int32, (expert_count, row_count), 0)
    chosen = jnp.where(experts == row_ref[...], 1.0, 0.0)
    before = multiply(
        chosen.astype(jnp.bfloat16), jnp.where(earlier, 1.0, 0.0).astype(jnp.bfloat16)
    )
    rank = jnp.sum(chosen * before, axis=0, keepdims=True)
    line = lax.broadcasted_iota(jnp.int32, (LABEL_ROWS, row_count), 0)
    labels = jnp.where(line == 0, row_ref[...].astype(jnp.float32), 0.0)
    labels = jnp.where(line == 1, rank, labels).astype(jnp.bfloat16)
    for offset, out_ref in enumerate(out_refs):
        columns = segment(rep_ref, offset, seg_rows)
        for block in range(block_count):
            rows = pl.ds(block * block_rows, block_rows)
            weight = task_ref[ids_ref[0, block]]
            out_ref[rows, :] = (grads_ref[rows, columns].astype(jnp.float32) * weight).astype(
                jnp.bfloat16
            )
        if row_count < seg_rows:
            out_ref[pl.ds(row_count, LABEL_ROWS), :] = jnp.zeros(
                (LABEL_ROWS, seg_rows), jnp.bfloat16
            )
        out_ref[pl.ds(row_count, LABEL_ROWS), pl.ds(0, row_count)] = labels


def one_hot(block_ref, row_count, slot_count, capacity):
    labels = block_ref[pl.ds(row_count, LABEL_ROWS), pl.ds(0, row_count)].astype(jnp.float32)
    slot = (labels[0:1] * capacity + labels[1:2]).astype(jnp.int32)
    places = lax.broadcasted_iota(jnp.int32, (slot_count, row_count), 0)
    return jnp.where(places == slot, 1.0, 0.0).astype(jnp.bfloat16)


def place_kernel(count, row_count, spot_ref, *refs):
    block_refs, out_refs, placed_ref = refs[:count], refs[count:-1], refs[-1]
    _, expert_count, capacity, seg_rows = placed_ref.shape
    slot_count = expert_count * capacity
    for offset, block_ref in enumerate(block_refs):
        placing = one_hot(block_ref, row_count, slot_count, capacity)
        placed = multiply(placing, block_ref[pl.ds(0, row_count), :])
        placed = placed.reshape(expert_count, capacity, seg_rows)
        placed_ref[offset] = placed.astype(jnp.bfloat16)
        for expert in range(expert_count):
            out_refs[expert // 2][expert % 2, offset] = placed_ref[offset, spot_ref[0] ^ expert]


def unplace_kernel(spot_ref, block_ref, *refs):
    returned_refs, out_ref, slots_ref = refs[:-2], refs[-2], refs[-1]
    expert_count, capacity, _ = slots_ref.shape
    slot_count = expert_count * capacity
    row_count = out_ref.shape[1]
    placing = one_hot(block_ref, row_count, slot_count, capacity)
    for expert in range(expert_count):
        block_ref = spread_block(expert_count // 2, returned_refs, expert)
        slots_ref[spot_ref[0] ^ expert] = block_ref[...]
    out_ref[0] = contract_first(placing, flat_rows(slots_ref[...])).astype(jnp.bfloat16)


def flat_rows(blocks):
    rows = blocks.shape[0] * blocks.shape[1]
    if blocks.shape[1] % 16:
        wide = blocks.astype(jnp.float32).reshape(rows, blocks.shape[2])
        return wide.astype(jnp.bfloat16)
    return blocks.reshape(rows, blocks.shape[2])


def back_kernel(chips, arrays, spot_ref, weight_ref, *refs):
    came_refs, incoming_ref, out_refs = refs[:arrays], refs[arrays], refs[arrays + 1 :]
    for offset, out_ref in enumerate(out_refs):
        for expert in range(2 * chips):
            block_ref = spread_block(chips, came_refs, expert)
            incoming_ref[offset, spot_ref[0] ^ expert] = block_ref[offset]
        rows = flat_rows(incoming_ref[offset])
        out_ref[...] = multiply(rows, weight_ref[...]).astype(out_ref.dtype)


def forward_kernel(offsets, lengths, has_start, rep_ref, inputs_ref, *refs):
    out_ref = refs[-1]
    weight_refs = refs[:-1]
    gate = up = None
    if has_start:
        gate, up = weight_refs[0][0], weight_refs[0][1]
        weight_refs = weight_refs[1:]
    for offset, group in zip(offsets, regroup(weight_refs, lengths)):
        gate_ref, up_ref = projection_rows(group)
        rows = inputs_ref[:, segment(rep_ref, offset, gate_ref.shape[0])]
        gate_part, up_part = multiply(rows, gate_ref[...]), multiply(rows, up_ref[...])
        gate = gate_part if gate is None else gate + gate_part
        up = up_part if up is None else up + up_part
    out_ref[0] = gate
    out_ref[1] = up


def factor_kernel(forward_ref, *refs):
    back_refs, out_ref = refs[:-1], refs[-1]
    slot_count = forward_ref.shape[1]
    half = slot_count // 2
    hidden_grad = back_refs[0][...]
    for back_ref in back_refs[1:]:
        hidden_grad = hidden_grad + back_ref[...].astype(jnp.float32)
    gate_pre, up_pre = forward_ref[0], forward_ref[1]
    sigmoid_gate = jax.nn.sigmoid(gate_pre)
    gate_act = gate_pre * sigmoid_gate
    hidden = (gate_act * up_pre).astype(jnp.bfloat16)
    gate_grad = hidden_grad * up_pre * sigmoid_gate * (1.0 + gate_pre * (1.0 - sigmoid_gate))
    out_ref[0, pl.ds(0, slot_count)] = gate_grad.astype(jnp.bfloat16)
    out_ref[1, pl.ds(0, slot_count)] = (hidden_grad * gate_act).astype(jnp.bfloat16)
    for part in range(2):
        out_ref[part, pl.ds(slot_count, half)] = hidden[part * half : (part + 1) * half]


def slot_kernel(lengths, rep_ref, spot_ref, factor_ref, *refs):
    chips = refs[-1].shape[1] // 2
    weight_refs, out_refs, slots_ref = refs[: -chips - 1], refs[-chips - 1 : -1], refs[-1]
    _, expert_count, capacity, seg_rows = slots_ref.shape
    rows = pl.ds(0, expert_count * capacity)
    gate_grad, up_grad = factor_ref[0, rows], factor_ref[1, rows]
    for offset, group in enumerate(regroup(weight_refs, lengths)):
        gate_ref, up_ref = projection_rows(group)
        total = contract_last(gate_grad, gate_ref[...]) + contract_last(up_grad, up_ref[...])
        total = total.reshape(expert_count, capacity, seg_rows)
        slots_ref[offset] = total.astype(jnp.bfloat16)
        columns = segment(rep_ref, offset, seg_rows)
        for expert in range(expert_count):
            out_ref = out_refs[expert // 2]
            out_ref[expert % 2, :, columns] = slots_ref[offset, spot_ref[0] ^ expert]


def gram_kernel(count, offsets, lengths, place, rep_ref, *refs):
    if place:
        before_ref, earlier_ref, refs = refs[0], refs[1], refs[2:]
    incoming_ref, operand_refs, grads_ref, gram_ref = refs[0], refs[1:-2], refs[-2], refs[-1]
    middle = incoming_ref.shape[1] // 2
    seg_rows, hidden_width = grads_ref.shape[2:]
    slot_count = incoming_ref.shape[1] * incoming_ref.shape[2]
    groups = regroup(operand_refs, lengths)
    known = list(range(place)) + list(offsets)
    pairs = [(i, j) for i, j in pair_list(len(known)) if j >= place]
    lines = 8
    tile = min(seg_rows, 256)
    sums = [jnp.zeros((lines, hidden_width), jnp.float32) for _ in pairs]
    operands = []
    for at, offset in enumerate(offsets):
        input_refs, factor_refs = groups[2 * at : 2 * at + 2]
        rest = pl.ds(slot_count, slot_count // 2)
        columns = input_rows(rep_ref, input_refs, slot_count, seg_rows)
        gate_ref, up_ref = (ref.at[pl.ds(0, slot_count)] for ref in halves(factor_refs))
        first_ref, second_ref = (ref.at[rest] for ref in halves(factor_refs))
        upper = flat_rows(incoming_ref[offset, :middle])
        lower = flat_rows(incoming_ref[offset, middle:])
        operands.append(
            [
                [(columns, gate_ref)],
                [(columns, up_ref)],
                [(upper, first_ref), (lower, second_ref)],
            ]
        )
    for matrix in range(3):
        for start in range(0, seg_rows, tile):
            rows = pl.ds(start, tile)
            blocks = [earlier_ref[at, matrix, rows] for at in range(place)]
            for at in range(len(offsets)):
                block = None
                for left, right_ref in operands[at][matrix]:
                    part = contract_first(left[:, start : start + tile], right_ref[...])
                    block = part if block is None else block + part
                grads_ref[at, matrix, rows] = block
                blocks.append(block)
            for place_of, (i, j) in enumerate(pairs):
                products = (blocks[i] * blocks[j]).reshape(tile // lines, lines, hidden_width)
                sums[place_of] = sums[place_of] + jnp.sum(products, axis=0)
    gram_ref[...] = before_ref[...] if place else jnp.zeros_like(gram_ref)
    for total, (i, j) in zip(sums, pairs):
        total = jnp.sum(total, axis=0, keepdims=True)
        part = total[:, :128]
        for lane in range(128, hidden_width, 128):
            part = part + total[:, lane : lane + 128]
        first, second = rep_ref[0] ^ known[i], rep_ref[0] ^ known[j]
        row = jnp.minimum(first, second) * count + jnp.maximum(first, second)
        gram_ref[pl.ds(row, 1), :] = part


def merge_coefs(gram, count):
    vectors = [{rep: None} for rep in range(count)]

    def term(coef, value):
        return value if coef is None else coef * value

    def inner(left, right):
        total = None
        for i, left_coef in left.items():
            for j, right_coef in right.items():
                value = term(left_coef, term(right_coef, gram[min(i, j), max(i, j)]))
                total = value if total is None else total + value
        return total

    while len(vectors) > 1:
        merged = []
        for first, second in zip(vectors[0::2], vectors[1::2]):
            norm_first = jnp.maximum(inner(first, first), 0.0)
            norm_second = jnp.maximum(inner(second, second), 0.0)
            bound = jnp.sqrt(norm_first) * jnp.sqrt(norm_second)
            cross = jnp.minimum(jnp.maximum(inner(first, second), -bound), bound)
            coef_first = 1.0 - cross / (2.0 * (norm_first + norm_eps))
            coef_second = 1.0 - cross / (2.0 * (norm_second + norm_eps))
            joined = {rep: term(coef, coef_first) for rep, coef in first.items()}
            joined.update({rep: term(coef, coef_second) for rep, coef in second.items()})
            merged.append(joined)
        vectors = merged
    return [vectors[0][rep] for rep in range(count)]


def adam_kernel(count, places, rep_ref, *refs):
    gram_refs, grads_refs = refs[:count], refs[count : count + len(places)]
    first_ref, second_ref, step_ref, coef_ref = refs[count + len(places) :]
    block_rows, hidden_width = step_ref.shape[2:]
    lines = coef_ref.shape[1]

    @pl.when((pl.program_id(0) == 0) & (pl.program_id(1) == 0))
    def _():
        sums = gram_refs[0][...]
        for gram_ref in gram_refs[1:]:
            sums = sums + gram_ref[...]
        sums = jnp.sum(sums, axis=1, keepdims=True)
        gram = {(i, j): sums[i * count + j : i * count + j + 1] for i, j in pair_list(count)}
        for rep, coef in enumerate(merge_coefs(gram, count)):
            coef_ref[rep] = jnp.broadcast_to(coef, coef_ref.shape[1:])

    matrix = pl.program_id(0)
    block = pl.program_id(1) * block_rows
    coefs = [[coef_ref[rep_ref[0] ^ offset] for offset in offsets] for offsets in places]

    def step(index, _):
        rows = pl.ds(pl.multiple_of(index * lines, lines), lines)
        all_rows = pl.ds(pl.multiple_of(block + index * lines, lines), lines)
        for lane in range(0, hidden_width, 128):
            columns = pl.ds(lane, 128)
            merged = None
            for grads_ref, group in zip(grads_refs, coefs):
                for at, coef in enumerate(group):
                    part = grads_ref[at, matrix, all_rows, columns] * coef
                    merged = part if merged is None else merged + part
            first_new = (beta_first / first_fix) * first_ref[0, matrix, all_rows, columns] + (
                (1.0 - beta_first) / first_fix
            ) * merged
            second_new = (beta_second / second_fix) * second_ref[0, matrix, all_rows, columns] + (
                (1.0 - beta_second) / second_fix
            ) * (merged * merged)
            root = second_new * lax.rsqrt(second_new)
            step_ref[0, 0, rows, columns] = first_new / (root + adam_eps)
        return 0

    lax.fori_loop(0, block_rows // lines, step, 0, unroll=4)


def adasum_adam_many(rep, inputs, incoming, factors, first_moment, second_moment):
    count = len(inputs)
    half = inputs[0].shape[0] // 2
    grads = []
    for offset in range(count):
        (payload,) = factors[offset]
        gate_grad, up_grad = payload[:, : 2 * half]
        hidden = payload[:, 2 * half :].reshape(2 * half, -1)
        received = incoming[offset].reshape(2 * half, incoming.shape[3])
        grads.append(
            jnp.stack(
                [
                    contract_first(inputs[offset], gate_grad),
                    contract_first(inputs[offset], up_grad),
                    contract_first(received, hidden),
                ]
            )
        )
    grads = jnp.stack(grads)[rep[0] ^ jnp.arange(count)]
    flat = grads.reshape(count, -1)
    gram = lax.psum(jnp.matmul(flat, flat.T, precision=lax.Precision.HIGHEST), "replica")
    coefs = jnp.eye(count, dtype=jnp.float32)
    while coefs.shape[0] > 1:
        inner = jnp.matmul(
            jnp.matmul(coefs, gram, precision=lax.Precision.HIGHEST),
            coefs.T,
            precision=lax.Precision.HIGHEST,
        )
        norms = jnp.maximum(jnp.diagonal(inner), 0.0)
        norm_first, norm_second = norms[0::2], norms[1::2]
        bound = jnp.sqrt(norm_first) * jnp.sqrt(norm_second)
        cross = jnp.clip(jnp.diagonal(inner, offset=1)[0::2], -bound, bound)
        coef_first = 1.0 - cross / (2.0 * (norm_first + norm_eps))
        coef_second = 1.0 - cross / (2.0 * (norm_second + norm_eps))
        coefs = coef_first[:, None] * coefs[0::2] + coef_second[:, None] * coefs[1::2]
    merged = jnp.sum(coefs[0][:, None, None, None] * grads, axis=0)
    first_new = beta_first * first_moment[0] + (1.0 - beta_first) * merged
    second_new = beta_second * second_moment[0] + (1.0 - beta_second) * merged * merged
    return ((first_new / first_fix) / (jnp.sqrt(second_new / second_fix) + adam_eps))[None]


def adasum(rep, inputs, incoming, factors):
    count = len(inputs)
    seg_rows, hidden_width = incoming.shape[3], factors[0][0].shape[2]
    shape = jax.ShapeDtypeStruct
    groups = [[k for k in range(count) if k < 3], [k for k in range(count) if k == 3]]
    groups = [group for group in groups if group]
    grads, gram, first_gram, place = [], None, None, 0
    for group in groups:
        operands = [rep] if gram is None else [rep, gram, grads[0]]
        parts = [x for k in group for x in (inputs[k], factors[k])]
        operands += [incoming] + flatten(parts)
        more, gram = call(
            functools.partial(gram_kernel, count, group, [len(x) for x in parts], place),
            "gram_late" if place else "gram",
            operands,
            [SMEM] + [VMEM] * (len(operands) - 1),
            [
                shape((len(group), 3, seg_rows, hidden_width), jnp.float32),
                shape((max(8, count * count), 128), jnp.float32),
            ],
            cost=0 if place else 0,
        )
        first_gram = gram if first_gram is None else first_gram
        grads.append(more)
        place += len(group)
    return groups, grads, gram, first_gram


def adam(rep, groups, grads, gram, first_moment, second_moment, after):
    count = sum(len(group) for group in groups)
    seg_rows, hidden_width = first_moment.shape[2:]
    grams = [gram] + [from_peer(gram, k) for k in reversed(range(1, count))]
    tile = min(seg_rows, 256)
    moment_spec = pl.BlockSpec((1, 1, tile, hidden_width), lambda m, d: (0, m, d, 0))
    (adam_step,) = call(
        functools.partial(adam_kernel, count, groups),
        "adam",
        [rep, *grams, *grads, first_moment, second_moment],
        [SMEM] + [VMEM] * (len(grams) + len(grads) + 2),
        [jax.ShapeDtypeStruct(first_moment.shape, jnp.float32)],
        out_specs=[moment_spec],
        grid=(3, seg_rows // tile),
        scratch=[pltpu.VMEM((count, 16, 128), jnp.float32)],
        after=after,
    )
    return adam_step


def shards(
    weights, first_moment, second_moment, out_grads, routes, task_ids, task_weights, saved_inputs
):
    expert_count = lax.axis_size("expert")
    rep_count = lax.axis_size("replica")
    row_count = out_grads.shape[1]
    model_width = out_grads.shape[2]
    hidden_width = weights.shape[3]
    slot_count = saved_inputs.shape[2]
    capacity = slot_count // expert_count
    seg_rows = model_width // rep_count
    half = slot_count // 2
    offsets = range(rep_count)
    chips = expert_count // 2
    rep = lax.axis_index("replica").astype(jnp.int32).reshape(1)
    spot = lax.axis_index("expert").astype(jnp.int32).reshape(1)
    shape = jax.ShapeDtypeStruct

    block = shape((row_count + LABEL_ROWS, seg_rows), jnp.bfloat16)
    small = [routes[0].reshape(1, row_count), out_grads[0]]
    row_blocks = call(
        functools.partial(rows_kernel, expert_count),
        "rows",
        [rep, task_ids, task_weights, *small],
        [SMEM] * 3 + [pl.BlockSpec(x.shape, lambda i: (0, 0)) for x in small],
        [block for _ in offsets],
        grid=(1,),
        room=56 * MIB,
    )
    routed = exchange(row_blocks)

    inputs_home = saved_inputs[0, 0]
    pair = weights[0, :2]
    packed = rep_count == 4 and seg_rows == hidden_width
    if packed:
        payload = shape((2 * seg_rows + slot_count + half, seg_rows), jnp.bfloat16)
        to_one, to_two = call(
            payload_kernel,
            "payload",
            [jnp.concatenate([rep, spot]), pair, inputs_home],
            [SMEM, VMEM, VMEM],
            [payload, payload],
            after=routed[1:],
        )
        from_two, from_one = from_peer(to_two, 2), from_peer(to_one, 1)
        projections = [(pair,), (from_one,), (from_two,)]
        inputs = [(inputs_home,), (from_one,), (from_two,)]
    else:
        projections = [(x,) for x in exchange([pair] * rep_count)]
        pieces = [shape((slot_count, seg_rows), jnp.bfloat16) for _ in offsets]
        pieces = call(split_kernel, "split", [rep, inputs_home], [SMEM, VMEM], pieces)
        inputs = [(x,) for x in exchange(pieces)]

    part = shape((2, rep_count, capacity, seg_rows), jnp.bfloat16)
    placed = (
        call(
            functools.partial(place_kernel, rep_count, row_count),
            "place",
            [spot, *routed],
            [SMEM] + [VMEM] * len(routed),
            [part] * chips,
            scratch=[
                pltpu.VMEM((rep_count, expert_count, capacity, seg_rows), jnp.bfloat16)
            ],
        )
    )

    came = across_chips(placed)

    came = finish_spread(came)

    back_shape = (slot_count, hidden_width)
    incoming, *back = call(
        functools.partial(back_kernel, chips, len(came)),
        "back",
        [spot, weights[0, 2], *came],
        [SMEM] + [VMEM] * (1 + len(came)),
        [shape((rep_count, expert_count, capacity, seg_rows), jnp.bfloat16)]
        + [shape(back_shape, jnp.bfloat16 if k else jnp.float32) for k in offsets],
    )
    own_back = back[:1]
    back = exchange(back)
    if packed:
        passed = shape((seg_rows + half, seg_rows), jnp.bfloat16)
        first, second = call(
            pass_kernel,
            "pass",
            [from_two, from_one],
            [VMEM, VMEM],
            [passed, passed],
            after=own_back,
        )
        last = (from_peer(first, 1), from_peer(second, 2))
        projections.append(last)
        inputs.append(last)

    forward = None
    late = [3] if packed else []
    for name, group in (("forward", [k for k in offsets if k not in late]), ("rest", late)):
        if not group:
            continue
        operands = [rep, inputs_home] + ([] if forward is None else [forward])
        operands += flatten(projections[k] for k in group)
        lengths = [len(projections[k]) for k in group]
        (forward,) = call(
            functools.partial(forward_kernel, group, lengths, forward is not None),
            name,
            operands,
            [SMEM] + [VMEM] * (len(operands) - 1),
            [shape((2, slot_count, hidden_width), jnp.float32)],
            cost=0 if name == "rest" else 0,
        )

    (own_factors,) = call(
        factor_kernel,
        "factors",
        [forward, *back],
        [VMEM] * (1 + len(back)),
        [shape((2, slot_count + half, hidden_width), jnp.bfloat16)],
    )
    near_factors = gather_near(own_factors)

    operands = [rep, spot, own_factors] + flatten(projections)
    returning = across_chips(
        call(
            functools.partial(slot_kernel, [len(group) for group in projections]),
            "slots",
            operands,
            [SMEM] * 2 + [VMEM] * (len(operands) - 2),
            [shape((2, capacity, model_width), jnp.bfloat16)] * chips,
            scratch=[
                pltpu.VMEM((rep_count, expert_count, capacity, seg_rows), jnp.bfloat16)
            ],
        )
    )
    factors = gather_rest(near_factors, after=returning[:1])
    if rep_count <= 4:
        *merging, first_gram = adasum(rep, inputs, incoming, factors)
        returned = finish_spread(returning, [first_gram], pieces=2)
        unplace_after = merging[2:]
    else:
        returned, unplace_after = finish_spread(returning), ()
    (input_grads,) = call(
        unplace_kernel,
        "unplace",
        [spot, routed[0], *returned],
        [SMEM] + [VMEM] * (1 + len(returned)),
        [shape((1, row_count, model_width), jnp.bfloat16)],
        scratch=[pltpu.VMEM((expert_count, capacity, model_width), jnp.bfloat16)],
        after=unplace_after,
    )
    if rep_count <= 4:
        adam_step = adam(rep, *merging, first_moment, second_moment, ())
    else:
        adam_step = adasum_adam_many(
            rep, [x for (x,) in inputs], incoming, factors, first_moment, second_moment
        )
    return (input_grads, adam_step)


def solution(mesh):
    return jax.shard_map(
        shards,
        mesh=mesh,
        in_specs=(
            P("expert", None, "replica", None),
            P("expert", None, "replica", None),
            P("expert", None, "replica", None),
            P("replica", "expert", None),
            P("replica", "expert", None),
            P("replica", "expert"),
            P(),
            P("replica", "expert", None, None),
        ),
        out_specs=(P("replica", "expert", None), P("expert", None, "replica", None)),
        check_vma=False,
    )
```

```python
import functools

import jax
import jax.numpy as jnp
from jax import lax
from jax.experimental import pallas as pl
from jax.experimental.pallas import tpu as pltpu
from jax.sharding import PartitionSpec as P

beta_first = 0.9
beta_second = 0.95
adam_eps = 1e-08
norm_eps = 1e-06
first_fix = 1.0 - (0.9**50) ** 2
second_fix = 1.0 - (0.95**50) ** 2
MIB = 1024 * 1024
LABEL_ROWS = 16


def contract_first(left, right):
    return lax.dot_general(
        left, right, (((0,), (0,)), ((), ())), preferred_element_type=jnp.float32
    )


def contract_last(left, right):
    return lax.dot_general(
        left, right, (((1,), (1,)), ((), ())), preferred_element_type=jnp.float32
    )


def multiply(left, right):
    return jnp.dot(left, right, preferred_element_type=jnp.float32)


def from_peer(array, offset):
    count = lax.axis_size("replica")
    return lax.ppermute(array, "replica", [(i, i ^ offset) for i in range(count)])


def across_chips(parts):
    count = lax.axis_size("expert")
    return [parts[0]] + [
        lax.ppermute(part, "expert", [(i, i ^ 2 * k) for i in range(count)])
        for k, part in enumerate(parts)
        if k
    ]


def pick_kernel(chips, *refs):
    block_refs = [ref.at[k] for ref in refs[chips:] for k in range(ref.shape[0])]
    for part_ref, block_ref in zip(refs[:chips], block_refs):
        block_ref[...] = part_ref[1]


def finish_spread(came, after=(), pieces=1):
    count = lax.axis_size("expert")
    chips = len(came)
    block = jax.ShapeDtypeStruct((chips // pieces,) + came[0].shape[1:], came[0].dtype)
    others = call(
        functools.partial(pick_kernel, chips),
        "pick",
        came,
        [VMEM] * chips,
        [block] * pieces,
        after=after,
    )
    swapped = [lax.ppermute(x, "expert", [(i, i ^ 1) for i in range(count)]) for x in others]
    return [*came, *swapped]


def spread_block(chips, refs, offset):
    if offset % 2 == 0:
        return refs[offset // 2].at[0]
    blocks = [ref.at[k] for ref in refs[chips:] for k in range(ref.shape[0])]
    return blocks[offset // 2]


def exchange(parts):
    return [parts[0]] + [from_peer(part, k) for k, part in enumerate(parts) if k]


def split_kernel(rep_ref, matrix_ref, *out_refs):
    for offset, out_ref in enumerate(out_refs):
        out_ref[...] = matrix_ref[:, segment(rep_ref, offset, out_ref.shape[1])]


def payload_kernel(rep_ref, pair_ref, inputs_ref, *out_refs):
    seg_rows = pair_ref.shape[1]
    slot_count = inputs_ref.shape[0]
    half = slot_count // 2
    for part, out_ref in enumerate(out_refs):
        out_ref[pl.ds(0, seg_rows), :] = pair_ref[0]
        out_ref[pl.ds(seg_rows, seg_rows), :] = pair_ref[1]
        columns = segment(rep_ref, part + 1, seg_rows)
        out_ref[pl.ds(2 * seg_rows, slot_count), :] = inputs_ref[:, columns]
        columns = segment(rep_ref, 3, seg_rows)
        out_ref[pl.ds(2 * seg_rows + slot_count, half), :] = inputs_ref[
            pl.ds(part * half, half), columns
        ]


def pass_kernel(from_two_ref, from_one_ref, first_ref, second_ref):
    seg_rows = first_ref.shape[1]
    half = (first_ref.shape[0] + second_ref.shape[0]) // 2 - seg_rows
    split = first_ref.shape[0] - half
    tail = pl.ds(from_one_ref.shape[0] - half, half)
    first_ref[pl.ds(0, split), :] = from_two_ref[pl.ds(0, split), :]
    first_ref[pl.ds(split, half), :] = from_two_ref[tail, :]
    rest = 2 * seg_rows - split
    second_ref[pl.ds(0, rest), :] = from_one_ref[pl.ds(split, rest), :]
    second_ref[pl.ds(rest, half), :] = from_one_ref[tail, :]


def projection_rows(refs):
    seg_rows = refs[0].shape[-1]
    if len(refs) == 1 and len(refs[0].shape) == 3:
        return refs[0][0], refs[0][1]
    if len(refs) == 1:
        return refs[0][pl.ds(0, seg_rows), :], refs[0][pl.ds(seg_rows, seg_rows), :]
    first_ref, second_ref = refs
    half = (first_ref.shape[0] + second_ref.shape[0]) // 2 - seg_rows
    split = first_ref.shape[0] - half
    rest = seg_rows - split
    gate = jnp.concatenate([first_ref[pl.ds(0, split), :], second_ref[pl.ds(0, rest), :]], axis=0)
    return gate, second_ref[pl.ds(rest, seg_rows), :]


def input_rows(rep_ref, refs, slot_count, seg_rows):
    if len(refs) == 2:
        half = slot_count // 2
        tails = [ref[pl.ds(ref.shape[0] - half, half), :] for ref in (refs[1], refs[0])]
        return jnp.concatenate(tails, axis=0)
    (ref,) = refs
    if ref.shape[0] > slot_count:
        return ref[pl.ds(2 * seg_rows, slot_count), :]
    return ref[...] if ref.shape[1] == seg_rows else ref[:, segment(rep_ref, 0, seg_rows)]


def cut_kernel(from_two_ref, from_one_ref, first_ref, second_ref):
    rows = first_ref.shape[0]
    first_ref[...] = from_two_ref[pl.ds(0, rows), :]
    second_ref[...] = from_one_ref[pl.ds(rows, second_ref.shape[0]), :]


def gather_near(payload):
    count = lax.axis_size("replica")
    if count != 4:
        return exchange([payload] * count)
    from_two = from_peer(payload, 2)
    return [payload, from_peer(payload, 1), from_two]


def gather_rest(near, after):
    whole = [(part,) for part in near]
    if lax.axis_size("replica") != 4:
        return whole
    rows, width = near[0].shape
    split = rows * 5 // 12 // 16 * 16
    parts = [
        jax.ShapeDtypeStruct((count, width), near[0].dtype) for count in (split, rows - split)
    ]
    first, second = call(
        cut_kernel, "cut", [near[2], near[1]], [VMEM, VMEM], parts, after=after
    )
    return whole + [(from_peer(first, 1), from_peer(second, 2))]


def factor_rows(refs, slot_count):
    if len(refs) == 1:
        return [refs[0].at[pl.ds(place * slot_count, slot_count)] for place in range(3)]
    payload = jnp.concatenate([ref[...] for ref in refs], axis=0)
    return [payload[place * slot_count : (place + 1) * slot_count] for place in range(3)]


def regroup(refs, lengths):
    groups, at = [], 0
    for length in lengths:
        groups.append(refs[at : at + length])
        at += length
    return groups


def flatten(groups):
    return [array for group in groups for array in group]


def pair_list(count):
    return [(i, j) for i in range(count) for j in range(i, count)]


SMEM = pl.BlockSpec(memory_space=pltpu.SMEM)
VMEM = pl.BlockSpec(memory_space=pltpu.VMEM)


def call(
    kernel, name, operands, specs, outs, out_specs=None, grid=(), scratch=(), after=(), cost=0, room=0
):
    size = sum(x.size * x.dtype.itemsize for x in list(operands) + list(outs))
    taken = len(operands)

    def body(*refs):
        kernel(*refs[:taken], *refs[taken + len(after) :])

    return pl.pallas_call(
        body,
        grid=grid,
        in_specs=list(specs) + [VMEM] * len(after),
        out_specs=out_specs if out_specs is not None else [VMEM for _ in outs],
        out_shape=outs,
        scratch_shapes=list(scratch),
        compiler_params=pltpu.CompilerParams(
            dimension_semantics=("arbitrary",) * len(grid),
            vmem_limit_bytes=max(room, min(56 * MIB, size + 8 * MIB)),
        ),
        cost_estimate=pl.CostEstimate(flops=0, bytes_accessed=cost, transcendentals=0),
        name=name,
    )(*operands, *after)


def segment(rep_ref, offset, width):
    return pl.ds(pl.multiple_of((rep_ref[0] ^ offset) * width, width), width)


def rows_kernel(expert_count, rep_ref, ids_ref, task_ref, row_ref, grads_ref, *out_refs):
    row_count = grads_ref.shape[0]
    seg_rows = out_refs[0].shape[1]
    block_count = ids_ref.shape[1]
    block_rows = row_count // block_count
    square = (row_count, row_count)
    earlier = lax.broadcasted_iota(jnp.int32, square, 0) < lax.broadcasted_iota(
        jnp.int32, square, 1
    )
    experts = lax.broadcasted_iota(jnp.int32, (expert_count, row_count), 0)
    chosen = jnp.where(experts == row_ref[...], 1.0, 0.0)
    before = multiply(
        chosen.astype(jnp.bfloat16), jnp.where(earlier, 1.0, 0.0).astype(jnp.bfloat16)
    )
    rank = jnp.sum(chosen * before, axis=0, keepdims=True)
    line = lax.broadcasted_iota(jnp.int32, (LABEL_ROWS, row_count), 0)
    labels = jnp.where(line == 0, row_ref[...].astype(jnp.float32), 0.0)
    labels = jnp.where(line == 1, rank, labels).astype(jnp.bfloat16)
    for offset, out_ref in enumerate(out_refs):
        columns = segment(rep_ref, offset, seg_rows)
        for block in range(block_count):
            rows = pl.ds(block * block_rows, block_rows)
            weight = task_ref[ids_ref[0, block]]
            out_ref[rows, :] = (grads_ref[rows, columns].astype(jnp.float32) * weight).astype(
                jnp.bfloat16
            )
        if row_count < seg_rows:
            out_ref[pl.ds(row_count, LABEL_ROWS), :] = jnp.zeros(
                (LABEL_ROWS, seg_rows), jnp.bfloat16
            )
        out_ref[pl.ds(row_count, LABEL_ROWS), pl.ds(0, row_count)] = labels


def one_hot(block_ref, row_count, slot_count, capacity):
    labels = block_ref[pl.ds(row_count, LABEL_ROWS), pl.ds(0, row_count)].astype(jnp.float32)
    slot = (labels[0:1] * capacity + labels[1:2]).astype(jnp.int32)
    places = lax.broadcasted_iota(jnp.int32, (slot_count, row_count), 0)
    return jnp.where(places == slot, 1.0, 0.0).astype(jnp.bfloat16)


def place_kernel(count, row_count, spot_ref, *refs):
    block_refs, out_refs, placed_ref = refs[:count], refs[count:-1], refs[-1]
    _, expert_count, capacity, seg_rows = placed_ref.shape
    slot_count = expert_count * capacity
    for offset, block_ref in enumerate(block_refs):
        placing = one_hot(block_ref, row_count, slot_count, capacity)
        placed = multiply(placing, block_ref[pl.ds(0, row_count), :])
        placed = placed.reshape(expert_count, capacity, seg_rows)
        placed_ref[offset] = placed.astype(jnp.bfloat16)
        for expert in range(expert_count):
            out_refs[expert // 2][expert % 2, offset] = placed_ref[offset, spot_ref[0] ^ expert]


def unplace_kernel(spot_ref, block_ref, *refs):
    returned_refs, out_ref, slots_ref = refs[:-2], refs[-2], refs[-1]
    expert_count, capacity, _ = slots_ref.shape
    slot_count = expert_count * capacity
    row_count = out_ref.shape[1]
    placing = one_hot(block_ref, row_count, slot_count, capacity)
    for expert in range(expert_count):
        block_ref = spread_block(expert_count // 2, returned_refs, expert)
        slots_ref[spot_ref[0] ^ expert] = block_ref[...]
    out_ref[0] = contract_first(placing, flat_rows(slots_ref[...])).astype(jnp.bfloat16)


def flat_rows(blocks):
    rows = blocks.shape[0] * blocks.shape[1]
    if blocks.shape[1] % 16:
        wide = blocks.astype(jnp.float32).reshape(rows, blocks.shape[2])
        return wide.astype(jnp.bfloat16)
    return blocks.reshape(rows, blocks.shape[2])


def back_kernel(chips, arrays, spot_ref, weight_ref, *refs):
    came_refs, incoming_ref, out_refs = refs[:arrays], refs[arrays], refs[arrays + 1 :]
    for offset, out_ref in enumerate(out_refs):
        for expert in range(2 * chips):
            block_ref = spread_block(chips, came_refs, expert)
            incoming_ref[offset, spot_ref[0] ^ expert] = block_ref[offset]
        rows = flat_rows(incoming_ref[offset])
        out_ref[...] = multiply(rows, weight_ref[...]).astype(out_ref.dtype)


def forward_kernel(offsets, lengths, has_start, rep_ref, inputs_ref, *refs):
    out_ref = refs[-1]
    weight_refs = refs[:-1]
    gate = up = None
    if has_start:
        gate, up = weight_refs[0][0], weight_refs[0][1]
        weight_refs = weight_refs[1:]
    for offset, group in zip(offsets, regroup(weight_refs, lengths)):
        gate_rows, up_rows = projection_rows(group)
        rows = inputs_ref[:, segment(rep_ref, offset, gate_rows.shape[0])]
        gate_part, up_part = multiply(rows, gate_rows), multiply(rows, up_rows)
        gate = gate_part if gate is None else gate + gate_part
        up = up_part if up is None else up + up_part
    out_ref[0] = gate
    out_ref[1] = up


def factor_kernel(forward_ref, *refs):
    back_refs, out_ref = refs[:-1], refs[-1]
    slot_count = forward_ref.shape[1]
    hidden_grad = back_refs[0][...]
    for back_ref in back_refs[1:]:
        hidden_grad = hidden_grad + back_ref[...].astype(jnp.float32)
    gate_pre, up_pre = forward_ref[0], forward_ref[1]
    sigmoid_gate = jax.nn.sigmoid(gate_pre)
    gate_act = gate_pre * sigmoid_gate
    gate_grad = hidden_grad * up_pre * sigmoid_gate * (1.0 + gate_pre * (1.0 - sigmoid_gate))
    parts = (gate_grad, hidden_grad * gate_act, gate_act * up_pre)
    for place, part in enumerate(parts):
        out_ref[pl.ds(place * slot_count, slot_count), :] = part.astype(jnp.bfloat16)


def slot_kernel(lengths, rep_ref, spot_ref, factor_ref, *refs):
    chips = refs[-1].shape[1] // 2
    weight_refs, out_refs, slots_ref = refs[: -chips - 1], refs[-chips - 1 : -1], refs[-1]
    _, expert_count, capacity, seg_rows = slots_ref.shape
    slot_count = expert_count * capacity
    gate_grad = factor_ref[pl.ds(0, slot_count), :]
    up_grad = factor_ref[pl.ds(slot_count, slot_count), :]
    for offset, group in enumerate(regroup(weight_refs, lengths)):
        gate_rows, up_rows = projection_rows(group)
        total = contract_last(gate_grad, gate_rows) + contract_last(up_grad, up_rows)
        total = total.reshape(expert_count, capacity, seg_rows)
        slots_ref[offset] = total.astype(jnp.bfloat16)
        columns = segment(rep_ref, offset, seg_rows)
        for expert in range(expert_count):
            out_ref = out_refs[expert // 2]
            out_ref[expert % 2, :, columns] = slots_ref[offset, spot_ref[0] ^ expert]


def gram_kernel(count, offsets, lengths, place, rep_ref, *refs):
    if place:
        before_ref, earlier_ref, refs = refs[0], refs[1], refs[2:]
    incoming_ref, operand_refs, grads_ref, gram_ref = refs[0], refs[1:-2], refs[-2], refs[-1]
    seg_rows, hidden_width = grads_ref.shape[2:]
    slot_count = incoming_ref.shape[1] * incoming_ref.shape[2]
    groups = regroup(operand_refs, lengths)
    known = list(range(place)) + list(offsets)
    pairs = [(i, j) for i, j in pair_list(len(known)) if j >= place]
    lines = 8
    tile = min(seg_rows, 256)
    sums = [jnp.zeros((lines, hidden_width), jnp.float32) for _ in pairs]
    operands = []
    for at, offset in enumerate(offsets):
        input_refs, factor_refs = groups[2 * at : 2 * at + 2]
        columns = input_rows(rep_ref, input_refs, slot_count, seg_rows)
        gate_ref, up_ref, hidden_ref = factor_rows(factor_refs, slot_count)
        received = flat_rows(incoming_ref[offset])
        operands.append([(columns, gate_ref), (columns, up_ref), (received, hidden_ref)])
    for matrix in range(3):
        for start in range(0, seg_rows, tile):
            rows = pl.ds(start, tile)
            blocks = [earlier_ref[at, matrix, rows] for at in range(place)]
            for at in range(len(offsets)):
                left, right_ref = operands[at][matrix]
                block = contract_first(left[:, start : start + tile], right_ref[...])
                grads_ref[at, matrix, rows] = block
                blocks.append(block)
            for place_of, (i, j) in enumerate(pairs):
                products = (blocks[i] * blocks[j]).reshape(tile // lines, lines, hidden_width)
                sums[place_of] = sums[place_of] + jnp.sum(products, axis=0)
    gram_ref[...] = before_ref[...] if place else jnp.zeros_like(gram_ref)
    for total, (i, j) in zip(sums, pairs):
        total = jnp.sum(total, axis=0, keepdims=True)
        part = total[:, :128]
        for lane in range(128, hidden_width, 128):
            part = part + total[:, lane : lane + 128]
        first, second = rep_ref[0] ^ known[i], rep_ref[0] ^ known[j]
        row = jnp.minimum(first, second) * count + jnp.maximum(first, second)
        gram_ref[pl.ds(row, 1), :] = part


def merge_coefs(gram, count):
    vectors = [{rep: None} for rep in range(count)]

    def term(coef, value):
        return value if coef is None else coef * value

    def inner(left, right):
        total = None
        for i, left_coef in left.items():
            for j, right_coef in right.items():
                value = term(left_coef, term(right_coef, gram[min(i, j), max(i, j)]))
                total = value if total is None else total + value
        return total

    while len(vectors) > 1:
        merged = []
        for first, second in zip(vectors[0::2], vectors[1::2]):
            norm_first = jnp.maximum(inner(first, first), 0.0)
            norm_second = jnp.maximum(inner(second, second), 0.0)
            bound = jnp.sqrt(norm_first) * jnp.sqrt(norm_second)
            cross = jnp.minimum(jnp.maximum(inner(first, second), -bound), bound)
            coef_first = 1.0 - cross / (2.0 * (norm_first + norm_eps))
            coef_second = 1.0 - cross / (2.0 * (norm_second + norm_eps))
            joined = {rep: term(coef, coef_first) for rep, coef in first.items()}
            joined.update({rep: term(coef, coef_second) for rep, coef in second.items()})
            merged.append(joined)
        vectors = merged
    return [vectors[0][rep] for rep in range(count)]


def adam_kernel(count, places, rep_ref, *refs):
    gram_refs, grads_refs = refs[:count], refs[count : count + len(places)]
    first_ref, second_ref, step_ref, coef_ref = refs[count + len(places) :]
    block_rows, hidden_width = step_ref.shape[2:]
    lines = coef_ref.shape[1]

    @pl.when((pl.program_id(0) == 0) & (pl.program_id(1) == 0))
    def _():
        sums = gram_refs[0][...]
        for gram_ref in gram_refs[1:]:
            sums = sums + gram_ref[...]
        sums = jnp.sum(sums, axis=1, keepdims=True)
        gram = {(i, j): sums[i * count + j : i * count + j + 1] for i, j in pair_list(count)}
        for rep, coef in enumerate(merge_coefs(gram, count)):
            coef_ref[rep] = jnp.broadcast_to(coef, coef_ref.shape[1:])

    matrix = pl.program_id(0)
    block = pl.program_id(1) * block_rows
    coefs = [[coef_ref[rep_ref[0] ^ offset] for offset in offsets] for offsets in places]

    def step(index, _):
        rows = pl.ds(pl.multiple_of(index * lines, lines), lines)
        all_rows = pl.ds(pl.multiple_of(block + index * lines, lines), lines)
        for lane in range(0, hidden_width, 128):
            columns = pl.ds(lane, 128)
            merged = None
            for grads_ref, group in zip(grads_refs, coefs):
                for at, coef in enumerate(group):
                    part = grads_ref[at, matrix, all_rows, columns] * coef
                    merged = part if merged is None else merged + part
            first_new = (beta_first / first_fix) * first_ref[0, matrix, all_rows, columns] + (
                (1.0 - beta_first) / first_fix
            ) * merged
            second_new = (beta_second / second_fix) * second_ref[0, matrix, all_rows, columns] + (
                (1.0 - beta_second) / second_fix
            ) * (merged * merged)
            root = second_new * lax.rsqrt(second_new)
            step_ref[0, 0, rows, columns] = first_new / (root + adam_eps)
        return 0

    lax.fori_loop(0, block_rows // lines, step, 0, unroll=4)


def adasum_adam_many(rep, inputs, incoming, factors, first_moment, second_moment):
    count = len(inputs)
    half = inputs[0].shape[0] // 2
    grads = []
    for offset in range(count):
        (payload,) = factors[offset]
        gate_grad, up_grad, hidden = payload.reshape(3, 2 * half, -1)
        received = incoming[offset].reshape(2 * half, incoming.shape[3])
        grads.append(
            jnp.stack(
                [
                    contract_first(inputs[offset], gate_grad),
                    contract_first(inputs[offset], up_grad),
                    contract_first(received, hidden),
                ]
            )
        )
    grads = jnp.stack(grads)[rep[0] ^ jnp.arange(count)]
    flat = grads.reshape(count, -1)
    gram = lax.psum(jnp.matmul(flat, flat.T, precision=lax.Precision.HIGHEST), "replica")
    coefs = jnp.eye(count, dtype=jnp.float32)
    while coefs.shape[0] > 1:
        inner = jnp.matmul(
            jnp.matmul(coefs, gram, precision=lax.Precision.HIGHEST),
            coefs.T,
            precision=lax.Precision.HIGHEST,
        )
        norms = jnp.maximum(jnp.diagonal(inner), 0.0)
        norm_first, norm_second = norms[0::2], norms[1::2]
        bound = jnp.sqrt(norm_first) * jnp.sqrt(norm_second)
        cross = jnp.clip(jnp.diagonal(inner, offset=1)[0::2], -bound, bound)
        coef_first = 1.0 - cross / (2.0 * (norm_first + norm_eps))
        coef_second = 1.0 - cross / (2.0 * (norm_second + norm_eps))
        coefs = coef_first[:, None] * coefs[0::2] + coef_second[:, None] * coefs[1::2]
    merged = jnp.sum(coefs[0][:, None, None, None] * grads, axis=0)
    first_new = beta_first * first_moment[0] + (1.0 - beta_first) * merged
    second_new = beta_second * second_moment[0] + (1.0 - beta_second) * merged * merged
    return ((first_new / first_fix) / (jnp.sqrt(second_new / second_fix) + adam_eps))[None]


def adasum(rep, inputs, incoming, factors):
    count = len(inputs)
    seg_rows, hidden_width = incoming.shape[3], factors[0][0].shape[-1]
    shape = jax.ShapeDtypeStruct
    groups = [[k for k in range(count) if k < 3], [k for k in range(count) if k == 3]]
    groups = [group for group in groups if group]
    grads, gram, first_gram, place = [], None, None, 0
    for group in groups:
        operands = [rep] if gram is None else [rep, gram, grads[0]]
        parts = [x for k in group for x in (inputs[k], factors[k])]
        operands += [incoming] + flatten(parts)
        more, gram = call(
            functools.partial(gram_kernel, count, group, [len(x) for x in parts], place),
            "gram_late" if place else "gram",
            operands,
            [SMEM] + [VMEM] * (len(operands) - 1),
            [
                shape((len(group), 3, seg_rows, hidden_width), jnp.float32),
                shape((max(8, count * count), 128), jnp.float32),
            ],
            cost=0 if place else 0,
        )
        first_gram = gram if first_gram is None else first_gram
        grads.append(more)
        place += len(group)
    return groups, grads, gram, first_gram


def adam(rep, groups, grads, gram, first_moment, second_moment, after):
    count = sum(len(group) for group in groups)
    seg_rows, hidden_width = first_moment.shape[2:]
    grams = [gram] + [from_peer(gram, k) for k in reversed(range(1, count))]
    tile = min(seg_rows, 256)
    moment_spec = pl.BlockSpec((1, 1, tile, hidden_width), lambda m, d: (0, m, d, 0))
    (adam_step,) = call(
        functools.partial(adam_kernel, count, groups),
        "adam",
        [rep, *grams, *grads, first_moment, second_moment],
        [SMEM] + [VMEM] * (len(grams) + len(grads) + 2),
        [jax.ShapeDtypeStruct(first_moment.shape, jnp.float32)],
        out_specs=[moment_spec],
        grid=(3, seg_rows // tile),
        scratch=[pltpu.VMEM((count, 16, 128), jnp.float32)],
        after=after,
    )
    return adam_step


def shards(
    weights, first_moment, second_moment, out_grads, routes, task_ids, task_weights, saved_inputs
):
    expert_count = lax.axis_size("expert")
    rep_count = lax.axis_size("replica")
    row_count = out_grads.shape[1]
    model_width = out_grads.shape[2]
    hidden_width = weights.shape[3]
    slot_count = saved_inputs.shape[2]
    capacity = slot_count // expert_count
    seg_rows = model_width // rep_count
    half = slot_count // 2
    offsets = range(rep_count)
    chips = expert_count // 2
    rep = lax.axis_index("replica").astype(jnp.int32).reshape(1)
    spot = lax.axis_index("expert").astype(jnp.int32).reshape(1)
    shape = jax.ShapeDtypeStruct

    block = shape((row_count + LABEL_ROWS, seg_rows), jnp.bfloat16)
    small = [routes[0].reshape(1, row_count), out_grads[0]]
    row_blocks = call(
        functools.partial(rows_kernel, expert_count),
        "rows",
        [rep, task_ids, task_weights, *small],
        [SMEM] * 3 + [pl.BlockSpec(x.shape, lambda i: (0, 0)) for x in small],
        [block for _ in offsets],
        grid=(1,),
        room=56 * MIB,
    )
    routed = exchange(row_blocks)

    inputs_home = saved_inputs[0, 0]
    pair = weights[0, :2]
    packed = rep_count == 4 and seg_rows == hidden_width
    if packed:
        payload = shape((2 * seg_rows + slot_count + half, seg_rows), jnp.bfloat16)
        to_one, to_two = call(
            payload_kernel,
            "payload",
            [jnp.concatenate([rep, spot]), pair, inputs_home],
            [SMEM, VMEM, VMEM],
            [payload, payload],
            after=routed[1:],
        )
        from_two, from_one = from_peer(to_two, 2), from_peer(to_one, 1)
        projections = [(pair,), (from_one,), (from_two,)]
        inputs = [(inputs_home,), (from_one,), (from_two,)]
    else:
        projections = [(x,) for x in exchange([pair] * rep_count)]
        pieces = [shape((slot_count, seg_rows), jnp.bfloat16) for _ in offsets]
        pieces = call(split_kernel, "split", [rep, inputs_home], [SMEM, VMEM], pieces)
        inputs = [(x,) for x in exchange(pieces)]

    part = shape((2, rep_count, capacity, seg_rows), jnp.bfloat16)
    placed = (
        call(
            functools.partial(place_kernel, rep_count, row_count),
            "place",
            [spot, *routed],
            [SMEM] + [VMEM] * len(routed),
            [part] * chips,
            scratch=[
                pltpu.VMEM((rep_count, expert_count, capacity, seg_rows), jnp.bfloat16)
            ],
        )
    )

    came = across_chips(placed)

    came = finish_spread(came)

    back_shape = (slot_count, hidden_width)
    incoming, *back = call(
        functools.partial(back_kernel, chips, len(came)),
        "back",
        [spot, weights[0, 2], *came],
        [SMEM] + [VMEM] * (1 + len(came)),
        [shape((rep_count, expert_count, capacity, seg_rows), jnp.bfloat16)]
        + [shape(back_shape, jnp.bfloat16 if k else jnp.float32) for k in offsets],
    )
    own_back = back[:1]
    back = exchange(back)
    if packed:
        split = seg_rows * 3 // 4
        passed = [
            shape((count + half, seg_rows), jnp.bfloat16) for count in (split, 2 * seg_rows - split)
        ]
        first, second = call(
            pass_kernel,
            "pass",
            [from_two, from_one],
            [VMEM, VMEM],
            passed,
            after=own_back,
        )
        last = (from_peer(first, 1), from_peer(second, 2))
        projections.append(last)
        inputs.append(last)

    forward = None
    late = [3] if packed else []
    for name, group in (("forward", [k for k in offsets if k not in late]), ("rest", late)):
        if not group:
            continue
        operands = [rep, inputs_home] + ([] if forward is None else [forward])
        operands += flatten(projections[k] for k in group)
        lengths = [len(projections[k]) for k in group]
        (forward,) = call(
            functools.partial(forward_kernel, group, lengths, forward is not None),
            name,
            operands,
            [SMEM] + [VMEM] * (len(operands) - 1),
            [shape((2, slot_count, hidden_width), jnp.float32)],
            cost=0 if name == "rest" else 0,
        )

    (own_factors,) = call(
        factor_kernel,
        "factors",
        [forward, *back],
        [VMEM] * (1 + len(back)),
        [shape((3 * slot_count, hidden_width), jnp.bfloat16)],
    )
    near_factors = gather_near(own_factors)

    operands = [rep, spot, own_factors] + flatten(projections)
    returning = across_chips(
        call(
            functools.partial(slot_kernel, [len(group) for group in projections]),
            "slots",
            operands,
            [SMEM] * 2 + [VMEM] * (len(operands) - 2),
            [shape((2, capacity, model_width), jnp.bfloat16)] * chips,
            scratch=[
                pltpu.VMEM((rep_count, expert_count, capacity, seg_rows), jnp.bfloat16)
            ],
        )
    )
    factors = gather_rest(near_factors, after=returning[:1])
    if rep_count <= 4:
        *merging, first_gram = adasum(rep, inputs, incoming, factors)
        returned = finish_spread(returning, [first_gram], pieces=2)
        unplace_after = merging[2:]
    else:
        returned, unplace_after = finish_spread(returning), ()
    (input_grads,) = call(
        unplace_kernel,
        "unplace",
        [spot, routed[0], *returned],
        [SMEM] + [VMEM] * (1 + len(returned)),
        [shape((1, row_count, model_width), jnp.bfloat16)],
        scratch=[pltpu.VMEM((expert_count, capacity, model_width), jnp.bfloat16)],
        after=unplace_after,
    )
    if rep_count <= 4:
        adam_step = adam(rep, *merging, first_moment, second_moment, ())
    else:
        adam_step = adasum_adam_many(
            rep, [x for (x,) in inputs], incoming, factors, first_moment, second_moment
        )
    return (input_grads, adam_step)


def solution(mesh):
    return jax.shard_map(
        shards,
        mesh=mesh,
        in_specs=(
            P("expert", None, "replica", None),
            P("expert", None, "replica", None),
            P("expert", None, "replica", None),
            P("replica", "expert", None),
            P("replica", "expert", None),
            P("replica", "expert"),
            P(),
            P("replica", "expert", None, None),
        ),
        out_specs=(P("replica", "expert", None), P("expert", None, "replica", None)),
        check_vma=False,
    )
```

```python
import functools

import jax
import jax.numpy as jnp
from jax import lax
from jax.experimental import pallas as pl
from jax.experimental.pallas import tpu as pltpu
from jax.sharding import PartitionSpec as P

beta_first = 0.9
beta_second = 0.95
adam_eps = 1e-08
norm_eps = 1e-06
first_fix = 1.0 - (0.9**50) ** 2
second_fix = 1.0 - (0.95**50) ** 2
MIB = 1024 * 1024
LABEL_ROWS = 16


def contract_first(left, right):
    return lax.dot_general(
        left, right, (((0,), (0,)), ((), ())), preferred_element_type=jnp.float32
    )


def contract_last(left, right):
    return lax.dot_general(
        left, right, (((1,), (1,)), ((), ())), preferred_element_type=jnp.float32
    )


def multiply(left, right):
    return jnp.dot(left, right, preferred_element_type=jnp.float32)


def from_peer(array, offset):
    count = lax.axis_size("replica")
    return lax.ppermute(array, "replica", [(i, i ^ offset) for i in range(count)])


def across_chips(parts):
    count = lax.axis_size("expert")
    return [parts[0]] + [
        lax.ppermute(part, "expert", [(i, i ^ 2 * k) for i in range(count)])
        for k, part in enumerate(parts)
        if k
    ]


def pick_kernel(chips, *refs):
    block_refs = [ref.at[k] for ref in refs[chips:] for k in range(ref.shape[0])]
    for part_ref, block_ref in zip(refs[:chips], block_refs):
        block_ref[...] = part_ref[1]


def finish_spread(came, after=(), pieces=1):
    count = lax.axis_size("expert")
    chips = len(came)
    block = jax.ShapeDtypeStruct((chips // pieces,) + came[0].shape[1:], came[0].dtype)
    others = call(
        functools.partial(pick_kernel, chips),
        "pick",
        came,
        [VMEM] * chips,
        [block] * pieces,
        after=after,
    )
    swapped = [lax.ppermute(x, "expert", [(i, i ^ 1) for i in range(count)]) for x in others]
    return [*came, *swapped]


def spread_block(chips, refs, offset):
    if offset % 2 == 0:
        return refs[offset // 2].at[0]
    blocks = [ref.at[k] for ref in refs[chips:] for k in range(ref.shape[0])]
    return blocks[offset // 2]


def exchange(parts):
    return [parts[0]] + [from_peer(part, k) for k, part in enumerate(parts) if k]


def split_kernel(rep_ref, matrix_ref, *out_refs):
    for offset, out_ref in enumerate(out_refs):
        out_ref[...] = matrix_ref[:, segment(rep_ref, offset, out_ref.shape[1])]


def payload_kernel(rep_ref, pair_ref, inputs_ref, *out_refs):
    seg_rows = pair_ref.shape[1]
    slot_count = inputs_ref.shape[0]
    half = slot_count // 2
    for part, out_ref in enumerate(out_refs):
        out_ref[pl.ds(0, seg_rows), :] = pair_ref[0]
        out_ref[pl.ds(seg_rows, seg_rows), :] = pair_ref[1]
        columns = segment(rep_ref, part + 1, seg_rows)
        out_ref[pl.ds(2 * seg_rows, slot_count), :] = inputs_ref[:, columns]
        columns = segment(rep_ref, 3, seg_rows)
        out_ref[pl.ds(2 * seg_rows + slot_count, half), :] = inputs_ref[
            pl.ds(part * half, half), columns
        ]


def pass_kernel(from_two_ref, from_one_ref, *out_refs):
    for part, (near_ref, out_ref) in enumerate(zip((from_two_ref, from_one_ref), out_refs)):
        seg_rows = near_ref.shape[1]
        half = out_ref.shape[0] - seg_rows
        out_ref[pl.ds(0, seg_rows), :] = near_ref[pl.ds(part * seg_rows, seg_rows), :]
        out_ref[pl.ds(seg_rows, half), :] = near_ref[pl.ds(near_ref.shape[0] - half, half), :]


def projection_rows(refs):
    if len(refs) == 1 and len(refs[0].shape) == 3:
        return refs[0].at[0], refs[0].at[1]
    seg_rows = refs[0].shape[1]
    start = 0 if len(refs) == 2 else seg_rows
    return refs[0].at[pl.ds(0, seg_rows)], refs[-1].at[pl.ds(start, seg_rows)]


def input_rows(rep_ref, refs, slot_count, seg_rows):
    if len(refs) == 2:
        rows = pl.ds(seg_rows, slot_count // 2)
        return jnp.concatenate([refs[1][rows], refs[0][rows]], axis=0)
    (ref,) = refs
    if ref.shape[0] > slot_count:
        return ref[pl.ds(2 * seg_rows, slot_count), :]
    return ref[...] if ref.shape[1] == seg_rows else ref[:, segment(rep_ref, 0, seg_rows)]


def cut_kernel(from_two_ref, from_one_ref, first_ref, second_ref):
    first_ref[...] = from_two_ref[0]
    second_ref[...] = from_one_ref[1]


def gather_near(payload):
    count = lax.axis_size("replica")
    if count != 4:
        return exchange([payload] * count)
    from_two = from_peer(payload, 2)
    return [payload, from_peer(payload, 1), from_two]


def gather_rest(near, after):
    whole = [(part,) for part in near]
    if lax.axis_size("replica") != 4:
        return whole
    half = jax.ShapeDtypeStruct(near[0].shape[1:], near[0].dtype)
    first, second = call(
        cut_kernel, "cut", [near[2], near[1]], [VMEM, VMEM], [half, half], after=after
    )
    return whole + [(from_peer(first, 1), from_peer(second, 2))]


def halves(refs):
    return refs if len(refs) == 2 else (refs[0].at[0], refs[0].at[1])


def regroup(refs, lengths):
    groups, at = [], 0
    for length in lengths:
        groups.append(refs[at : at + length])
        at += length
    return groups


def flatten(groups):
    return [array for group in groups for array in group]


def pair_list(count):
    return [(i, j) for i in range(count) for j in range(i, count)]


SMEM = pl.BlockSpec(memory_space=pltpu.SMEM)
VMEM = pl.BlockSpec(memory_space=pltpu.VMEM)


def call(
    kernel, name, operands, specs, outs, out_specs=None, grid=(), scratch=(), after=(), cost=0, room=0
):
    size = sum(x.size * x.dtype.itemsize for x in list(operands) + list(outs))
    taken = len(operands)

    def body(*refs):
        kernel(*refs[:taken], *refs[taken + len(after) :])

    return pl.pallas_call(
        body,
        grid=grid,
        in_specs=list(specs) + [VMEM] * len(after),
        out_specs=out_specs if out_specs is not None else [VMEM for _ in outs],
        out_shape=outs,
        scratch_shapes=list(scratch),
        compiler_params=pltpu.CompilerParams(
            dimension_semantics=("arbitrary",) * len(grid),
            vmem_limit_bytes=max(room, min(56 * MIB, size + 8 * MIB)),
        ),
        cost_estimate=pl.CostEstimate(flops=0, bytes_accessed=cost, transcendentals=0),
        name=name,
    )(*operands, *after)


def segment(rep_ref, offset, width):
    return pl.ds(pl.multiple_of((rep_ref[0] ^ offset) * width, width), width)


def rows_kernel(expert_count, rep_ref, ids_ref, task_ref, row_ref, grads_ref, *out_refs):
    row_count = grads_ref.shape[0]
    seg_rows = out_refs[0].shape[1]
    block_count = ids_ref.shape[1]
    block_rows = row_count // block_count
    square = (row_count, row_count)
    earlier = lax.broadcasted_iota(jnp.int32, square, 0) < lax.broadcasted_iota(
        jnp.int32, square, 1
    )
    experts = lax.broadcasted_iota(jnp.int32, (expert_count, row_count), 0)
    chosen = jnp.where(experts == row_ref[...], 1.0, 0.0)
    before = multiply(
        chosen.astype(jnp.bfloat16), jnp.where(earlier, 1.0, 0.0).astype(jnp.bfloat16)
    )
    rank = jnp.sum(chosen * before, axis=0, keepdims=True)
    line = lax.broadcasted_iota(jnp.int32, (LABEL_ROWS, row_count), 0)
    labels = jnp.where(line == 0, row_ref[...].astype(jnp.float32), 0.0)
    labels = jnp.where(line == 1, rank, labels).astype(jnp.bfloat16)
    for offset, out_ref in enumerate(out_refs):
        columns = segment(rep_ref, offset, seg_rows)
        for block in range(block_count):
            rows = pl.ds(block * block_rows, block_rows)
            weight = task_ref[ids_ref[0, block]]
            out_ref[rows, :] = (grads_ref[rows, columns].astype(jnp.float32) * weight).astype(
                jnp.bfloat16
            )
        if row_count < seg_rows:
            out_ref[pl.ds(row_count, LABEL_ROWS), :] = jnp.zeros(
                (LABEL_ROWS, seg_rows), jnp.bfloat16
            )
        out_ref[pl.ds(row_count, LABEL_ROWS), pl.ds(0, row_count)] = labels


def one_hot(block_ref, row_count, slot_count, capacity):
    labels = block_ref[pl.ds(row_count, LABEL_ROWS), pl.ds(0, row_count)].astype(jnp.float32)
    slot = (labels[0:1] * capacity + labels[1:2]).astype(jnp.int32)
    places = lax.broadcasted_iota(jnp.int32, (slot_count, row_count), 0)
    return jnp.where(places == slot, 1.0, 0.0).astype(jnp.bfloat16)


def place_kernel(count, row_count, spot_ref, *refs):
    block_refs, out_refs, placed_ref = refs[:count], refs[count:-1], refs[-1]
    _, expert_count, capacity, seg_rows = placed_ref.shape
    slot_count = expert_count * capacity
    for offset, block_ref in enumerate(block_refs):
        placing = one_hot(block_ref, row_count, slot_count, capacity)
        placed = multiply(placing, block_ref[pl.ds(0, row_count), :])
        placed = placed.reshape(expert_count, capacity, seg_rows)
        placed_ref[offset] = placed.astype(jnp.bfloat16)
        for expert in range(expert_count):
            out_refs[expert // 2][expert % 2, offset] = placed_ref[offset, spot_ref[0] ^ expert]


def unplace_kernel(spot_ref, block_ref, *refs):
    returned_refs, out_ref, slots_ref = refs[:-2], refs[-2], refs[-1]
    expert_count, capacity, _ = slots_ref.shape
    slot_count = expert_count * capacity
    row_count = out_ref.shape[1]
    placing = one_hot(block_ref, row_count, slot_count, capacity)
    for expert in range(expert_count):
        block_ref = spread_block(expert_count // 2, returned_refs, expert)
        slots_ref[spot_ref[0] ^ expert] = block_ref[...]
    out_ref[0] = contract_first(placing, flat_rows(slots_ref[...])).astype(jnp.bfloat16)


def flat_rows(blocks):
    rows = blocks.shape[0] * blocks.shape[1]
    if blocks.shape[1] % 16:
        wide = blocks.astype(jnp.float32).reshape(rows, blocks.shape[2])
        return wide.astype(jnp.bfloat16)
    return blocks.reshape(rows, blocks.shape[2])


def back_kernel(chips, arrays, packed, spot_ref, weight_ref, *refs):
    came_refs, incoming_ref, out_refs = refs[:arrays], refs[arrays], refs[arrays + 1 :]
    for offset in range(incoming_ref.shape[0]):
        for expert in range(2 * chips):
            block_ref = spread_block(chips, came_refs, expert)
            incoming_ref[offset, spot_ref[0] ^ expert] = block_ref[offset]
        rows = flat_rows(incoming_ref[offset])
        total = multiply(rows, weight_ref[...])
        if not packed or offset == 0:
            out_refs[offset][...] = total.astype(out_refs[offset].dtype)
            continue
        _, near_ref, one_ref, two_ref = out_refs
        half = total.shape[0] // 2
        upper, lower = pl.ds(0, half), pl.ds(half, half)
        if offset == 1:
            one_ref[upper, :] = total[:half].astype(jnp.bfloat16)
            near_ref[lower, :] = total[half:]
        elif offset == 2:
            two_ref[upper, :] = total[half:].astype(jnp.bfloat16)
            near_ref[upper, :] = total[:half]
        else:
            one_ref[lower, :] = total[:half].astype(jnp.bfloat16)
            two_ref[lower, :] = total[half:].astype(jnp.bfloat16)


def add_kernel(near_ref, from_one_ref, from_two_ref, to_one_ref, to_two_ref):
    half = to_one_ref.shape[0]
    upper, lower = pl.ds(0, half), pl.ds(half, half)
    to_two_ref[...] = (near_ref[upper, :] + from_one_ref[lower, :].astype(jnp.float32)).astype(
        jnp.bfloat16
    )
    to_one_ref[...] = (near_ref[lower, :] + from_two_ref[lower, :].astype(jnp.float32)).astype(
        jnp.bfloat16
    )


def forward_kernel(offsets, lengths, has_start, rep_ref, inputs_ref, *refs):
    out_ref = refs[-1]
    weight_refs = refs[:-1]
    gate = up = None
    if has_start:
        gate, up = weight_refs[0][0], weight_refs[0][1]
        weight_refs = weight_refs[1:]
    for offset, group in zip(offsets, regroup(weight_refs, lengths)):
        gate_ref, up_ref = projection_rows(group)
        rows = inputs_ref[:, segment(rep_ref, offset, gate_ref.shape[0])]
        gate_part, up_part = multiply(rows, gate_ref[...]), multiply(rows, up_ref[...])
        gate = gate_part if gate is None else gate + gate_part
        up = up_part if up is None else up + up_part
    out_ref[0] = gate
    out_ref[1] = up


def factor_kernel(packed, forward_ref, *refs):
    back_refs, out_ref = refs[:-1], refs[-1]
    slot_count = forward_ref.shape[1]
    half = slot_count // 2
    hidden_grad = back_refs[0][...]
    if packed:
        upper, lower = [
            near_ref[pl.ds(0, half), :].astype(jnp.float32) + far_ref[...].astype(jnp.float32)
            for near_ref, far_ref in zip(back_refs[1:3], back_refs[3:])
        ]
        hidden_grad = hidden_grad + jnp.concatenate([upper, lower], axis=0)
        back_refs = back_refs[:1]
    for back_ref in back_refs[1:]:
        hidden_grad = hidden_grad + back_ref[...].astype(jnp.float32)
    gate_pre, up_pre = forward_ref[0], forward_ref[1]
    sigmoid_gate = jax.nn.sigmoid(gate_pre)
    gate_act = gate_pre * sigmoid_gate
    hidden = (gate_act * up_pre).astype(jnp.bfloat16)
    gate_grad = hidden_grad * up_pre * sigmoid_gate * (1.0 + gate_pre * (1.0 - sigmoid_gate))
    out_ref[0, pl.ds(0, slot_count)] = gate_grad.astype(jnp.bfloat16)
    out_ref[1, pl.ds(0, slot_count)] = (hidden_grad * gate_act).astype(jnp.bfloat16)
    for part in range(2):
        out_ref[part, pl.ds(slot_count, half)] = hidden[part * half : (part + 1) * half]


def slot_kernel(lengths, rep_ref, spot_ref, factor_ref, *refs):
    chips = refs[-1].shape[1] // 2
    weight_refs, out_refs, slots_ref = refs[: -chips - 1], refs[-chips - 1 : -1], refs[-1]
    _, expert_count, capacity, seg_rows = slots_ref.shape
    rows = pl.ds(0, expert_count * capacity)
    gate_grad, up_grad = factor_ref[0, rows], factor_ref[1, rows]
    for offset, group in enumerate(regroup(weight_refs, lengths)):
        gate_ref, up_ref = projection_rows(group)
        total = contract_last(gate_grad, gate_ref[...]) + contract_last(up_grad, up_ref[...])
        total = total.reshape(expert_count, capacity, seg_rows)
        slots_ref[offset] = total.astype(jnp.bfloat16)
        columns = segment(rep_ref, offset, seg_rows)
        for expert in range(expert_count):
            out_ref = out_refs[expert // 2]
            out_ref[expert % 2, :, columns] = slots_ref[offset, spot_ref[0] ^ expert]


def gram_kernel(count, offsets, lengths, place, rep_ref, *refs):
    if place:
        before_ref, earlier_ref, refs = refs[0], refs[1], refs[2:]
    incoming_ref, operand_refs, grads_ref, gram_ref = refs[0], refs[1:-2], refs[-2], refs[-1]
    middle = incoming_ref.shape[1] // 2
    seg_rows, hidden_width = grads_ref.shape[2:]
    slot_count = incoming_ref.shape[1] * incoming_ref.shape[2]
    groups = regroup(operand_refs, lengths)
    known = list(range(place)) + list(offsets)
    pairs = [(i, j) for i, j in pair_list(len(known)) if j >= place]
    lines = 8
    tile = min(seg_rows, 256)
    sums = [jnp.zeros((lines, hidden_width), jnp.float32) for _ in pairs]
    operands = []
    for at, offset in enumerate(offsets):
        input_refs, factor_refs = groups[2 * at : 2 * at + 2]
        rest = pl.ds(slot_count, slot_count // 2)
        columns = input_rows(rep_ref, input_refs, slot_count, seg_rows)
        gate_ref, up_ref = (ref.at[pl.ds(0, slot_count)] for ref in halves(factor_refs))
        first_ref, second_ref = (ref.at[rest] for ref in halves(factor_refs))
        upper = flat_rows(incoming_ref[offset, :middle])
        lower = flat_rows(incoming_ref[offset, middle:])
        operands.append(
            [
                [(columns, gate_ref)],
                [(columns, up_ref)],
                [(upper, first_ref), (lower, second_ref)],
            ]
        )
    for matrix in range(3):
        for start in range(0, seg_rows, tile):
            rows = pl.ds(start, tile)
            blocks = [earlier_ref[at, matrix, rows] for at in range(place)]
            for at in range(len(offsets)):
                block = None
                for left, right_ref in operands[at][matrix]:
                    part = contract_first(left[:, start : start + tile], right_ref[...])
                    block = part if block is None else block + part
                grads_ref[at, matrix, rows] = block
                blocks.append(block)
            for place_of, (i, j) in enumerate(pairs):
                products = (blocks[i] * blocks[j]).reshape(tile // lines, lines, hidden_width)
                sums[place_of] = sums[place_of] + jnp.sum(products, axis=0)
    gram_ref[...] = before_ref[...] if place else jnp.zeros_like(gram_ref)
    for total, (i, j) in zip(sums, pairs):
        total = jnp.sum(total, axis=0, keepdims=True)
        part = total[:, :128]
        for lane in range(128, hidden_width, 128):
            part = part + total[:, lane : lane + 128]
        first, second = rep_ref[0] ^ known[i], rep_ref[0] ^ known[j]
        row = jnp.minimum(first, second) * count + jnp.maximum(first, second)
        gram_ref[pl.ds(row, 1), :] = part


def merge_coefs(gram, count):
    vectors = [{rep: None} for rep in range(count)]

    def term(coef, value):
        return value if coef is None else coef * value

    def inner(left, right):
        total = None
        for i, left_coef in left.items():
            for j, right_coef in right.items():
                value = term(left_coef, term(right_coef, gram[min(i, j), max(i, j)]))
                total = value if total is None else total + value
        return total

    while len(vectors) > 1:
        merged = []
        for first, second in zip(vectors[0::2], vectors[1::2]):
            norm_first = jnp.maximum(inner(first, first), 0.0)
            norm_second = jnp.maximum(inner(second, second), 0.0)
            bound = jnp.sqrt(norm_first) * jnp.sqrt(norm_second)
            cross = jnp.minimum(jnp.maximum(inner(first, second), -bound), bound)
            coef_first = 1.0 - cross / (2.0 * (norm_first + norm_eps))
            coef_second = 1.0 - cross / (2.0 * (norm_second + norm_eps))
            joined = {rep: term(coef, coef_first) for rep, coef in first.items()}
            joined.update({rep: term(coef, coef_second) for rep, coef in second.items()})
            merged.append(joined)
        vectors = merged
    return [vectors[0][rep] for rep in range(count)]


def adam_kernel(count, places, rep_ref, *refs):
    gram_refs, grads_refs = refs[:count], refs[count : count + len(places)]
    first_ref, second_ref, step_ref, coef_ref = refs[count + len(places) :]
    block_rows, hidden_width = step_ref.shape[2:]
    lines = coef_ref.shape[1]

    @pl.when((pl.program_id(0) == 0) & (pl.program_id(1) == 0))
    def _():
        sums = gram_refs[0][...]
        for gram_ref in gram_refs[1:]:
            sums = sums + gram_ref[...]
        sums = jnp.sum(sums, axis=1, keepdims=True)
        gram = {(i, j): sums[i * count + j : i * count + j + 1] for i, j in pair_list(count)}
        for rep, coef in enumerate(merge_coefs(gram, count)):
            coef_ref[rep] = jnp.broadcast_to(coef, coef_ref.shape[1:])

    matrix = pl.program_id(0)
    block = pl.program_id(1) * block_rows
    coefs = [[coef_ref[rep_ref[0] ^ offset] for offset in offsets] for offsets in places]

    def step(index, _):
        rows = pl.ds(pl.multiple_of(index * lines, lines), lines)
        all_rows = pl.ds(pl.multiple_of(block + index * lines, lines), lines)
        for lane in range(0, hidden_width, 128):
            columns = pl.ds(lane, 128)
            merged = None
            for grads_ref, group in zip(grads_refs, coefs):
                for at, coef in enumerate(group):
                    part = grads_ref[at, matrix, all_rows, columns] * coef
                    merged = part if merged is None else merged + part
            first_new = (beta_first / first_fix) * first_ref[0, matrix, all_rows, columns] + (
                (1.0 - beta_first) / first_fix
            ) * merged
            second_new = (beta_second / second_fix) * second_ref[0, matrix, all_rows, columns] + (
                (1.0 - beta_second) / second_fix
            ) * (merged * merged)
            root = second_new * lax.rsqrt(second_new)
            step_ref[0, 0, rows, columns] = first_new / (root + adam_eps)
        return 0

    lax.fori_loop(0, block_rows // lines, step, 0, unroll=4)


def adasum_adam_many(rep, inputs, incoming, factors, first_moment, second_moment):
    count = len(inputs)
    half = inputs[0].shape[0] // 2
    grads = []
    for offset in range(count):
        (payload,) = factors[offset]
        gate_grad, up_grad = payload[:, : 2 * half]
        hidden = payload[:, 2 * half :].reshape(2 * half, -1)
        received = incoming[offset].reshape(2 * half, incoming.shape[3])
        grads.append(
            jnp.stack(
                [
                    contract_first(inputs[offset], gate_grad),
                    contract_first(inputs[offset], up_grad),
                    contract_first(received, hidden),
                ]
            )
        )
    grads = jnp.stack(grads)[rep[0] ^ jnp.arange(count)]
    flat = grads.reshape(count, -1)
    gram = lax.psum(jnp.matmul(flat, flat.T, precision=lax.Precision.HIGHEST), "replica")
    coefs = jnp.eye(count, dtype=jnp.float32)
    while coefs.shape[0] > 1:
        inner = jnp.matmul(
            jnp.matmul(coefs, gram, precision=lax.Precision.HIGHEST),
            coefs.T,
            precision=lax.Precision.HIGHEST,
        )
        norms = jnp.maximum(jnp.diagonal(inner), 0.0)
        norm_first, norm_second = norms[0::2], norms[1::2]
        bound = jnp.sqrt(norm_first) * jnp.sqrt(norm_second)
        cross = jnp.clip(jnp.diagonal(inner, offset=1)[0::2], -bound, bound)
        coef_first = 1.0 - cross / (2.0 * (norm_first + norm_eps))
        coef_second = 1.0 - cross / (2.0 * (norm_second + norm_eps))
        coefs = coef_first[:, None] * coefs[0::2] + coef_second[:, None] * coefs[1::2]
    merged = jnp.sum(coefs[0][:, None, None, None] * grads, axis=0)
    first_new = beta_first * first_moment[0] + (1.0 - beta_first) * merged
    second_new = beta_second * second_moment[0] + (1.0 - beta_second) * merged * merged
    return ((first_new / first_fix) / (jnp.sqrt(second_new / second_fix) + adam_eps))[None]


def adasum(rep, inputs, incoming, factors):
    count = len(inputs)
    seg_rows, hidden_width = incoming.shape[3], factors[0][0].shape[2]
    shape = jax.ShapeDtypeStruct
    groups = [[k for k in range(count) if k < 3], [k for k in range(count) if k == 3]]
    groups = [group for group in groups if group]
    grads, gram, first_gram, place = [], None, None, 0
    for group in groups:
        operands = [rep] if gram is None else [rep, gram, grads[0]]
        parts = [x for k in group for x in (inputs[k], factors[k])]
        operands += [incoming] + flatten(parts)
        more, gram = call(
            functools.partial(gram_kernel, count, group, [len(x) for x in parts], place),
            "gram_late" if place else "gram",
            operands,
            [SMEM] + [VMEM] * (len(operands) - 1),
            [
                shape((len(group), 3, seg_rows, hidden_width), jnp.float32),
                shape((max(8, count * count), 128), jnp.float32),
            ],
            cost=0 if place else 0,
        )
        first_gram = gram if first_gram is None else first_gram
        grads.append(more)
        place += len(group)
    return groups, grads, gram, first_gram


def adam(rep, groups, grads, gram, first_moment, second_moment, after):
    count = sum(len(group) for group in groups)
    seg_rows, hidden_width = first_moment.shape[2:]
    grams = [gram] + [from_peer(gram, k) for k in reversed(range(1, count))]
    tile = min(seg_rows, 256)
    moment_spec = pl.BlockSpec((1, 1, tile, hidden_width), lambda m, d: (0, m, d, 0))
    (adam_step,) = call(
        functools.partial(adam_kernel, count, groups),
        "adam",
        [rep, *grams, *grads, first_moment, second_moment],
        [SMEM] + [VMEM] * (len(grams) + len(grads) + 2),
        [jax.ShapeDtypeStruct(first_moment.shape, jnp.float32)],
        out_specs=[moment_spec],
        grid=(3, seg_rows // tile),
        scratch=[pltpu.VMEM((count, 16, 128), jnp.float32)],
        after=after,
    )
    return adam_step


def shards(
    weights, first_moment, second_moment, out_grads, routes, task_ids, task_weights, saved_inputs
):
    expert_count = lax.axis_size("expert")
    rep_count = lax.axis_size("replica")
    row_count = out_grads.shape[1]
    model_width = out_grads.shape[2]
    hidden_width = weights.shape[3]
    slot_count = saved_inputs.shape[2]
    capacity = slot_count // expert_count
    seg_rows = model_width // rep_count
    half = slot_count // 2
    offsets = range(rep_count)
    chips = expert_count // 2
    rep = lax.axis_index("replica").astype(jnp.int32).reshape(1)
    spot = lax.axis_index("expert").astype(jnp.int32).reshape(1)
    shape = jax.ShapeDtypeStruct

    block = shape((row_count + LABEL_ROWS, seg_rows), jnp.bfloat16)
    small = [routes[0].reshape(1, row_count), out_grads[0]]
    row_blocks = call(
        functools.partial(rows_kernel, expert_count),
        "rows",
        [rep, task_ids, task_weights, *small],
        [SMEM] * 3 + [pl.BlockSpec(x.shape, lambda i: (0, 0)) for x in small],
        [block for _ in offsets],
        grid=(1,),
        room=56 * MIB,
    )
    routed = exchange(row_blocks)

    inputs_home = saved_inputs[0, 0]
    pair = weights[0, :2]
    packed = rep_count == 4 and seg_rows == hidden_width
    if packed:
        payload = shape((2 * seg_rows + slot_count + half, seg_rows), jnp.bfloat16)
        to_one, to_two = call(
            payload_kernel,
            "payload",
            [jnp.concatenate([rep, spot]), pair, inputs_home],
            [SMEM, VMEM, VMEM],
            [payload, payload],
            after=routed[1:],
        )
        from_two, from_one = from_peer(to_two, 2), from_peer(to_one, 1)
        projections = [(pair,), (from_one,), (from_two,)]
        inputs = [(inputs_home,), (from_one,), (from_two,)]
    else:
        projections = [(x,) for x in exchange([pair] * rep_count)]
        pieces = [shape((slot_count, seg_rows), jnp.bfloat16) for _ in offsets]
        pieces = call(split_kernel, "split", [rep, inputs_home], [SMEM, VMEM], pieces)
        inputs = [(x,) for x in exchange(pieces)]

    part = shape((2, rep_count, capacity, seg_rows), jnp.bfloat16)
    placed = (
        call(
            functools.partial(place_kernel, rep_count, row_count),
            "place",
            [spot, *routed],
            [SMEM] + [VMEM] * len(routed),
            [part] * chips,
            scratch=[
                pltpu.VMEM((rep_count, expert_count, capacity, seg_rows), jnp.bfloat16)
            ],
        )
    )

    came = across_chips(placed)

    came = finish_spread(came)

    back_shape = (slot_count, hidden_width)
    incoming, *back = call(
        functools.partial(back_kernel, chips, len(came), packed),
        "back",
        [spot, weights[0, 2], *came],
        [SMEM] + [VMEM] * (1 + len(came)),
        [shape((rep_count, expert_count, capacity, seg_rows), jnp.bfloat16)]
        + [
            shape(back_shape, jnp.float32 if k == 0 or packed and k == 1 else jnp.bfloat16)
            for k in offsets
        ],
    )
    if not packed:
        back = exchange(back)
    if packed:
        own_back, near_back, to_one, to_two = back
        back_one, back_two = from_peer(to_one, 1), from_peer(to_two, 2)
        passed = shape((seg_rows + half, seg_rows), jnp.bfloat16)
        first, second = call(
            pass_kernel,
            "pass",
            [from_two, from_one],
            [VMEM, VMEM],
            [passed, passed],
            after=[back_one, back_two],
        )
        last = (from_peer(first, 1), from_peer(second, 2))
        to_one, to_two = call(
            add_kernel,
            "add",
            [near_back, back_one, back_two],
            [VMEM] * 3,
            [shape((half, hidden_width), jnp.bfloat16)] * 2,
        )
        back = [own_back, back_one, back_two, from_peer(to_two, 2), from_peer(to_one, 1)]
        projections.append(last)
        inputs.append(last)

    forward = None
    late = [3] if packed else []
    for name, group in (("forward", [k for k in offsets if k not in late]), ("rest", late)):
        if not group:
            continue
        operands = [rep, inputs_home] + ([] if forward is None else [forward])
        operands += flatten(projections[k] for k in group)
        lengths = [len(projections[k]) for k in group]
        (forward,) = call(
            functools.partial(forward_kernel, group, lengths, forward is not None),
            name,
            operands,
            [SMEM] + [VMEM] * (len(operands) - 1),
            [shape((2, slot_count, hidden_width), jnp.float32)],
            cost=0 if name == "rest" else 0,
        )

    (own_factors,) = call(
        functools.partial(factor_kernel, packed),
        "factors",
        [forward, *back],
        [VMEM] * (1 + len(back)),
        [shape((2, slot_count + half, hidden_width), jnp.bfloat16)],
    )
    near_factors = gather_near(own_factors)

    operands = [rep, spot, own_factors] + flatten(projections)
    returning = across_chips(
        call(
            functools.partial(slot_kernel, [len(group) for group in projections]),
            "slots",
            operands,
            [SMEM] * 2 + [VMEM] * (len(operands) - 2),
            [shape((2, capacity, model_width), jnp.bfloat16)] * chips,
            scratch=[
                pltpu.VMEM((rep_count, expert_count, capacity, seg_rows), jnp.bfloat16)
            ],
        )
    )
    factors = gather_rest(near_factors, after=returning[:1])
    if rep_count <= 4:
        *merging, first_gram = adasum(rep, inputs, incoming, factors)
        returned = finish_spread(returning, [first_gram], pieces=2)
        unplace_after = merging[2:]
    else:
        returned, unplace_after = finish_spread(returning), ()
    (input_grads,) = call(
        unplace_kernel,
        "unplace",
        [spot, routed[0], *returned],
        [SMEM] + [VMEM] * (1 + len(returned)),
        [shape((1, row_count, model_width), jnp.bfloat16)],
        scratch=[pltpu.VMEM((expert_count, capacity, model_width), jnp.bfloat16)],
        after=unplace_after,
    )
    if rep_count <= 4:
        adam_step = adam(rep, *merging, first_moment, second_moment, ())
    else:
        adam_step = adasum_adam_many(
            rep, [x for (x,) in inputs], incoming, factors, first_moment, second_moment
        )
    return (input_grads, adam_step)


def solution(mesh):
    return jax.shard_map(
        shards,
        mesh=mesh,
        in_specs=(
            P("expert", None, "replica", None),
            P("expert", None, "replica", None),
            P("expert", None, "replica", None),
            P("replica", "expert", None),
            P("replica", "expert", None),
            P("replica", "expert"),
            P(),
            P("replica", "expert", None, None),
        ),
        out_specs=(P("replica", "expert", None), P("expert", None, "replica", None)),
        check_vma=False,
    )
```

```python
import functools

import jax
import jax.numpy as jnp
from jax import lax
from jax.experimental import pallas as pl
from jax.experimental.pallas import tpu as pltpu
from jax.sharding import PartitionSpec as P

beta_first = 0.9
beta_second = 0.95
adam_eps = 1e-08
norm_eps = 1e-06
first_fix = 1.0 - (0.9**50) ** 2
second_fix = 1.0 - (0.95**50) ** 2
MIB = 1024 * 1024
LABEL_ROWS = 16


def contract_first(left, right):
    return lax.dot_general(
        left, right, (((0,), (0,)), ((), ())), preferred_element_type=jnp.float32
    )


def contract_last(left, right):
    return lax.dot_general(
        left, right, (((1,), (1,)), ((), ())), preferred_element_type=jnp.float32
    )


def multiply(left, right):
    return jnp.dot(left, right, preferred_element_type=jnp.float32)


def from_peer(array, offset):
    count = lax.axis_size("replica")
    return lax.ppermute(array, "replica", [(i, i ^ offset) for i in range(count)])


def across_chips(parts):
    count = lax.axis_size("expert")
    return [parts[0]] + [
        lax.ppermute(part, "expert", [(i, i ^ 2 * k) for i in range(count)])
        for k, part in enumerate(parts)
        if k
    ]


def pick_kernel(chips, *refs):
    block_refs = [ref.at[k] for ref in refs[chips:] for k in range(ref.shape[0])]
    for part_ref, block_ref in zip(refs[:chips], block_refs):
        block_ref[...] = part_ref[1]


def finish_spread(came, after=(), pieces=1):
    count = lax.axis_size("expert")
    chips = len(came)
    block = jax.ShapeDtypeStruct((chips // pieces,) + came[0].shape[1:], came[0].dtype)
    others = call(
        functools.partial(pick_kernel, chips),
        "pick",
        came,
        [VMEM] * chips,
        [block] * pieces,
        after=after,
    )
    swapped = [lax.ppermute(x, "expert", [(i, i ^ 1) for i in range(count)]) for x in others]
    return [*came, *swapped]


def spread_block(chips, refs, offset):
    if offset % 2 == 0:
        return refs[offset // 2].at[0]
    blocks = [ref.at[k] for ref in refs[chips:] for k in range(ref.shape[0])]
    return blocks[offset // 2]


def exchange(parts):
    return [parts[0]] + [from_peer(part, k) for k, part in enumerate(parts) if k]


def split_kernel(rep_ref, matrix_ref, *out_refs):
    for offset, out_ref in enumerate(out_refs):
        out_ref[...] = matrix_ref[:, segment(rep_ref, offset, out_ref.shape[1])]


def payload_kernel(rep_ref, pair_ref, inputs_ref, *out_refs):
    seg_rows = pair_ref.shape[1]
    slot_count = inputs_ref.shape[0]
    half = slot_count // 2
    for part, out_ref in enumerate(out_refs):
        out_ref[pl.ds(0, seg_rows), :] = pair_ref[0]
        out_ref[pl.ds(seg_rows, seg_rows), :] = pair_ref[1]
        columns = segment(rep_ref, part + 1, seg_rows)
        out_ref[pl.ds(2 * seg_rows, slot_count), :] = inputs_ref[:, columns]
        columns = segment(rep_ref, 3, seg_rows)
        out_ref[pl.ds(2 * seg_rows + slot_count, half), :] = inputs_ref[
            pl.ds(part * half, half), columns
        ]


def pass_kernel(from_two_ref, from_one_ref, *out_refs):
    for part, (near_ref, out_ref) in enumerate(zip((from_two_ref, from_one_ref), out_refs)):
        seg_rows = near_ref.shape[1]
        half = out_ref.shape[0] - seg_rows
        out_ref[pl.ds(0, seg_rows), :] = near_ref[pl.ds(part * seg_rows, seg_rows), :]
        out_ref[pl.ds(seg_rows, half), :] = near_ref[pl.ds(near_ref.shape[0] - half, half), :]


def projection_rows(refs):
    if len(refs) == 1 and len(refs[0].shape) == 3:
        return refs[0].at[0], refs[0].at[1]
    seg_rows = refs[0].shape[1]
    start = 0 if len(refs) == 2 else seg_rows
    return refs[0].at[pl.ds(0, seg_rows)], refs[-1].at[pl.ds(start, seg_rows)]


def input_rows(rep_ref, refs, slot_count, seg_rows):
    if len(refs) == 2:
        rows = pl.ds(seg_rows, slot_count // 2)
        return jnp.concatenate([refs[1][rows], refs[0][rows]], axis=0)
    (ref,) = refs
    if ref.shape[0] > slot_count:
        return ref[pl.ds(2 * seg_rows, slot_count), :]
    return ref[...] if ref.shape[1] == seg_rows else ref[:, segment(rep_ref, 0, seg_rows)]


def cut_kernel(from_two_ref, from_one_ref, first_ref, second_ref):
    first_ref[...] = from_two_ref[0]
    second_ref[...] = from_one_ref[1]


def gather_near(payload):
    count = lax.axis_size("replica")
    if count != 4:
        return exchange([payload] * count)
    from_two = from_peer(payload, 2)
    return [payload, from_peer(payload, 1), from_two]


def gather_rest(near, after):
    whole = [(part,) for part in near]
    if lax.axis_size("replica") != 4:
        return whole
    half = jax.ShapeDtypeStruct(near[0].shape[1:], near[0].dtype)
    first, second = call(
        cut_kernel, "cut", [near[2], near[1]], [VMEM, VMEM], [half, half], after=after
    )
    return whole + [(from_peer(first, 1), from_peer(second, 2))]


def halves(refs):
    return refs if len(refs) == 2 else (refs[0].at[0], refs[0].at[1])


def regroup(refs, lengths):
    groups, at = [], 0
    for length in lengths:
        groups.append(refs[at : at + length])
        at += length
    return groups


def flatten(groups):
    return [array for group in groups for array in group]


def pair_list(count):
    return [(i, j) for i in range(count) for j in range(i, count)]


SMEM = pl.BlockSpec(memory_space=pltpu.SMEM)
VMEM = pl.BlockSpec(memory_space=pltpu.VMEM)


def call(
    kernel, name, operands, specs, outs, out_specs=None, grid=(), scratch=(), after=(), cost=0, room=0
):
    size = sum(x.size * x.dtype.itemsize for x in list(operands) + list(outs))
    taken = len(operands)

    def body(*refs):
        kernel(*refs[:taken], *refs[taken + len(after) :])

    return pl.pallas_call(
        body,
        grid=grid,
        in_specs=list(specs) + [VMEM] * len(after),
        out_specs=out_specs if out_specs is not None else [VMEM for _ in outs],
        out_shape=outs,
        scratch_shapes=list(scratch),
        compiler_params=pltpu.CompilerParams(
            dimension_semantics=("arbitrary",) * len(grid),
            vmem_limit_bytes=max(room, min(56 * MIB, size + 8 * MIB)),
        ),
        cost_estimate=pl.CostEstimate(flops=0, bytes_accessed=cost, transcendentals=0),
        name=name,
    )(*operands, *after)


def segment(rep_ref, offset, width):
    return pl.ds(pl.multiple_of((rep_ref[0] ^ offset) * width, width), width)


def rows_kernel(expert_count, rep_ref, ids_ref, task_ref, row_ref, grads_ref, *out_refs):
    row_count = grads_ref.shape[0]
    seg_rows = out_refs[0].shape[1]
    block_count = ids_ref.shape[1]
    block_rows = row_count // block_count
    square = (row_count, row_count)
    earlier = lax.broadcasted_iota(jnp.int32, square, 0) < lax.broadcasted_iota(
        jnp.int32, square, 1
    )
    experts = lax.broadcasted_iota(jnp.int32, (expert_count, row_count), 0)
    chosen = jnp.where(experts == row_ref[...], 1.0, 0.0)
    before = multiply(
        chosen.astype(jnp.bfloat16), jnp.where(earlier, 1.0, 0.0).astype(jnp.bfloat16)
    )
    rank = jnp.sum(chosen * before, axis=0, keepdims=True)
    line = lax.broadcasted_iota(jnp.int32, (LABEL_ROWS, row_count), 0)
    labels = jnp.where(line == 0, row_ref[...].astype(jnp.float32), 0.0)
    labels = jnp.where(line == 1, rank, labels).astype(jnp.bfloat16)
    for offset, out_ref in enumerate(out_refs):
        columns = segment(rep_ref, offset, seg_rows)
        for block in range(block_count):
            rows = pl.ds(block * block_rows, block_rows)
            weight = task_ref[ids_ref[0, block]]
            out_ref[rows, :] = (grads_ref[rows, columns].astype(jnp.float32) * weight).astype(
                jnp.bfloat16
            )
        if row_count < seg_rows:
            out_ref[pl.ds(row_count, LABEL_ROWS), :] = jnp.zeros(
                (LABEL_ROWS, seg_rows), jnp.bfloat16
            )
        out_ref[pl.ds(row_count, LABEL_ROWS), pl.ds(0, row_count)] = labels


def one_hot(block_ref, row_count, slot_count, capacity):
    labels = block_ref[pl.ds(row_count, LABEL_ROWS), pl.ds(0, row_count)].astype(jnp.float32)
    slot = (labels[0:1] * capacity + labels[1:2]).astype(jnp.int32)
    places = lax.broadcasted_iota(jnp.int32, (slot_count, row_count), 0)
    return jnp.where(places == slot, 1.0, 0.0).astype(jnp.bfloat16)


def place_kernel(count, row_count, spot_ref, *refs):
    block_refs, out_refs, placed_ref = refs[:count], refs[count:-1], refs[-1]
    _, expert_count, capacity, seg_rows = placed_ref.shape
    slot_count = expert_count * capacity
    for offset, block_ref in enumerate(block_refs):
        placing = one_hot(block_ref, row_count, slot_count, capacity)
        placed = multiply(placing, block_ref[pl.ds(0, row_count), :])
        placed = placed.reshape(expert_count, capacity, seg_rows)
        placed_ref[offset] = placed.astype(jnp.bfloat16)
        for expert in range(expert_count):
            out_refs[expert // 2][expert % 2, offset] = placed_ref[offset, spot_ref[0] ^ expert]


def unplace_kernel(spot_ref, block_ref, *refs):
    returned_refs, out_ref, slots_ref = refs[:-2], refs[-2], refs[-1]
    expert_count, capacity, _ = slots_ref.shape
    slot_count = expert_count * capacity
    row_count = out_ref.shape[1]
    placing = one_hot(block_ref, row_count, slot_count, capacity)
    for expert in range(expert_count):
        block_ref = spread_block(expert_count // 2, returned_refs, expert)
        slots_ref[spot_ref[0] ^ expert] = block_ref[...]
    out_ref[0] = contract_first(placing, flat_rows(slots_ref[...])).astype(jnp.bfloat16)


def flat_rows(blocks):
    rows = blocks.shape[0] * blocks.shape[1]
    if blocks.shape[1] % 16:
        wide = blocks.astype(jnp.float32).reshape(rows, blocks.shape[2])
        return wide.astype(jnp.bfloat16)
    return blocks.reshape(rows, blocks.shape[2])


def back_kernel(chips, arrays, packed, spot_ref, weight_ref, *refs):
    came_refs, incoming_ref, out_refs = refs[:arrays], refs[arrays], refs[arrays + 1 :]
    for offset in range(incoming_ref.shape[0]):
        for expert in range(2 * chips):
            block_ref = spread_block(chips, came_refs, expert)
            incoming_ref[offset, spot_ref[0] ^ expert] = block_ref[offset]
        rows = flat_rows(incoming_ref[offset])
        total = multiply(rows, weight_ref[...])
        if not packed or offset == 0:
            out_refs[offset][...] = total.astype(out_refs[offset].dtype)
            continue
        _, near_ref, one_ref, two_ref = out_refs
        half = total.shape[0] // 2
        upper, lower = pl.ds(0, half), pl.ds(half, half)
        if offset == 1:
            one_ref[upper, :] = total[:half].astype(jnp.bfloat16)
            near_ref[lower, :] = total[half:]
        elif offset == 2:
            two_ref[upper, :] = total[half:].astype(jnp.bfloat16)
            near_ref[upper, :] = total[:half]
        else:
            one_ref[lower, :] = total[:half].astype(jnp.bfloat16)
            two_ref[lower, :] = total[half:].astype(jnp.bfloat16)


def add_kernel(near_ref, from_one_ref, from_two_ref, to_one_ref, to_two_ref):
    half = to_one_ref.shape[0]
    upper, lower = pl.ds(0, half), pl.ds(half, half)
    to_two_ref[...] = (near_ref[upper, :] + from_one_ref[lower, :].astype(jnp.float32)).astype(
        jnp.bfloat16
    )
    to_one_ref[...] = (near_ref[lower, :] + from_two_ref[lower, :].astype(jnp.float32)).astype(
        jnp.bfloat16
    )


def forward_kernel(offsets, lengths, has_start, rep_ref, inputs_ref, *refs):
    out_ref = refs[-1]
    weight_refs = refs[:-1]
    gate = up = None
    if has_start:
        gate, up = weight_refs[0][0], weight_refs[0][1]
        weight_refs = weight_refs[1:]
    for offset, group in zip(offsets, regroup(weight_refs, lengths)):
        gate_ref, up_ref = projection_rows(group)
        rows = inputs_ref[:, segment(rep_ref, offset, gate_ref.shape[0])]
        gate_part, up_part = multiply(rows, gate_ref[...]), multiply(rows, up_ref[...])
        gate = gate_part if gate is None else gate + gate_part
        up = up_part if up is None else up + up_part
    out_ref[0] = gate
    out_ref[1] = up


def factor_kernel(packed, forward_ref, *refs):
    back_refs, out_ref = refs[:-1], refs[-1]
    slot_count = forward_ref.shape[1]
    half = slot_count // 2
    hidden_grad = back_refs[0][...]
    if packed:
        upper, lower = [
            near_ref[pl.ds(0, half), :].astype(jnp.float32) + far_ref[...].astype(jnp.float32)
            for near_ref, far_ref in zip(back_refs[1:3], back_refs[3:])
        ]
        hidden_grad = hidden_grad + jnp.concatenate([upper, lower], axis=0)
        back_refs = back_refs[:1]
    for back_ref in back_refs[1:]:
        hidden_grad = hidden_grad + back_ref[...].astype(jnp.float32)
    gate_pre, up_pre = forward_ref[0], forward_ref[1]
    sigmoid_gate = jax.nn.sigmoid(gate_pre)
    gate_act = gate_pre * sigmoid_gate
    hidden = (gate_act * up_pre).astype(jnp.bfloat16)
    gate_grad = hidden_grad * up_pre * sigmoid_gate * (1.0 + gate_pre * (1.0 - sigmoid_gate))
    out_ref[0, pl.ds(0, slot_count)] = gate_grad.astype(jnp.bfloat16)
    out_ref[1, pl.ds(0, slot_count)] = (hidden_grad * gate_act).astype(jnp.bfloat16)
    for part in range(2):
        out_ref[part, pl.ds(slot_count, half)] = hidden[part * half : (part + 1) * half]


def slot_kernel(lengths, rep_ref, spot_ref, factor_ref, *refs):
    chips = refs[-1].shape[1] // 2
    weight_refs, out_refs, slots_ref = refs[: -chips - 1], refs[-chips - 1 : -1], refs[-1]
    _, expert_count, capacity, seg_rows = slots_ref.shape
    rows = pl.ds(0, expert_count * capacity)
    gate_grad, up_grad = factor_ref[0, rows], factor_ref[1, rows]
    for offset, group in enumerate(regroup(weight_refs, lengths)):
        gate_ref, up_ref = projection_rows(group)
        total = contract_last(gate_grad, gate_ref[...]) + contract_last(up_grad, up_ref[...])
        total = total.reshape(expert_count, capacity, seg_rows)
        slots_ref[offset] = total.astype(jnp.bfloat16)
        columns = segment(rep_ref, offset, seg_rows)
        for expert in range(expert_count):
            out_ref = out_refs[expert // 2]
            out_ref[expert % 2, :, columns] = slots_ref[offset, spot_ref[0] ^ expert]


def gram_kernel(count, offsets, lengths, place, rep_ref, *refs):
    if place:
        before_ref, earlier_ref, refs = refs[0], refs[1], refs[2:]
    incoming_ref, operand_refs, grads_ref, gram_ref = refs[0], refs[1:-2], refs[-2], refs[-1]
    middle = incoming_ref.shape[1] // 2
    seg_rows, hidden_width = grads_ref.shape[2:]
    slot_count = incoming_ref.shape[1] * incoming_ref.shape[2]
    groups = regroup(operand_refs, lengths)
    known = list(range(place)) + list(offsets)
    pairs = [(i, j) for i, j in pair_list(len(known)) if j >= place]
    lines = 8
    tile = min(seg_rows, 256)
    sums = [jnp.zeros((lines, hidden_width), jnp.float32) for _ in pairs]
    operands = []
    for at, offset in enumerate(offsets):
        input_refs, factor_refs = groups[2 * at : 2 * at + 2]
        rest = pl.ds(slot_count, slot_count // 2)
        columns = input_rows(rep_ref, input_refs, slot_count, seg_rows)
        gate_ref, up_ref = (ref.at[pl.ds(0, slot_count)] for ref in halves(factor_refs))
        first_ref, second_ref = (ref.at[rest] for ref in halves(factor_refs))
        upper = flat_rows(incoming_ref[offset, :middle])
        lower = flat_rows(incoming_ref[offset, middle:])
        operands.append(
            [
                [(columns, gate_ref)],
                [(columns, up_ref)],
                [(upper, first_ref), (lower, second_ref)],
            ]
        )
    for matrix in range(3):
        for start in range(0, seg_rows, tile):
            rows = pl.ds(start, tile)
            blocks = [earlier_ref[at, matrix, rows] for at in range(place)]
            for at in range(len(offsets)):
                block = None
                for left, right_ref in operands[at][matrix]:
                    part = contract_first(left[:, start : start + tile], right_ref[...])
                    block = part if block is None else block + part
                grads_ref[at, matrix, rows] = block
                blocks.append(block)
            for place_of, (i, j) in enumerate(pairs):
                products = (blocks[i] * blocks[j]).reshape(tile // lines, lines, hidden_width)
                sums[place_of] = sums[place_of] + jnp.sum(products, axis=0)
    gram_ref[...] = before_ref[...] if place else jnp.zeros_like(gram_ref)
    for total, (i, j) in zip(sums, pairs):
        total = jnp.sum(total, axis=0, keepdims=True)
        part = total[:, :128]
        for lane in range(128, hidden_width, 128):
            part = part + total[:, lane : lane + 128]
        first, second = rep_ref[0] ^ known[i], rep_ref[0] ^ known[j]
        row = jnp.minimum(first, second) * count + jnp.maximum(first, second)
        gram_ref[pl.ds(row, 1), :] = part


def merge_coefs(gram, count):
    vectors = [{rep: None} for rep in range(count)]

    def term(coef, value):
        return value if coef is None else coef * value

    def inner(left, right):
        total = None
        for i, left_coef in left.items():
            for j, right_coef in right.items():
                value = term(left_coef, term(right_coef, gram[min(i, j), max(i, j)]))
                total = value if total is None else total + value
        return total

    while len(vectors) > 1:
        merged = []
        for first, second in zip(vectors[0::2], vectors[1::2]):
            norm_first = jnp.maximum(inner(first, first), 0.0)
            norm_second = jnp.maximum(inner(second, second), 0.0)
            bound = jnp.sqrt(norm_first) * jnp.sqrt(norm_second)
            cross = jnp.minimum(jnp.maximum(inner(first, second), -bound), bound)
            coef_first = 1.0 - cross / (2.0 * (norm_first + norm_eps))
            coef_second = 1.0 - cross / (2.0 * (norm_second + norm_eps))
            joined = {rep: term(coef, coef_first) for rep, coef in first.items()}
            joined.update({rep: term(coef, coef_second) for rep, coef in second.items()})
            merged.append(joined)
        vectors = merged
    return [vectors[0][rep] for rep in range(count)]


def adam_kernel(count, places, rep_ref, *refs):
    gram_refs, grads_refs = refs[:count], refs[count : count + len(places)]
    first_ref, second_ref, step_ref, coef_ref = refs[count + len(places) :]
    block_rows, hidden_width = step_ref.shape[2:]
    lines = coef_ref.shape[1]

    @pl.when((pl.program_id(0) == 0) & (pl.program_id(1) == 0))
    def _():
        sums = gram_refs[0][...]
        for gram_ref in gram_refs[1:]:
            sums = sums + gram_ref[...]
        sums = jnp.sum(sums, axis=1, keepdims=True)
        gram = {(i, j): sums[i * count + j : i * count + j + 1] for i, j in pair_list(count)}
        for rep, coef in enumerate(merge_coefs(gram, count)):
            coef_ref[rep] = jnp.broadcast_to(coef, coef_ref.shape[1:])

    matrix = pl.program_id(0)
    block = pl.program_id(1) * block_rows
    coefs = [[coef_ref[rep_ref[0] ^ offset] for offset in offsets] for offsets in places]

    def step(index, _):
        rows = pl.ds(pl.multiple_of(index * lines, lines), lines)
        all_rows = pl.ds(pl.multiple_of(block + index * lines, lines), lines)
        for lane in range(0, hidden_width, 128):
            columns = pl.ds(lane, 128)
            merged = None
            for grads_ref, group in zip(grads_refs, coefs):
                for at, coef in enumerate(group):
                    part = grads_ref[at, matrix, all_rows, columns] * coef
                    merged = part if merged is None else merged + part
            first_new = (beta_first / first_fix) * first_ref[0, matrix, all_rows, columns] + (
                (1.0 - beta_first) / first_fix
            ) * merged
            second_new = (beta_second / second_fix) * second_ref[0, matrix, all_rows, columns] + (
                (1.0 - beta_second) / second_fix
            ) * (merged * merged)
            root = second_new * lax.rsqrt(second_new)
            step_ref[0, 0, rows, columns] = first_new / (root + adam_eps)
        return 0

    lax.fori_loop(0, block_rows // lines, step, 0, unroll=4)


def adasum_adam_many(rep, inputs, incoming, factors, first_moment, second_moment):
    count = len(inputs)
    half = inputs[0].shape[0] // 2
    grads = []
    for offset in range(count):
        (payload,) = factors[offset]
        gate_grad, up_grad = payload[:, : 2 * half]
        hidden = payload[:, 2 * half :].reshape(2 * half, -1)
        received = incoming[offset].reshape(2 * half, incoming.shape[3])
        grads.append(
            jnp.stack(
                [
                    contract_first(inputs[offset], gate_grad),
                    contract_first(inputs[offset], up_grad),
                    contract_first(received, hidden),
                ]
            )
        )
    grads = jnp.stack(grads)[rep[0] ^ jnp.arange(count)]
    flat = grads.reshape(count, -1)
    gram = lax.psum(jnp.matmul(flat, flat.T, precision=lax.Precision.HIGHEST), "replica")
    coefs = jnp.eye(count, dtype=jnp.float32)
    while coefs.shape[0] > 1:
        inner = jnp.matmul(
            jnp.matmul(coefs, gram, precision=lax.Precision.HIGHEST),
            coefs.T,
            precision=lax.Precision.HIGHEST,
        )
        norms = jnp.maximum(jnp.diagonal(inner), 0.0)
        norm_first, norm_second = norms[0::2], norms[1::2]
        bound = jnp.sqrt(norm_first) * jnp.sqrt(norm_second)
        cross = jnp.clip(jnp.diagonal(inner, offset=1)[0::2], -bound, bound)
        coef_first = 1.0 - cross / (2.0 * (norm_first + norm_eps))
        coef_second = 1.0 - cross / (2.0 * (norm_second + norm_eps))
        coefs = coef_first[:, None] * coefs[0::2] + coef_second[:, None] * coefs[1::2]
    merged = jnp.sum(coefs[0][:, None, None, None] * grads, axis=0)
    first_new = beta_first * first_moment[0] + (1.0 - beta_first) * merged
    second_new = beta_second * second_moment[0] + (1.0 - beta_second) * merged * merged
    return ((first_new / first_fix) / (jnp.sqrt(second_new / second_fix) + adam_eps))[None]


def adasum(rep, inputs, incoming, factors):
    count = len(inputs)
    seg_rows, hidden_width = incoming.shape[3], factors[0][0].shape[2]
    shape = jax.ShapeDtypeStruct
    groups = [[k for k in range(count) if k < 3], [k for k in range(count) if k == 3]]
    groups = [group for group in groups if group]
    grads, gram, first_gram, place = [], None, None, 0
    for group in groups:
        operands = [rep] if gram is None else [rep, gram, grads[0]]
        parts = [x for k in group for x in (inputs[k], factors[k])]
        operands += [incoming] + flatten(parts)
        more, gram = call(
            functools.partial(gram_kernel, count, group, [len(x) for x in parts], place),
            "gram_late" if place else "gram",
            operands,
            [SMEM] + [VMEM] * (len(operands) - 1),
            [
                shape((len(group), 3, seg_rows, hidden_width), jnp.float32),
                shape((max(8, count * count), 128), jnp.float32),
            ],
            cost=0 if place else 0,
        )
        first_gram = gram if first_gram is None else first_gram
        grads.append(more)
        place += len(group)
    return groups, grads, gram, first_gram


def adam(rep, groups, grads, gram, first_moment, second_moment, after):
    count = sum(len(group) for group in groups)
    seg_rows, hidden_width = first_moment.shape[2:]
    grams = [gram] + [from_peer(gram, k) for k in reversed(range(1, count))]
    tile = min(seg_rows, 512)
    moment_spec = pl.BlockSpec((1, 1, tile, hidden_width), lambda m, d: (0, m, d, 0))
    (adam_step,) = call(
        functools.partial(adam_kernel, count, groups),
        "adam",
        [rep, *grams, *grads, first_moment, second_moment],
        [SMEM] + [VMEM] * (len(grams) + len(grads) + 2),
        [jax.ShapeDtypeStruct(first_moment.shape, jnp.float32)],
        out_specs=[moment_spec],
        grid=(3, seg_rows // tile),
        scratch=[pltpu.VMEM((count, 16, 128), jnp.float32)],
        after=after,
    )
    return adam_step


def shards(
    weights, first_moment, second_moment, out_grads, routes, task_ids, task_weights, saved_inputs
):
    expert_count = lax.axis_size("expert")
    rep_count = lax.axis_size("replica")
    row_count = out_grads.shape[1]
    model_width = out_grads.shape[2]
    hidden_width = weights.shape[3]
    slot_count = saved_inputs.shape[2]
    capacity = slot_count // expert_count
    seg_rows = model_width // rep_count
    half = slot_count // 2
    offsets = range(rep_count)
    chips = expert_count // 2
    rep = lax.axis_index("replica").astype(jnp.int32).reshape(1)
    spot = lax.axis_index("expert").astype(jnp.int32).reshape(1)
    shape = jax.ShapeDtypeStruct

    block = shape((row_count + LABEL_ROWS, seg_rows), jnp.bfloat16)
    small = [routes[0].reshape(1, row_count), out_grads[0]]
    row_blocks = call(
        functools.partial(rows_kernel, expert_count),
        "rows",
        [rep, task_ids, task_weights, *small],
        [SMEM] * 3 + [pl.BlockSpec(x.shape, lambda i: (0, 0)) for x in small],
        [block for _ in offsets],
        grid=(1,),
        room=56 * MIB,
    )
    routed = exchange(row_blocks)

    inputs_home = saved_inputs[0, 0]
    pair = weights[0, :2]
    packed = rep_count == 4 and seg_rows == hidden_width
    if packed:
        payload = shape((2 * seg_rows + slot_count + half, seg_rows), jnp.bfloat16)
        to_one, to_two = call(
            payload_kernel,
            "payload",
            [jnp.concatenate([rep, spot]), pair, inputs_home],
            [SMEM, VMEM, VMEM],
            [payload, payload],
            after=routed[1:],
        )
        from_two, from_one = from_peer(to_two, 2), from_peer(to_one, 1)
        projections = [(pair,), (from_one,), (from_two,)]
        inputs = [(inputs_home,), (from_one,), (from_two,)]
    else:
        projections = [(x,) for x in exchange([pair] * rep_count)]
        pieces = [shape((slot_count, seg_rows), jnp.bfloat16) for _ in offsets]
        pieces = call(split_kernel, "split", [rep, inputs_home], [SMEM, VMEM], pieces)
        inputs = [(x,) for x in exchange(pieces)]

    part = shape((2, rep_count, capacity, seg_rows), jnp.bfloat16)
    placed = (
        call(
            functools.partial(place_kernel, rep_count, row_count),
            "place",
            [spot, *routed],
            [SMEM] + [VMEM] * len(routed),
            [part] * chips,
            scratch=[
                pltpu.VMEM((rep_count, expert_count, capacity, seg_rows), jnp.bfloat16)
            ],
        )
    )

    came = across_chips(placed)

    came = finish_spread(came)

    back_shape = (slot_count, hidden_width)
    incoming, *back = call(
        functools.partial(back_kernel, chips, len(came), packed),
        "back",
        [spot, weights[0, 2], *came],
        [SMEM] + [VMEM] * (1 + len(came)),
        [shape((rep_count, expert_count, capacity, seg_rows), jnp.bfloat16)]
        + [
            shape(back_shape, jnp.float32 if k == 0 or packed and k == 1 else jnp.bfloat16)
            for k in offsets
        ],
    )
    if not packed:
        back = exchange(back)
    if packed:
        own_back, near_back, to_one, to_two = back
        back_one, back_two = from_peer(to_one, 1), from_peer(to_two, 2)
        passed = shape((seg_rows + half, seg_rows), jnp.bfloat16)
        first, second = call(
            pass_kernel,
            "pass",
            [from_two, from_one],
            [VMEM, VMEM],
            [passed, passed],
            after=[back_one, back_two],
        )
        last = (from_peer(first, 1), from_peer(second, 2))
        to_one, to_two = call(
            add_kernel,
            "add",
            [near_back, back_one, back_two],
            [VMEM] * 3,
            [shape((half, hidden_width), jnp.bfloat16)] * 2,
        )
        back = [own_back, back_one, back_two, from_peer(to_two, 2), from_peer(to_one, 1)]
        projections.append(last)
        inputs.append(last)

    forward = None
    late = [3] if packed else []
    for name, group in (("forward", [k for k in offsets if k not in late]), ("rest", late)):
        if not group:
            continue
        operands = [rep, inputs_home] + ([] if forward is None else [forward])
        operands += flatten(projections[k] for k in group)
        lengths = [len(projections[k]) for k in group]
        (forward,) = call(
            functools.partial(forward_kernel, group, lengths, forward is not None),
            name,
            operands,
            [SMEM] + [VMEM] * (len(operands) - 1),
            [shape((2, slot_count, hidden_width), jnp.float32)],
            cost=0 if name == "rest" else 0,
        )

    (own_factors,) = call(
        functools.partial(factor_kernel, packed),
        "factors",
        [forward, *back],
        [VMEM] * (1 + len(back)),
        [shape((2, slot_count + half, hidden_width), jnp.bfloat16)],
    )
    near_factors = gather_near(own_factors)

    operands = [rep, spot, own_factors] + flatten(projections)
    returning = across_chips(
        call(
            functools.partial(slot_kernel, [len(group) for group in projections]),
            "slots",
            operands,
            [SMEM] * 2 + [VMEM] * (len(operands) - 2),
            [shape((2, capacity, model_width), jnp.bfloat16)] * chips,
            scratch=[
                pltpu.VMEM((rep_count, expert_count, capacity, seg_rows), jnp.bfloat16)
            ],
        )
    )
    factors = gather_rest(near_factors, after=returning[:1])
    if rep_count <= 4:
        *merging, first_gram = adasum(rep, inputs, incoming, factors)
        returned = finish_spread(returning, [first_gram], pieces=2)
        unplace_after = merging[2:]
    else:
        returned, unplace_after = finish_spread(returning), ()
    (input_grads,) = call(
        unplace_kernel,
        "unplace",
        [spot, routed[0], *returned],
        [SMEM] + [VMEM] * (1 + len(returned)),
        [shape((1, row_count, model_width), jnp.bfloat16)],
        scratch=[pltpu.VMEM((expert_count, capacity, model_width), jnp.bfloat16)],
        after=unplace_after,
    )
    if rep_count <= 4:
        adam_step = adam(rep, *merging, first_moment, second_moment, ())
    else:
        adam_step = adasum_adam_many(
            rep, [x for (x,) in inputs], incoming, factors, first_moment, second_moment
        )
    return (input_grads, adam_step)


def solution(mesh):
    return jax.shard_map(
        shards,
        mesh=mesh,
        in_specs=(
            P("expert", None, "replica", None),
            P("expert", None, "replica", None),
            P("expert", None, "replica", None),
            P("replica", "expert", None),
            P("replica", "expert", None),
            P("replica", "expert"),
            P(),
            P("replica", "expert", None, None),
        ),
        out_specs=(P("replica", "expert", None), P("expert", None, "replica", None)),
        check_vma=False,
    )
```
